32 devices in a mesh: node: 16 (over z, y, x), col: 2 (over core).
Axes of the slice: x: 2, y: 2, z: 4, core: 2. Of those that a mesh axis runs over, the one named last changes fastest.
Arguments:
- x_t: bfloat16 [512, 8192], P('col', 'node'), may hold values from -6 to 6
- adj_tiles: bfloat16 [1024, 128, 128], P('node'), may hold values from -0.1875 to 0.1875
- tile_rows: int32 [1024], P('node'), may hold values from 0 to 3
- tile_cols: int32 [1024], P('node'), may hold values from 0 to 63, as said below
- tile_counts: int32 [16], P('node'), may hold values from 8 to 64, as said below
- w_first: bfloat16 [512, 512], P('col'), may hold values from -0.25 to 0.25
- b_first: float32 [512], P('col'), may hold values from -3 to 3
- w_second: bfloat16 [512, 512], P('col'), may hold values from -0.25 to 0.25
- b_second: float32 [512], P('col'), may hold values from -3 to 3
Outputs:
- out_t: float32 [512, 8192], P('col', 'node')
The draws below stay inside these ranges and needn't reach their ends.
Inputs may be any that keep to these rules, and one draw needn't show every extreme that they name: `tile_cols`: column blocks q * 4 to q * 4 + 3 belong to device q of node. Among the live tiles of one device, at most 2 distinct column blocks belong to any one device, and every device's first 2 tiles name 2 distinct blocks of one device. `tile_counts`: some device has all 64 slots live.
All inputs are finite; a program needn't handle non-finite values.
Results may differ from the reference program's by a relative error of at most 0.004.
Values may be sent and summed in bfloat16 or wider, within the bound.
No kernel may reach another device: no remote copies, remote signals or barrier semaphores. Data moves between devices by JAX's collectives and lax.ppermute only.
A program may use at most 64 MiB of HBM per device.

```python
import jax
import jax.numpy as jnp
from jax import lax

F = 512
BLK = 128
RB = 4
TILES = 64
CAP = 2
NBLK = 64
NODES = 8192
TILE_SLOTS = 1024


def draw_tile_cols(key, part):
    peer_count = NBLK // RB
    key_peer = jax.random.fold_in(key, 11)
    key_block = jax.random.fold_in(key, 23)
    peer_scores = jax.random.randint(key_peer, (peer_count, peer_count), 0, 1 << 20) * peer_count + jnp.arange(peer_count)[None, :]
    peer_order = jnp.argsort(peer_scores, axis=1).astype(jnp.int32)
    block_scores = jax.random.randint(key_block, (peer_count, peer_count, RB), 0, 1 << 20) * RB + jnp.arange(RB)[None, None, :]
    allowed = jnp.argsort(block_scores, axis=2)[:, :, :CAP].astype(jnp.int32)
    index = jnp.arange(TILES)
    which = index // CAP % peer_count
    slot = index % CAP
    owner = peer_order[:, which]
    source = jnp.arange(peer_count)[:, None]
    block = allowed[source, owner, slot[None, :]]
    return (owner * RB + block).reshape(-1).astype(jnp.int32)


def draw_tile_counts(key, part):
    peer_count = NBLK // RB
    shifts = jax.random.randint(jax.random.fold_in(key, 5), (peer_count,), 0, 4)
    counts = TILES // jnp.left_shift(jnp.ones((peer_count,), jnp.int32), shifts.astype(jnp.int32))
    chosen = jax.random.randint(jax.random.fold_in(key, 9), (), 0, peer_count)
    counts = jnp.where(jnp.arange(peer_count) == chosen, TILES, counts)
    return counts.astype(jnp.int32)


def plant(values, key, smallest, top_value):
    extent = values.shape
    spot = [jax.random.randint(jax.random.fold_in(key, axis), (), 0, extent[axis]) for axis in range(len(extent))]
    values = values.at[tuple(spot)].set(smallest)
    longest = extent.index(max(extent))
    spot[longest] = (spot[longest] + 1) % extent[longest]
    return values.at[tuple(spot)].set(top_value)


def block_scale(own_key, extent, pieces, least, high):
    gain, own = 1.0, jax.random.fold_in(own_key, 6)
    for axis_at, shards_of in pieces:
        heights = jnp.exp(jax.random.uniform(jax.random.fold_in(own, axis_at), (shards_of,), jnp.float32, least / len(pieces), high / len(pieces)))
        gain = gain * jnp.repeat(heights, extent[axis_at] // shards_of).reshape([-1 if axis == axis_at else 1 for axis in range(len(extent))])
    return gain


def centred(rng, shape, spread, bound, cuts=(), held_as=jnp.bfloat16):
    level = block_scale(rng, shape, cuts, -0.22, 0.18) if cuts else 1.0
    values = jax.random.normal(rng, shape, jnp.float32) * spread * level
    return jnp.minimum(jnp.maximum(values, -bound), bound).astype(held_as)


def setup_inputs(seed: int = 0) -> dict:
    splits = jax.random.split(jax.random.key(seed), 10)
    return {
        "x_t": centred(splits[0], (F, NODES), 1.0, 6.0, ((0, 2), (1, 16))),
        "adj_tiles": centred(splits[1], (TILE_SLOTS, BLK, BLK), (BLK * TILES // (2 * RB)) ** -0.5, 0.1875, ((0, 16),)),
        "tile_rows": plant(jax.random.randint(splits[2], (TILE_SLOTS,), 0, RB), jax.random.fold_in(splits[2], 1), 0, RB - 1).astype(jnp.int32),
        "tile_cols": draw_tile_cols(jax.random.fold_in(splits[9], 71), 0),
        "tile_counts": draw_tile_counts(jax.random.fold_in(splits[9], 71), 0),
        "w_first": centred(splits[5], (F, F), F ** -0.5, 0.25, ((0, 2),)),
        "b_first": centred(splits[6], (F,), 0.5, 3.0, ((0, 2),), jnp.float32),
        "w_second": centred(splits[7], (F, F), F ** -0.5, 0.25, ((0, 2),)),
        "b_second": centred(splits[8], (F,), 0.5, 3.0, ((0, 2),), jnp.float32),
    }


def aggregate(feat_t, adj_tiles, tile_rows, tile_cols, tile_counts):
    peer_count = NBLK // RB
    blocks = feat_t.reshape(F, NBLK, BLK)
    tile_values = adj_tiles.reshape(peer_count, TILES, BLK, BLK)
    row_table = tile_rows.reshape(peer_count, TILES)
    col_table = tile_cols.reshape(peer_count, TILES)

    def one_part(packed):
        values_p, rows_p, cols_p, count_p = packed
        x_blocks = jnp.take(blocks, cols_p.astype(jnp.int32), axis=1).astype(jnp.float32)
        products = jnp.einsum("fnj,nij->fni", x_blocks, values_p.astype(jnp.float32), precision=lax.Precision.HIGHEST)
        is_live = jnp.arange(TILES, dtype=jnp.int32) < count_p
        selector = ((rows_p[:, None] == jnp.arange(RB, dtype=jnp.int32)[None, :]) & is_live[:, None]).astype(jnp.float32)
        summed = jnp.einsum("fni,nb->fbi", products, selector, precision=lax.Precision.HIGHEST)
        return summed.reshape(F, RB * BLK)

    result = lax.map(one_part, (tile_values, row_table, col_table, tile_counts))
    return jnp.transpose(result, (1, 0, 2)).reshape(F, NODES).astype(jnp.bfloat16)


def reference(x_t, adj_tiles, tile_rows, tile_cols, tile_counts, w_first, b_first, w_second, b_second):
    y_first = aggregate(x_t, adj_tiles, tile_rows, tile_cols, tile_counts)
    z_first = jnp.dot(w_first, y_first, preferred_element_type=jnp.float32) + b_first[:, None]
    h_first = jnp.maximum(z_first, 0.0).astype(jnp.bfloat16)
    y_second = aggregate(h_first, adj_tiles, tile_rows, tile_cols, tile_counts)
    return jnp.dot(w_second, y_second, preferred_element_type=jnp.float32) + b_second[:, None]
```

```python
import jax
import jax.numpy as jnp
from jax import lax
from jax.experimental import pallas as pl
from jax.experimental.pallas import tpu as pltpu
from jax.sharding import PartitionSpec as P

BLK = 128
UNROLL = 4


def aggregate_kernel(count_ref, rows_ref, cols_ref, feats_ref, tiles_ref, out_ref, total):
    row_blocks = feats_ref.shape[2] // BLK
    total[...] = jnp.zeros_like(total)
    live = count_ref[0]

    @pl.loop(0, (live + UNROLL - 1) // UNROLL)
    def _(group):
        for step in range(UNROLL):
            slot = group * UNROLL + step
            column = cols_ref[slot]
            row = jnp.where(slot < live, rows_ref[slot], row_blocks)
            owner = column // row_blocks
            lane = pl.multiple_of((column - owner * row_blocks) * BLK, BLK)
            block = feats_ref[owner, :, pl.ds(lane, BLK)]
            total[row] += lax.dot_general(
                block,
                tiles_ref[slot],
                (((1,), (1,)), ((), ())),
                preferred_element_type=jnp.float32,
            )

    for row in range(row_blocks):
        out_ref[:, row * BLK : (row + 1) * BLK] = total[row].astype(out_ref.dtype)


def aggregate(feat_t, adj_tiles, tile_rows, tile_cols, tile_counts):
    feat_local, nodes_local = feat_t.shape
    row_blocks = nodes_local // BLK
    gathered = lax.all_gather(feat_t, "node", axis=0, tiled=False)
    tile_total = adj_tiles.shape[0]
    smem = pl.BlockSpec(memory_space=pltpu.SMEM)
    vmem = pl.BlockSpec(memory_space=pltpu.VMEM)
    return pl.pallas_call(
        aggregate_kernel,
        out_shape=jax.ShapeDtypeStruct((feat_local, nodes_local), jnp.bfloat16),
        in_specs=[smem, smem, smem, vmem, vmem],
        out_specs=vmem,
        scratch_shapes=[pltpu.VMEM((row_blocks + 1, feat_local, BLK), jnp.float32)],
        compiler_params=pltpu.CompilerParams(vmem_limit_bytes=32 * 1024 * 1024),
        cost_estimate=pl.CostEstimate(
            flops=2 * tile_total * feat_local * BLK * BLK,
            bytes_accessed=2 * (gathered.size + adj_tiles.size + feat_t.size),
            transcendentals=0,
        ),
    )(tile_counts, tile_rows, tile_cols, gathered, adj_tiles)


def dense_layer(aggregated, weight_local, bias_local):
    summed = jnp.dot(
        weight_local,
        lax.all_gather(aggregated, "col", axis=0, tiled=True),
        preferred_element_type=jnp.float32,
    )
    return summed + bias_local[:, None]


def body(x_t, adj_tiles, tile_rows, tile_cols, tile_counts, w_first, b_first, w_second, b_second):
    graph = (adj_tiles, tile_rows, tile_cols, tile_counts)
    y_first = aggregate(x_t, *graph)
    h_first = jnp.maximum(dense_layer(y_first, w_first, b_first), 0.0).astype(jnp.bfloat16)
    y_second = aggregate(h_first, *graph)
    return dense_layer(y_second, w_second, b_second)


def solution(mesh):
    return jax.shard_map(
        body,
        mesh=mesh,
        in_specs=(
            P("col", "node"),
            P("node", None, None),
            P("node"),
            P("node"),
            P("node"),
            P("col", None),
            P("col"),
            P("col", None),
            P("col"),
        ),
        out_specs=P("col", "node"),
        check_vma=False,
    )
```

```python
import functools

import jax
import jax.numpy as jnp
from jax import lax
from jax.experimental import pallas as pl
from jax.experimental.pallas import tpu as pltpu
from jax.sharding import PartitionSpec as P

BLK = 128
CAP = 2
PLANE = 4
UNROLL = 4
SMEM = pl.BlockSpec(memory_space=pltpu.SMEM)
ANYWHERE = pl.BlockSpec(memory_space=pl.ANY)


def unit_source(line, unit):
    return jnp.where(unit <= line, line - unit, unit)


def lowest(mask):
    return jnp.where(mask & 1 != 0, 0, jnp.where(mask & 2 != 0, 1, jnp.where(mask & 4 != 0, 2, 3)))


def highest(mask):
    return jnp.where(mask & 8 != 0, 3, jnp.where(mask & 4 != 0, 2, jnp.where(mask & 2 != 0, 1, 0)))


def plan_kernel(lines, row_blocks, *refs):
    named = refs[:PLANE]
    sent_ref, place_ref, masks = refs[PLANE:]
    tile_total = place_ref.shape[0]
    peers = lines * PLANE
    node = lax.axis_index("node")
    line, corner = node // PLANE, node % PLANE

    @pl.loop(0, PLANE * peers)
    def _(at):
        masks[at] = 0

    for partner in range(PLANE):

        @pl.loop(0, named[partner][tile_total])
        def _(slot):
            column = named[partner][slot]
            owner = column // row_blocks
            at = partner * peers + owner
            masks[at] = masks[at] | (1 << (column - owner * row_blocks))

    for unit in range(lines):
        source = unit_source(line, unit)
        for partner in range(PLANE):
            mask = masks[partner * peers + source * PLANE + corner]
            sent_ref[(unit * PLANE + partner) * CAP] = lowest(mask)
            sent_ref[(unit * PLANE + partner) * CAP + 1] = highest(mask)

    @pl.loop(0, tile_total)
    def _(slot):
        column = named[0][slot]
        owner = column // row_blocks
        block = column - owner * row_blocks
        source = owner // PLANE
        unit = jnp.where(source <= line, line - source, source)
        partner = (owner - source * PLANE) ^ corner
        second = jnp.where(block == lowest(masks[owner]), 0, 1)
        place_ref[slot] = (unit * PLANE + partner) * CAP + second


def make_plan(tile_cols, tile_counts, lines, row_blocks):
    tile_total = tile_cols.shape[0]
    peers = lines * PLANE
    named = [jnp.concatenate([tile_cols, tile_counts])]
    for partner in range(1, PLANE):
        named.append(lax.ppermute(named[0], "node", [(n, n ^ partner) for n in range(peers)]))
    return pl.pallas_call(
        functools.partial(plan_kernel, lines, row_blocks),
        out_shape=[
            jax.ShapeDtypeStruct((lines * PLANE * CAP,), jnp.int32),
            jax.ShapeDtypeStruct((tile_total,), jnp.int32),
        ],
        in_specs=[SMEM] * PLANE,
        out_specs=[SMEM] * 2,
        scratch_shapes=[pltpu.SMEM((PLANE * peers,), jnp.int32)],
    )(*named)


def pack_kernel(unit, sent_ref, *refs):
    held, packed, done = refs[:-PLANE - 1], refs[-PLANE - 1 : -1], refs[-1]
    line = lax.axis_index("node") // PLANE

    def copies(source):
        out = []
        for partner in range(PLANE):
            for slot in range(CAP):
                at = (unit * PLANE + partner) * CAP + slot
                lane = pl.multiple_of(sent_ref[at] * BLK, BLK)
                out.append(
                    pltpu.make_async_copy(
                        source.at[:, pl.ds(lane, BLK)],
                        packed[partner].at[slot],
                        done.at[partner * CAP + slot],
                    )
                )
        return out

    for which, source in enumerate(held):
        chosen = unit <= line if which == 0 else line == unit - which

        @pl.when(chosen)
        def _():
            for copy in copies(source):
                copy.start()

    for copy in copies(held[0]):
        copy.wait()


def pack(unit, sent, held):
    feat_local = held[0].shape[0]
    one = jax.ShapeDtypeStruct((CAP, feat_local, BLK), jnp.bfloat16)
    return pl.pallas_call(
        functools.partial(pack_kernel, unit),
        out_shape=[one] * PLANE,
        in_specs=[SMEM] + [ANYWHERE] * len(held),
        out_specs=[ANYWHERE] * PLANE,
        scratch_shapes=[pltpu.SemaphoreType.DMA((PLANE * CAP,))],
        cost_estimate=pl.CostEstimate(
            flops=0, bytes_accessed=4 * PLANE * CAP * feat_local * BLK, transcendentals=0
        ),
    )(sent, *held)


def spread(feat_t, sent, lines):
    peers = lines * PLANE
    up, down = [feat_t], [feat_t]
    received = []
    for unit in range(lines):
        if unit:
            climb = [(n, n + PLANE) for n in range((unit - 1) * PLANE, peers - PLANE)]
            sink = [(n, n - PLANE) for n in range(PLANE, peers - (unit - 1) * PLANE)]
            up.append(lax.ppermute(up[-1], "node", climb))
            down.append(lax.ppermute(down[-1], "node", sink))
        packed = pack(unit, sent, [up[unit]] + down[1 : unit + 1])
        received.append(packed[0])
        for partner in range(1, PLANE):
            received.append(
                lax.ppermute(packed[partner], "node", [(n, n ^ partner) for n in range(peers)])
            )
    return received


def aggregate_kernel(count_ref, rows_ref, place_ref, tiles_hbm, *refs):
    received, (out_ref, tiles, blocks, total, tiles_done, blocks_done) = refs[:-6], refs[-6:]
    row_blocks = out_ref.shape[1] // BLK
    copies = [pltpu.make_async_copy(tiles_hbm, tiles, tiles_done)]
    for at, buffer in enumerate(received):
        copies.append(
            pltpu.make_async_copy(buffer, blocks.at[pl.ds(at * CAP, CAP)], blocks_done.at[at])
        )
    for copy in copies:
        copy.start()
    total[...] = jnp.zeros_like(total)
    live = count_ref[0]
    for copy in copies:
        copy.wait()

    @pl.loop(0, (live + UNROLL - 1) // UNROLL)
    def _(group):
        for step in range(UNROLL):
            slot = group * UNROLL + step
            row = jnp.where(slot < live, rows_ref[slot], row_blocks)
            total[row] += lax.dot_general(
                blocks[place_ref[slot]],
                tiles[slot],
                (((1,), (1,)), ((), ())),
                preferred_element_type=jnp.float32,
            )

    for row in range(row_blocks):
        out_ref[:, row * BLK : (row + 1) * BLK] = total[row].astype(out_ref.dtype)


def aggregate(feat_t, adj_tiles, tile_rows, tile_counts, plan, lines):
    sent, place = plan
    feat_local, nodes_local = feat_t.shape
    row_blocks = nodes_local // BLK
    received = spread(feat_t, sent, lines)
    tile_total = adj_tiles.shape[0]
    return pl.pallas_call(
        aggregate_kernel,
        out_shape=jax.ShapeDtypeStruct((feat_local, nodes_local), jnp.bfloat16),
        in_specs=[SMEM] * 3 + [ANYWHERE] * (1 + len(received)),
        out_specs=pl.BlockSpec(memory_space=pltpu.VMEM),
        scratch_shapes=[
            pltpu.VMEM(adj_tiles.shape, jnp.bfloat16),
            pltpu.VMEM((len(received) * CAP, feat_local, BLK), jnp.bfloat16),
            pltpu.VMEM((row_blocks + 1, feat_local, BLK), jnp.float32),
            pltpu.SemaphoreType.DMA,
            pltpu.SemaphoreType.DMA((len(received),)),
        ],
        compiler_params=pltpu.CompilerParams(vmem_limit_bytes=32 * 1024 * 1024),
        cost_estimate=pl.CostEstimate(
            flops=2 * tile_total * feat_local * BLK * BLK,
            bytes_accessed=2 * (len(received) * CAP * feat_local * BLK + adj_tiles.size),
            transcendentals=0,
        ),
    )(tile_counts, tile_rows, place, adj_tiles, *received)


def dense_layer(aggregated, weight_local, bias_local):
    summed = jnp.dot(
        weight_local,
        lax.all_gather(aggregated, "col", axis=0, tiled=True),
        preferred_element_type=jnp.float32,
    )
    return summed + bias_local[:, None]


def body(x_t, adj_tiles, tile_rows, tile_cols, tile_counts, w_first, b_first, w_second, b_second):
    lines = lax.axis_size("node") // PLANE
    row_blocks = x_t.shape[1] // BLK
    plan = make_plan(tile_cols, tile_counts, lines, row_blocks)
    graph = (adj_tiles, tile_rows, tile_counts, plan, lines)
    y_first = aggregate(x_t, *graph)
    h_first = jnp.maximum(dense_layer(y_first, w_first, b_first), 0.0).astype(jnp.bfloat16)
    y_second = aggregate(h_first, *graph)
    return dense_layer(y_second, w_second, b_second)


def solution(mesh):
    return jax.shard_map(
        body,
        mesh=mesh,
        in_specs=(
            P("col", "node"),
            P("node", None, None),
            P("node"),
            P("node"),
            P("node"),
            P("col", None),
            P("col"),
            P("col", None),
            P("col"),
        ),
        out_specs=P("col", "node"),
        check_vma=False,
    )
```

```python
import functools

import jax
import jax.numpy as jnp
from jax import lax
from jax.experimental import pallas as pl
from jax.experimental.pallas import tpu as pltpu
from jax.sharding import PartitionSpec as P

BLK = 128
CAP = 2
PLANE = 4
UNROLL = 4
SMEM = pl.BlockSpec(memory_space=pltpu.SMEM)
ANYWHERE = pl.BlockSpec(memory_space=pltpu.HBM)


def unit_source(line, unit):
    return jnp.where(unit <= line, line - unit, unit)


def lowest(mask):
    return jnp.where(mask & 1 != 0, 0, jnp.where(mask & 2 != 0, 1, jnp.where(mask & 4 != 0, 2, 3)))


def highest(mask):
    return jnp.where(mask & 8 != 0, 3, jnp.where(mask & 4 != 0, 2, jnp.where(mask & 2 != 0, 1, 0)))


def masks_of(columns, live, words):
    def step(slot, found):
        column = columns(slot)
        bit = 1 << (column & 31)
        word = column >> 5
        bit = jnp.where(slot < live, bit, 0)
        return tuple(
            one | (bit if words == 1 else jnp.where(word == at, bit, 0))
            for at, one in enumerate(found)
        )

    return step, tuple(jnp.int32(0) for _ in range(words))


def owner_mask(found, owner, row_blocks):
    first = owner * row_blocks
    word = found[0]
    for at in range(1, len(found)):
        word = jnp.where(first >> 5 == at, found[at], word)
    return (word >> (first & 31)) & ((1 << row_blocks) - 1)


def scan_columns(named, corner, tile_total, words):
    step, start = masks_of(lambda slot: named[corner, slot], named[corner, tile_total], words)
    return lax.fori_loop(0, tile_total, step, start, unroll=8)


def sent_kernel(lines, row_blocks, named, sent_ref):
    tile_total = named.shape[1] - 1
    words = -(-lines * PLANE * row_blocks // 32)
    node = lax.axis_index("node")
    line, corner = node // PLANE, node % PLANE
    for other in range(PLANE):
        found = scan_columns(named, other, tile_total, words)
        for unit in range(lines):
            mask = owner_mask(found, unit_source(line, unit) * PLANE + corner, row_blocks)
            sent_ref[(unit * PLANE + other) * CAP] = lowest(mask)
            sent_ref[(unit * PLANE + other) * CAP + 1] = highest(mask)


def place_kernel(lines, row_blocks, named, place_ref):
    tile_total = named.shape[1] - 1
    words = -(-lines * PLANE * row_blocks // 32)
    node = lax.axis_index("node")
    line, corner = node // PLANE, node % PLANE
    found = scan_columns(named, corner, tile_total, words)

    @pl.loop(0, tile_total)
    def _(slot):
        column = named[corner, slot]
        owner = column // row_blocks
        source = owner // PLANE
        unit = jnp.where(source <= line, line - source, source)
        second = column - owner * row_blocks != lowest(owner_mask(found, owner, row_blocks))
        at = unit * PLANE + owner - source * PLANE
        place_ref[slot] = at * CAP + jnp.where(second, 1, 0)


def plane_groups(lines):
    return [list(range(line * PLANE, (line + 1) * PLANE)) for line in range(lines)]


def make_plan(tile_cols, tile_counts, lines, row_blocks):
    own = jnp.concatenate([tile_cols, tile_counts])
    named = lax.all_to_all(
        jnp.broadcast_to(own, (PLANE,) + own.shape),
        "node",
        split_axis=0,
        concat_axis=0,
        axis_index_groups=plane_groups(lines),
    )

    def table(kernel, size):
        return pl.pallas_call(
            functools.partial(kernel, lines, row_blocks),
            out_shape=jax.ShapeDtypeStruct((size,), jnp.int32),
            in_specs=[SMEM],
            out_specs=SMEM,
        )(named)

    return table(sent_kernel, lines * PLANE * CAP), table(place_kernel, tile_cols.shape[0])


def pack_kernel(unit, sent_ref, *refs):
    held, packed, done = refs[:-2], refs[-2], refs[-1]
    line = lax.axis_index("node") // PLANE

    def copies(source):
        out = []
        for other in range(PLANE):
            for slot in range(CAP):
                at = other * CAP + slot
                lane = pl.multiple_of(sent_ref[unit * PLANE * CAP + at] * BLK, BLK)
                out.append(
                    pltpu.make_async_copy(
                        source.at[:, pl.ds(lane, BLK)], packed.at[other, slot], done.at[at]
                    )
                )
        return out

    for which, source in enumerate(held):
        chosen = unit <= line if which == 0 else line == unit - which

        @pl.when(chosen)
        def _():
            for copy in copies(source):
                copy.start()

    for copy in copies(held[0]):
        copy.wait()


def pack(unit, sent, held):
    feat_local = held[0].shape[0]
    return pl.pallas_call(
        functools.partial(pack_kernel, unit),
        out_shape=jax.ShapeDtypeStruct((PLANE, CAP, feat_local, BLK), jnp.bfloat16),
        in_specs=[SMEM] + [ANYWHERE] * len(held),
        out_specs=pl.BlockSpec(memory_space=pltpu.VMEM),
        scratch_shapes=[pltpu.SemaphoreType.DMA((PLANE * CAP,))],
        cost_estimate=pl.CostEstimate(
            flops=0, bytes_accessed=4 * PLANE * CAP * feat_local * BLK, transcendentals=0
        ),
    )(sent, *held)


def spread(feat_t, sent, lines):
    peers = lines * PLANE
    up, down = [feat_t], [feat_t]
    received = []
    for unit in range(lines):
        if unit:
            climb = [(n, n + PLANE) for n in range((unit - 1) * PLANE, peers - PLANE)]
            sink = [(n, n - PLANE) for n in range(PLANE, peers - (unit - 1) * PLANE)]
            up.append(lax.ppermute(up[-1], "node", climb))
            down.append(lax.ppermute(down[-1], "node", sink))
        packed = pack(unit, sent, [up[unit]] + down[1 : unit + 1])
        received.append(
            lax.all_to_all(
                packed,
                "node",
                split_axis=0,
                concat_axis=0,
                tiled=True,
                axis_index_groups=plane_groups(lines),
            )
        )
    return received


def aggregate_kernel(count_ref, rows_ref, place_ref, tiles_hbm, *refs):
    received, (out_ref, tiles, blocks, total, tiles_done, blocks_done) = refs[:-6], refs[-6:]
    row_blocks = out_ref.shape[1] // BLK
    copies = [pltpu.make_async_copy(tiles_hbm, tiles, tiles_done)]
    for at, buffer in enumerate(received):
        copies.append(
            pltpu.make_async_copy(buffer, blocks.at[at], blocks_done.at[at])
        )
    for copy in copies:
        copy.start()
    total[...] = jnp.zeros_like(total)
    live = count_ref[0]
    for copy in copies:
        copy.wait()

    @pl.loop(0, (live + UNROLL - 1) // UNROLL)
    def _(group):
        for step in range(UNROLL):
            slot = group * UNROLL + step
            row = jnp.where(slot < live, rows_ref[slot], row_blocks)
            place = place_ref[slot]
            block = blocks[place // (PLANE * CAP), place // CAP % PLANE, place % CAP]
            total[row] += lax.dot_general(
                block,
                tiles[slot],
                (((1,), (1,)), ((), ())),
                preferred_element_type=jnp.float32,
            )

    for row in range(row_blocks):
        out_ref[:, row * BLK : (row + 1) * BLK] = total[row].astype(out_ref.dtype)


def aggregate(feat_t, adj_tiles, tile_rows, tile_counts, plan, lines):
    sent, place = plan
    feat_local, nodes_local = feat_t.shape
    row_blocks = nodes_local // BLK
    received = spread(feat_t, sent, lines)
    tile_total = adj_tiles.shape[0]
    return pl.pallas_call(
        aggregate_kernel,
        out_shape=jax.ShapeDtypeStruct((feat_local, nodes_local), jnp.bfloat16),
        in_specs=[SMEM] * 3 + [ANYWHERE] * (1 + len(received)),
        out_specs=pl.BlockSpec(memory_space=pltpu.VMEM),
        scratch_shapes=[
            pltpu.VMEM(adj_tiles.shape, jnp.bfloat16),
            pltpu.VMEM((lines, PLANE, CAP, feat_local, BLK), jnp.bfloat16),
            pltpu.VMEM((row_blocks + 1, feat_local, BLK), jnp.float32),
            pltpu.SemaphoreType.DMA,
            pltpu.SemaphoreType.DMA((len(received),)),
        ],
        compiler_params=pltpu.CompilerParams(vmem_limit_bytes=32 * 1024 * 1024),
        cost_estimate=pl.CostEstimate(
            flops=2 * tile_total * feat_local * BLK * BLK,
            bytes_accessed=2 * (lines * received[0].size + adj_tiles.size),
            transcendentals=0,
        ),
    )(tile_counts, tile_rows, place, adj_tiles, *received)


def dense_layer(aggregated, weight_local, bias_local):
    summed = jnp.dot(
        weight_local,
        lax.all_gather(aggregated, "col", axis=0, tiled=True),
        preferred_element_type=jnp.float32,
    )
    return summed + bias_local[:, None]


def body(x_t, adj_tiles, tile_rows, tile_cols, tile_counts, w_first, b_first, w_second, b_second):
    lines = lax.axis_size("node") // PLANE
    row_blocks = x_t.shape[1] // BLK
    plan = make_plan(tile_cols, tile_counts, lines, row_blocks)
    graph = (adj_tiles, tile_rows, tile_counts, plan, lines)
    y_first = aggregate(x_t, *graph)
    h_first = jnp.maximum(dense_layer(y_first, w_first, b_first), 0.0).astype(jnp.bfloat16)
    y_second = aggregate(h_first, *graph)
    return dense_layer(y_second, w_second, b_second)


def solution(mesh):
    return jax.shard_map(
        body,
        mesh=mesh,
        in_specs=(
            P("col", "node"),
            P("node", None, None),
            P("node"),
            P("node"),
            P("node"),
            P("col", None),
            P("col"),
            P("col", None),
            P("col"),
        ),
        out_specs=P("col", "node"),
        check_vma=False,
    )
```

```python
import functools

import jax
import jax.numpy as jnp
from jax import lax
from jax.experimental import pallas as pl
from jax.experimental.pallas import tpu as pltpu
from jax.sharding import PartitionSpec as P

BLK = 128
CAP = 2
PLANE = 4
CHUNKS = 2
UNROLL = 4
SMEM = pl.BlockSpec(memory_space=pltpu.SMEM)
VMEM = pl.BlockSpec(memory_space=pltpu.VMEM)


def lowest(mask):
    return jnp.where(mask & 1 != 0, 0, jnp.where(mask & 2 != 0, 1, jnp.where(mask & 4 != 0, 2, 3)))


def highest(mask):
    return jnp.where(mask & 8 != 0, 3, jnp.where(mask & 4 != 0, 2, jnp.where(mask & 2 != 0, 1, 0)))


def scan_columns(named, corner, tile_total, words):
    live = named[corner, tile_total]

    def step(slot, found):
        column = named[corner, slot]
        bit = jnp.where(slot < live, 1 << (column & 31), 0)
        word = column >> 5
        return tuple(one | jnp.where(word == at, bit, 0) for at, one in enumerate(found))

    start = tuple(jnp.int32(0) for _ in range(words))
    return lax.fori_loop(0, tile_total, step, start, unroll=8)


def owner_mask(found, owner, row_blocks):
    first = owner * row_blocks
    word = found[0]
    for at in range(1, len(found)):
        word = jnp.where(first >> 5 == at, found[at], word)
    return (word >> (first & 31)) & ((1 << row_blocks) - 1)


def sent_kernel(lines, row_blocks, named, sent_ref):
    tile_total = named.shape[1] - 1
    words = -(-lines * PLANE * row_blocks // 32)
    node = lax.axis_index("node")
    line, corner = node // PLANE, node % PLANE
    for other in range(PLANE):
        found = scan_columns(named, other, tile_total, words)
        for unit in range(lines):
            source = (line + unit) % lines
            mask = owner_mask(found, source * PLANE + corner, row_blocks)
            sent_ref[(other * lines + unit) * CAP] = lowest(mask)
            sent_ref[(other * lines + unit) * CAP + 1] = highest(mask)


def place_kernel(lines, row_blocks, named, place_ref):
    tile_total = named.shape[1] - 1
    words = -(-lines * PLANE * row_blocks // 32)
    node = lax.axis_index("node")
    line, corner = node // PLANE, node % PLANE
    found = scan_columns(named, corner, tile_total, words)

    @pl.loop(0, tile_total)
    def _(slot):
        column = named[corner, slot]
        owner = column // row_blocks
        source = owner // PLANE
        unit = (source - line + lines) % lines
        second = column - owner * row_blocks != lowest(owner_mask(found, owner, row_blocks))
        at = (owner - source * PLANE) * lines + unit
        place_ref[slot] = at * CAP + jnp.where(second, 1, 0)


def line_groups(lines):
    return [[line * PLANE + corner for line in range(lines)] for corner in range(PLANE)]


def plane_exchange(packed, lines):
    return lax.all_to_all(
        packed,
        "node",
        split_axis=0,
        concat_axis=0,
        axis_index_groups=[
            [line * PLANE + corner for corner in range(PLANE)] for line in range(lines)
        ],
    )


def make_plan(tile_cols, tile_counts, lines, row_blocks):
    own = jnp.concatenate([tile_cols, tile_counts])
    named = plane_exchange(jnp.broadcast_to(own, (PLANE,) + own.shape), lines)

    def table(kernel, size):
        return pl.pallas_call(
            functools.partial(kernel, lines, row_blocks),
            out_shape=jax.ShapeDtypeStruct((size,), jnp.int32),
            in_specs=[SMEM],
            out_specs=SMEM,
        )(named)

    return table(sent_kernel, lines * PLANE * CAP), table(place_kernel, tile_cols.shape[0])


def pack_own_kernel(lines, sent_ref, held, packed):
    for other in range(PLANE):
        for slot in range(CAP):
            block = sent_ref[other * lines * CAP + slot]
            lane = pl.multiple_of(block * BLK, BLK)
            packed[other, slot] = held[:, pl.ds(lane, BLK)]


def pack_line_kernel(lines, sent_ref, held, packed):
    line = lax.axis_index("node") // PLANE
    for unit in range(1, lines):
        source = (line + unit) % lines
        for other in range(PLANE):
            for slot in range(CAP):
                block = sent_ref[(other * lines + unit) * CAP + slot]
                lane = pl.multiple_of(block * BLK, BLK)
                packed[other, unit - 1, slot] = held[source, :, pl.ds(lane, BLK)]


def pack(kernel, sent, held, shape, lines):
    return pl.pallas_call(
        functools.partial(kernel, lines),
        out_shape=jax.ShapeDtypeStruct(shape, jnp.bfloat16),
        in_specs=[SMEM, VMEM],
        out_specs=VMEM,
        compiler_params=pltpu.CompilerParams(vmem_limit_bytes=32 * 1024 * 1024),
    )(sent, held)


def aggregate_kernel(
    chunk, lines, count_ref, rows_ref, place_ref, tiles, own_hbm, line_hbm, out_ref, blocks, total, done
):
    height, row_blocks = out_ref.shape[0], out_ref.shape[1] // BLK
    copies = [
        pltpu.make_async_copy(
            own_hbm.at[:, :, pl.ds(chunk * height, height)], blocks.at[:, 0], done.at[0]
        ),
        pltpu.make_async_copy(line_hbm, blocks.at[:, pl.ds(1, lines - 1)], done.at[1]),
    ]
    for copy in copies:
        copy.start()
    total[...] = jnp.zeros_like(total)
    live = count_ref[0]
    for copy in copies:
        copy.wait()

    @pl.loop(0, (live + UNROLL - 1) // UNROLL)
    def _(group):
        for step in range(UNROLL):
            slot = group * UNROLL + step
            row = jnp.where(slot < live, rows_ref[slot], row_blocks)
            place = place_ref[slot]
            corner = place // (lines * CAP)
            total[row] += lax.dot_general(
                blocks[corner, place // CAP - corner * lines, place % CAP],
                tiles[slot],
                (((1,), (1,)), ((), ())),
                preferred_element_type=jnp.float32,
            )

    for row in range(row_blocks):
        out_ref[:, row * BLK : (row + 1) * BLK] = total[row].astype(out_ref.dtype)


def aggregate(chunk, lines, graph, own, remote):
    adj_tiles, tile_rows, tile_counts, place, nodes_local = graph
    tile_total = adj_tiles.shape[0]
    height = remote.shape[3]
    anywhere = pl.BlockSpec(memory_space=pl.ANY)
    return pl.pallas_call(
        functools.partial(aggregate_kernel, chunk, lines),
        out_shape=jax.ShapeDtypeStruct((height, nodes_local), jnp.bfloat16),
        in_specs=[SMEM] * 3 + [VMEM, anywhere, anywhere],
        out_specs=VMEM,
        scratch_shapes=[
            pltpu.VMEM((PLANE, lines, CAP, height, BLK), jnp.bfloat16),
            pltpu.VMEM((nodes_local // BLK + 1, height, BLK), jnp.float32),
            pltpu.SemaphoreType.DMA((2,)),
        ],
        compiler_params=pltpu.CompilerParams(vmem_limit_bytes=32 * 1024 * 1024),
        cost_estimate=pl.CostEstimate(
            flops=2 * tile_total * height * BLK * BLK,
            bytes_accessed=2 * (lines * PLANE * CAP * height * BLK + adj_tiles.size),
            transcendentals=0,
        ),
    )(tile_counts, tile_rows, place, adj_tiles, own, remote)


def layer(feat_t, sent, graph, weight, bias, lines):
    feat_local = feat_t.shape[0]
    height = feat_local // CHUNKS
    gathered = [
        lax.all_gather(
            feat_t[chunk * height : (chunk + 1) * height],
            "node",
            axis=0,
            axis_index_groups=line_groups(lines),
        )
        for chunk in range(CHUNKS)
    ]
    own = plane_exchange(
        pack(pack_own_kernel, sent, feat_t, (PLANE, CAP, feat_local, BLK), lines), lines
    )
    shape = (PLANE, lines - 1, CAP, height, BLK)
    by_chunk = weight.reshape(weight.shape[0], -1, CHUNKS, height)
    summed = bias[:, None]
    for chunk in range(CHUNKS):
        remote = plane_exchange(pack(pack_line_kernel, sent, gathered[chunk], shape, lines), lines)
        part = aggregate(chunk, lines, graph, own, remote)
        part = lax.all_gather(part, "col", axis=0, tiled=True)
        summed = summed + jnp.dot(
            by_chunk[:, :, chunk].reshape(weight.shape[0], -1),
            part,
            preferred_element_type=jnp.float32,
        )
    return summed


def body(x_t, adj_tiles, tile_rows, tile_cols, tile_counts, w_first, b_first, w_second, b_second):
    lines = lax.axis_size("node") // PLANE
    nodes_local = x_t.shape[1]
    sent, place = make_plan(tile_cols, tile_counts, lines, nodes_local // BLK)
    graph = (adj_tiles, tile_rows, tile_counts, place, nodes_local)
    z_first = layer(x_t, sent, graph, w_first, b_first, lines)
    h_first = jnp.maximum(z_first, 0.0).astype(jnp.bfloat16)
    return layer(h_first, sent, graph, w_second, b_second, lines)


def solution(mesh):
    return jax.shard_map(
        body,
        mesh=mesh,
        in_specs=(
            P("col", "node"),
            P("node", None, None),
            P("node"),
            P("node"),
            P("node"),
            P("col", None),
            P("col"),
            P("col", None),
            P("col"),
        ),
        out_specs=P("col", "node"),
        check_vma=False,
    )
```

```python
import functools

import jax
import jax.numpy as jnp
from jax import lax
from jax.experimental import pallas as pl
from jax.experimental.pallas import tpu as pltpu
from jax.sharding import PartitionSpec as P

BLK = 128
CAP = 2
GROUP = 8
UNROLL = 4
SMEM = pl.BlockSpec(memory_space=pltpu.SMEM)
VMEM = pl.BlockSpec(memory_space=pltpu.VMEM)
PARAMS = pltpu.CompilerParams(vmem_limit_bytes=16 * 1024 * 1024)


def lowest(mask):
    return jnp.where(mask & 1 != 0, 0, jnp.where(mask & 2 != 0, 1, jnp.where(mask & 4 != 0, 2, 3)))


def highest(mask):
    return jnp.where(mask & 8 != 0, 3, jnp.where(mask & 4 != 0, 2, jnp.where(mask & 2 != 0, 1, 0)))


def owner_mask(words, owner, row_blocks):
    first = owner * row_blocks
    word = words[0]
    for at in range(1, len(words)):
        word = jnp.where(first >> 5 == at, words[at], word)
    return (word >> (first & 31)) & ((1 << row_blocks) - 1)


def words_kernel(count_ref, cols_ref, words_ref):
    live = count_ref[0]
    word_total = words_ref.shape[1]

    def step(slot, found):
        column = cols_ref[slot]
        bit = jnp.where(slot < live, 1 << (column & 31), 0)
        word = column >> 5
        return tuple(one | jnp.where(word == at, bit, 0) for at, one in enumerate(found))

    start = tuple(jnp.int32(0) for _ in range(word_total))
    found = lax.fori_loop(0, cols_ref.shape[0], step, start, unroll=8)
    for member in range(GROUP):
        for at in range(word_total):
            words_ref[member, at] = found[at]


def list_kernel(cubes, row_blocks, count_ref, rows_ref, cols_ref, words_ref, *refs):
    filled, slots, lanes, places = refs
    tile_total = cols_ref.shape[0]
    cube = lax.axis_index("node") // GROUP
    words = [words_ref[0, at] for at in range(words_ref.shape[1])]
    for unit in range(cubes):
        filled[unit] = 0

    @pl.loop(0, cubes * tile_total)
    def _(at):
        slots[at] = 0
        lanes[at] = row_blocks
        places[at] = 0

    @pl.loop(0, count_ref[0])
    def _(slot):
        column = cols_ref[slot]
        owner = column // row_blocks
        home = owner // GROUP
        unit = jnp.where(home >= cube, home - cube, home - cube + cubes)
        second = column - owner * row_blocks != lowest(owner_mask(words, owner, row_blocks))
        at = unit * tile_total + filled[unit]
        filled[unit] = filled[unit] + 1
        slots[at] = slot
        lanes[at] = rows_ref[slot]
        places[at] = (owner - home * GROUP) * CAP + jnp.where(second, 1, 0)


def cube_exchange(packed, cubes):
    return lax.all_to_all(
        packed,
        "node",
        split_axis=0,
        concat_axis=0,
        tiled=True,
        axis_index_groups=[
            [cube * GROUP + member for member in range(GROUP)] for cube in range(cubes)
        ],
    )


def make_plan(tile_rows, tile_cols, tile_counts, cubes, row_blocks):
    tile_total = tile_cols.shape[0]
    word_total = -(-cubes * GROUP * row_blocks // 32)
    own = pl.pallas_call(
        words_kernel,
        out_shape=jax.ShapeDtypeStruct((GROUP, word_total), jnp.int32),
        in_specs=[SMEM] * 2,
        out_specs=SMEM,
    )(tile_counts, tile_cols)
    lists = pl.pallas_call(
        functools.partial(list_kernel, cubes, row_blocks),
        out_shape=[jax.ShapeDtypeStruct((cubes,), jnp.int32)]
        + [jax.ShapeDtypeStruct((cubes * tile_total,), jnp.int32)] * 3,
        in_specs=[SMEM] * 4,
        out_specs=[SMEM] * 4,
    )(tile_counts, tile_rows, tile_cols, own)
    return cube_exchange(own, cubes), lists


def pack_kernel(cubes, unit, words_ref, held, packed):
    row_blocks = held.shape[1] // BLK
    node = lax.axis_index("node")
    cube, member = node // GROUP, node % GROUP
    owner = (cube + unit) % cubes * GROUP + member
    for other in range(GROUP):
        words = [words_ref[other, at] for at in range(words_ref.shape[1])]
        mask = owner_mask(words, owner, row_blocks)
        for slot, block in enumerate((lowest(mask), highest(mask))):
            lane = pl.multiple_of(block * BLK, BLK)
            packed[other, slot] = held[:, pl.ds(lane, BLK)]


def pack(cubes, unit, words, held):
    shape = (GROUP, CAP, held.shape[0], BLK)
    return pl.pallas_call(
        functools.partial(pack_kernel, cubes, unit),
        out_shape=jax.ShapeDtypeStruct(shape, jnp.bfloat16),
        in_specs=[SMEM, VMEM],
        out_specs=VMEM,
        compiler_params=PARAMS,
    )(words, held)


def aggregate_kernel(unit, last, filled, slots, lanes, places, tiles, received, *refs):
    tile_total = tiles.shape[0]
    if unit:
        before, refs = refs[0], refs[1:]
    out_ref = refs[0]
    total = refs[1] if last else out_ref
    total[...] = before[...] if unit else jnp.zeros_like(total)

    @pl.loop(0, (filled[unit] + UNROLL - 1) // UNROLL)
    def _(group):
        for step in range(UNROLL):
            at = unit * tile_total + group * UNROLL + step
            place = places[at]
            total[lanes[at]] += lax.dot_general(
                received[place // CAP, place % CAP],
                tiles[slots[at]],
                (((1,), (1,)), ((), ())),
                preferred_element_type=jnp.float32,
            )

    if last:
        for row in range(total.shape[0] - 1):
            out_ref[:, row * BLK : (row + 1) * BLK] = total[row].astype(out_ref.dtype)


def aggregate(cubes, unit, lists, adj_tiles, received, before, nodes_local):
    feat_local = received.shape[2]
    last = unit == cubes - 1
    total = jax.ShapeDtypeStruct((nodes_local // BLK + 1, feat_local, BLK), jnp.float32)
    out = jax.ShapeDtypeStruct((feat_local, nodes_local), jnp.bfloat16) if last else total
    return pl.pallas_call(
        functools.partial(aggregate_kernel, unit, last),
        out_shape=out,
        in_specs=[SMEM] * 4 + [VMEM] * (2 + len(before)),
        out_specs=VMEM,
        scratch_shapes=[pltpu.VMEM(total.shape, total.dtype)] if last else [],
        compiler_params=PARAMS,
        cost_estimate=pl.CostEstimate(
            flops=2 * adj_tiles.shape[0] * feat_local * BLK * BLK,
            bytes_accessed=2 * (received.size + adj_tiles.size) + 8 * total.size,
            transcendentals=0,
        ),
    )(*lists, adj_tiles, received, *before)


def layer(feat_t, adj_tiles, plan, weight, bias, cubes):
    words, lists = plan
    nodes = cubes * GROUP
    held = [feat_t]
    for unit in range(1, cubes):
        pairs = [(n, (n - unit * GROUP) % nodes) for n in range(nodes)]
        held.append(lax.ppermute(feat_t, "node", pairs))
    before = ()
    for unit in range(cubes):
        received = cube_exchange(pack(cubes, unit, words, held[unit]), cubes)
        before = (
            aggregate(cubes, unit, lists, adj_tiles, received, before, feat_t.shape[1]),
        )
    summed = jnp.dot(
        weight,
        lax.all_gather(before[0], "col", axis=0, tiled=True),
        preferred_element_type=jnp.float32,
    )
    return summed + bias[:, None]


def body(x_t, adj_tiles, tile_rows, tile_cols, tile_counts, w_first, b_first, w_second, b_second):
    cubes = lax.axis_size("node") // GROUP
    plan = make_plan(tile_rows, tile_cols, tile_counts, cubes, x_t.shape[1] // BLK)
    z_first = layer(x_t, adj_tiles, plan, w_first, b_first, cubes)
    h_first = jnp.maximum(z_first, 0.0).astype(jnp.bfloat16)
    return layer(h_first, adj_tiles, plan, w_second, b_second, cubes)


def solution(mesh):
    return jax.shard_map(
        body,
        mesh=mesh,
        in_specs=(
            P("col", "node"),
            P("node", None, None),
            P("node"),
            P("node"),
            P("node"),
            P("col", None),
            P("col"),
            P("col", None),
            P("col"),
        ),
        out_specs=P("col", "node"),
        check_vma=False,
    )
```

```python
import functools

import jax
import jax.numpy as jnp
from jax import lax
from jax.experimental import pallas as pl
from jax.experimental.pallas import tpu as pltpu
from jax.sharding import PartitionSpec as P

BLK = 128
CAP = 2
GROUP = 8
UNROLL = 4
RELAY_WORK = 50_000_000_000
SMEM = pl.BlockSpec(memory_space=pltpu.SMEM)
VMEM = pl.BlockSpec(memory_space=pltpu.VMEM)
HBM = pl.BlockSpec(memory_space=pltpu.HBM)
PARAMS = pltpu.CompilerParams(vmem_limit_bytes=16 * 1024 * 1024)


def lowest(mask):
    return jnp.where(mask & 1 != 0, 0, jnp.where(mask & 2 != 0, 1, jnp.where(mask & 4 != 0, 2, 3)))


def highest(mask):
    return jnp.where(mask & 8 != 0, 3, jnp.where(mask & 4 != 0, 2, jnp.where(mask & 2 != 0, 1, 0)))


def owner_mask(words, owner, row_blocks):
    first = owner * row_blocks
    word = words[0]
    for at in range(1, len(words)):
        word = jnp.where(first >> 5 == at, words[at], word)
    return (word >> (first & 31)) & ((1 << row_blocks) - 1)


def words_kernel(count_ref, cols_ref, words_ref):
    live = count_ref[0]
    word_total = words_ref.shape[1]

    def step(slot, found):
        column = cols_ref[slot]
        bit = jnp.where(slot < live, 1 << (column & 31), 0)
        word = column >> 5
        return tuple(one | jnp.where(word == at, bit, 0) for at, one in enumerate(found))

    start = tuple(jnp.int32(0) for _ in range(word_total))
    found = lax.fori_loop(0, cols_ref.shape[0], step, start, unroll=8)
    for member in range(GROUP):
        for at in range(word_total):
            words_ref[member, at] = found[at]


def list_size(tile_total):
    return 1 + 3 * tile_total


def list_kernel(cubes, row_blocks, count_ref, rows_ref, cols_ref, words_ref, lists):
    tile_total = cols_ref.shape[0]
    cube = lax.axis_index("node") // GROUP
    words = [words_ref[0, at] for at in range(words_ref.shape[1])]
    size = list_size(tile_total)
    for unit in range(cubes):
        lists[unit * size] = 0

    for unit in range(cubes):

        @pl.loop(0, tile_total)
        def _(at):
            entry = unit * size + 1 + 3 * at
            lists[entry] = 0
            lists[entry + 1] = row_blocks
            lists[entry + 2] = 0

    @pl.loop(0, count_ref[0])
    def _(slot):
        column = cols_ref[slot]
        owner = column // row_blocks
        home = owner // GROUP
        unit = jnp.where(home >= cube, home - cube, home - cube + cubes)
        second = column - owner * row_blocks != lowest(owner_mask(words, owner, row_blocks))
        filled = lists[unit * size]
        lists[unit * size] = filled + 1
        entry = unit * size + 1 + 3 * filled
        lists[entry] = slot
        lists[entry + 1] = rows_ref[slot]
        lists[entry + 2] = (owner - home * GROUP) * CAP + jnp.where(second, 1, 0)


def cube_exchange(packed, cubes):
    return lax.all_to_all(
        packed,
        "node",
        split_axis=0,
        concat_axis=0,
        tiled=True,
        axis_index_groups=[
            [cube * GROUP + member for member in range(GROUP)] for cube in range(cubes)
        ],
    )


def make_plan(tile_rows, tile_cols, tile_counts, cubes, row_blocks):
    tile_total = tile_cols.shape[0]
    word_total = -(-cubes * GROUP * row_blocks // 32)
    own = pl.pallas_call(
        words_kernel,
        out_shape=jax.ShapeDtypeStruct((GROUP, word_total), jnp.int32),
        in_specs=[SMEM] * 2,
        out_specs=SMEM,
    )(tile_counts, tile_cols)
    lists = pl.pallas_call(
        functools.partial(list_kernel, cubes, row_blocks),
        out_shape=jax.ShapeDtypeStruct((cubes * list_size(tile_total),), jnp.int32),
        in_specs=[SMEM] * 4,
        out_specs=SMEM,
    )(tile_counts, tile_rows, tile_cols, own)
    return cube_exchange(own, cubes), lists


def pack_kernel(cubes, unit, words_ref, held, packed_hbm, packed, done):
    row_blocks = held.shape[1] // BLK
    node = lax.axis_index("node")
    cube, member = node // GROUP, node % GROUP
    owner = (cube + unit) % cubes * GROUP + member
    copies = []
    for other in range(GROUP):
        words = [words_ref[other, at] for at in range(words_ref.shape[1])]
        mask = owner_mask(words, owner, row_blocks)
        for slot, block in enumerate((lowest(mask), highest(mask))):
            lane = pl.multiple_of(block * BLK, BLK)
            packed[other, slot] = held[:, pl.ds(lane, BLK)]
        copies.append(pltpu.make_async_copy(packed.at[other], packed_hbm.at[other], done.at[other]))
        copies[-1].start()
    for copy in copies:
        copy.wait()


def pack(cubes, unit, words, held):
    shape = (GROUP, CAP, held.shape[0], BLK)
    work = RELAY_WORK if unit else 0
    return pl.pallas_call(
        functools.partial(pack_kernel, cubes, unit),
        out_shape=jax.ShapeDtypeStruct(shape, jnp.bfloat16),
        in_specs=[SMEM, VMEM],
        out_specs=HBM,
        scratch_shapes=[pltpu.VMEM(shape, jnp.bfloat16), pltpu.SemaphoreType.DMA((GROUP,))],
        compiler_params=PARAMS,
        cost_estimate=pl.CostEstimate(flops=work, bytes_accessed=0, transcendentals=0),
    )(words, held)


def aggregate_kernel(unit, last, lists, tiles, received, *refs):
    size = list_size(tiles.shape[0])
    if unit:
        before_hbm, refs = refs[0], refs[1:]
        before = refs[2]
        fetch = pltpu.make_async_copy(before_hbm, before, refs[3])
        fetch.start()
    out_ref, total = refs[0], refs[1]
    total[...] = jnp.zeros_like(total)

    @pl.loop(0, (lists[unit * size] + UNROLL - 1) // UNROLL)
    def _(group):
        for step in range(UNROLL):
            entry = unit * size + 1 + 3 * (group * UNROLL + step)
            place = lists[entry + 2]
            total[lists[entry + 1]] += lax.dot_general(
                received[place // CAP, place % CAP],
                tiles[lists[entry]],
                (((1,), (1,)), ((), ())),
                preferred_element_type=jnp.float32,
            )

    if unit:
        fetch.wait()
    for row in range(total.shape[0] - 1):
        summed = total[row] + before[row] if unit else total[row]
        if last:
            out_ref[:, row * BLK : (row + 1) * BLK] = summed.astype(out_ref.dtype)
        elif unit:
            total[row] = summed
    if not last:
        store = pltpu.make_async_copy(total.at[pl.ds(0, out_ref.shape[0])], out_ref, refs[-1])
        store.start()
        store.wait()


def aggregate(cubes, unit, lists, adj_tiles, received, before, nodes_local):
    feat_local = received.shape[2]
    row_blocks = nodes_local // BLK
    last = unit == cubes - 1
    total = (row_blocks, feat_local, BLK)
    scratch = [pltpu.VMEM((row_blocks + 1, feat_local, BLK), jnp.float32)]
    if unit:
        scratch += [pltpu.VMEM(total, jnp.float32), pltpu.SemaphoreType.DMA]
    if not last:
        scratch += [pltpu.SemaphoreType.DMA]
    return pl.pallas_call(
        functools.partial(aggregate_kernel, unit, last),
        out_shape=jax.ShapeDtypeStruct((feat_local, nodes_local), jnp.bfloat16)
        if last
        else jax.ShapeDtypeStruct(total, jnp.float32),
        in_specs=[SMEM] + [VMEM] * 2 + [HBM] * len(before),
        out_specs=VMEM if last else HBM,
        scratch_shapes=scratch,
        compiler_params=PARAMS,
        cost_estimate=pl.CostEstimate(
            flops=2 * adj_tiles.shape[0] * feat_local * BLK * BLK,
            bytes_accessed=2 * (received.size + adj_tiles.size + feat_local * nodes_local),
            transcendentals=0,
        ),
    )(lists, adj_tiles, received, *before)


def layer(feat_t, adj_tiles, plan, weight, bias, cubes):
    words, lists = plan
    nodes = cubes * GROUP
    held = [feat_t]
    for unit in range(1, cubes):
        pairs = [(n, (n - unit * GROUP) % nodes) for n in range(nodes)]
        held.append(lax.ppermute(feat_t, "node", pairs))
    before = ()
    for unit in range(cubes):
        received = cube_exchange(pack(cubes, unit, words, held[unit]), cubes)
        before = (
            aggregate(cubes, unit, lists, adj_tiles, received, before, feat_t.shape[1]),
        )
    summed = jnp.dot(
        weight,
        lax.all_gather(before[0], "col", axis=0, tiled=True),
        preferred_element_type=jnp.float32,
    )
    return summed + bias[:, None]


def body(x_t, adj_tiles, tile_rows, tile_cols, tile_counts, w_first, b_first, w_second, b_second):
    cubes = lax.axis_size("node") // GROUP
    plan = make_plan(tile_rows, tile_cols, tile_counts, cubes, x_t.shape[1] // BLK)
    z_first = layer(x_t, adj_tiles, plan, w_first, b_first, cubes)
    h_first = jnp.maximum(z_first, 0.0).astype(jnp.bfloat16)
    return layer(h_first, adj_tiles, plan, w_second, b_second, cubes)


def solution(mesh):
    return jax.shard_map(
        body,
        mesh=mesh,
        in_specs=(
            P("col", "node"),
            P("node", None, None),
            P("node"),
            P("node"),
            P("node"),
            P("col", None),
            P("col"),
            P("col", None),
            P("col"),
        ),
        out_specs=P("col", "node"),
        check_vma=False,
    )
```

```python
import functools

import jax
import jax.numpy as jnp
from jax import lax
from jax.experimental import pallas as pl
from jax.experimental.pallas import tpu as pltpu
from jax.sharding import PartitionSpec as P

BLK = 128
CAP = 2
GROUP = 8
UNROLL = 4
STEPS = range(1, GROUP)
RELAY_WORK = 50_000_000_000
SMEM = pl.BlockSpec(memory_space=pltpu.SMEM)
VMEM = pl.BlockSpec(memory_space=pltpu.VMEM)
HBM = pl.BlockSpec(memory_space=pltpu.HBM)
PARAMS = pltpu.CompilerParams(vmem_limit_bytes=16 * 1024 * 1024)


def lowest(mask):
    return jnp.where(mask & 1 != 0, 0, jnp.where(mask & 2 != 0, 1, jnp.where(mask & 4 != 0, 2, 3)))


def highest(mask):
    return jnp.where(mask & 8 != 0, 3, jnp.where(mask & 4 != 0, 2, jnp.where(mask & 2 != 0, 1, 0)))


def owner_mask(words, owner, row_blocks):
    first = owner * row_blocks
    word = words[0]
    for at in range(1, len(words)):
        word = jnp.where(first >> 5 == at, words[at], word)
    return (word >> (first & 31)) & ((1 << row_blocks) - 1)


def words_kernel(count_ref, cols_ref, words_ref):
    live = count_ref[0]
    word_total = words_ref.shape[1]

    def step(slot, found):
        column = cols_ref[slot]
        bit = jnp.where(slot < live, 1 << (column & 31), 0)
        word = column >> 5
        return tuple(one | jnp.where(word == at, bit, 0) for at, one in enumerate(found))

    start = tuple(jnp.int32(0) for _ in range(word_total))
    found = lax.fori_loop(0, cols_ref.shape[0], step, start, unroll=8)
    for member in range(GROUP):
        for at in range(word_total):
            words_ref[member, at] = found[at]


def list_size(tile_total):
    return 1 + 3 * tile_total


def list_kernel(cubes, row_blocks, count_ref, rows_ref, cols_ref, words_ref, lists):
    tile_total = cols_ref.shape[0]
    node = lax.axis_index("node")
    cube, member = node // GROUP, node % GROUP
    words = [words_ref[0, at] for at in range(words_ref.shape[1])]
    size = list_size(tile_total)
    for unit in range(cubes):
        lists[unit * size] = 0

    for unit in range(cubes):

        @pl.loop(0, tile_total)
        def _(at):
            entry = unit * size + 1 + 3 * at
            lists[entry] = 0
            lists[entry + 1] = row_blocks
            lists[entry + 2] = 0

    @pl.loop(0, count_ref[0])
    def _(slot):
        column = cols_ref[slot]
        owner = column // row_blocks
        home = owner // GROUP
        unit = jnp.where(home >= cube, home - cube, home - cube + cubes)
        second = column - owner * row_blocks != lowest(owner_mask(words, owner, row_blocks))
        filled = lists[unit * size]
        lists[unit * size] = filled + 1
        entry = unit * size + 1 + 3 * filled
        lists[entry] = slot
        lists[entry + 1] = rows_ref[slot]
        lists[entry + 2] = ((owner - home * GROUP) ^ member) * CAP + jnp.where(second, 1, 0)


def cube_exchange(packed, cubes):
    return lax.all_to_all(
        packed,
        "node",
        split_axis=0,
        concat_axis=0,
        tiled=True,
        axis_index_groups=[
            [cube * GROUP + member for member in range(GROUP)] for cube in range(cubes)
        ],
    )


def make_plan(tile_rows, tile_cols, tile_counts, cubes, row_blocks):
    tile_total = tile_cols.shape[0]
    word_total = -(-cubes * GROUP * row_blocks // 32)
    own = pl.pallas_call(
        words_kernel,
        out_shape=jax.ShapeDtypeStruct((GROUP, word_total), jnp.int32),
        in_specs=[SMEM] * 2,
        out_specs=SMEM,
    )(tile_counts, tile_cols)
    lists = pl.pallas_call(
        functools.partial(list_kernel, cubes, row_blocks),
        out_shape=jax.ShapeDtypeStruct((cubes * list_size(tile_total),), jnp.int32),
        in_specs=[SMEM] * 4,
        out_specs=SMEM,
    )(tile_counts, tile_rows, tile_cols, own)
    return cube_exchange(own, cubes), lists


def pack_kernel(cubes, unit, words_ref, held, *refs):
    packed_hbm, (packed, done) = refs[:GROUP], refs[GROUP:]
    row_blocks = held.shape[1] // BLK
    node = lax.axis_index("node")
    cube, member = node // GROUP, node % GROUP
    owner = (cube + unit) % cubes * GROUP + member
    copies = []
    for step in range(GROUP):
        words = [words_ref[member ^ step, at] for at in range(words_ref.shape[1])]
        mask = owner_mask(words, owner, row_blocks)
        for slot, block in enumerate((lowest(mask), highest(mask))):
            lane = pl.multiple_of(block * BLK, BLK)
            packed[step, slot] = held[:, pl.ds(lane, BLK)]
        copies.append(pltpu.make_async_copy(packed.at[step], packed_hbm[step], done.at[step]))
        copies[-1].start()
    for copy in copies:
        copy.wait()


def pack(cubes, unit, words, held):
    shape = (CAP, held.shape[0], BLK)
    work = RELAY_WORK if unit else 0
    return pl.pallas_call(
        functools.partial(pack_kernel, cubes, unit),
        out_shape=[pltpu.HBM(shape, jnp.bfloat16)] * GROUP,
        in_specs=[SMEM, VMEM],
        out_specs=[HBM] * GROUP,
        scratch_shapes=[
            pltpu.VMEM((GROUP,) + shape, jnp.bfloat16),
            pltpu.SemaphoreType.DMA((GROUP,)),
        ],
        compiler_params=PARAMS,
        cost_estimate=pl.CostEstimate(flops=work, bytes_accessed=0, transcendentals=0),
    )(words, held)


def cube_steps(packed, cubes):
    nodes = cubes * GROUP
    return [packed[0]] + [
        lax.ppermute(packed[step], "node", [(n, n ^ step) for n in range(nodes)])
        for step in STEPS
    ]


def aggregate_kernel(unit, last, lists, tiles, *refs):
    received, refs = refs[:GROUP], refs[GROUP:]
    blocks, refs = refs[-1], refs[:-1]
    size = list_size(tiles.shape[0])
    if unit:
        before_hbm, refs = refs[0], refs[1:]
        before = refs[2]
        fetch = pltpu.make_async_copy(before_hbm, before, refs[3])
        fetch.start()
    out_ref, total = refs[0], refs[1]
    total[...] = jnp.zeros_like(total)
    for step in range(GROUP):
        blocks[step] = received[step][...]

    @pl.loop(0, (lists[unit * size] + UNROLL - 1) // UNROLL)
    def _(group):
        for step in range(UNROLL):
            entry = unit * size + 1 + 3 * (group * UNROLL + step)
            place = lists[entry + 2]
            total[lists[entry + 1]] += lax.dot_general(
                blocks[place // CAP, place % CAP],
                tiles[lists[entry]],
                (((1,), (1,)), ((), ())),
                preferred_element_type=jnp.float32,
            )

    if unit:
        fetch.wait()
    for row in range(total.shape[0] - 1):
        summed = total[row] + before[row] if unit else total[row]
        if last:
            out_ref[:, row * BLK : (row + 1) * BLK] = summed.astype(out_ref.dtype)
        elif unit:
            total[row] = summed
    if not last:
        store = pltpu.make_async_copy(total.at[pl.ds(0, out_ref.shape[0])], out_ref, refs[-1])
        store.start()
        store.wait()


def aggregate(cubes, unit, lists, adj_tiles, received, before, nodes_local):
    feat_local = received[0].shape[1]
    row_blocks = nodes_local // BLK
    last = unit == cubes - 1
    total = (row_blocks, feat_local, BLK)
    scratch = [pltpu.VMEM((row_blocks + 1, feat_local, BLK), jnp.float32)]
    if unit:
        scratch += [pltpu.VMEM(total, jnp.float32), pltpu.SemaphoreType.DMA]
    if not last:
        scratch += [pltpu.SemaphoreType.DMA]
    scratch += [pltpu.VMEM((GROUP,) + received[0].shape, jnp.bfloat16)]
    return pl.pallas_call(
        functools.partial(aggregate_kernel, unit, last),
        out_shape=jax.ShapeDtypeStruct((feat_local, nodes_local), jnp.bfloat16)
        if last
        else pltpu.HBM(total, jnp.float32),
        in_specs=[SMEM] + [VMEM] * (1 + GROUP) + [HBM] * len(before),
        out_specs=VMEM if last else HBM,
        scratch_shapes=scratch,
        compiler_params=PARAMS,
        cost_estimate=pl.CostEstimate(
            flops=2 * adj_tiles.shape[0] * feat_local * BLK * BLK,
            bytes_accessed=2 * (GROUP * received[0].size + adj_tiles.size + feat_local * nodes_local),
            transcendentals=0,
        ),
    )(lists, adj_tiles, *received, *before)


def layer(feat_t, adj_tiles, plan, weight, bias, cubes):
    words, lists = plan
    nodes = cubes * GROUP
    held = [feat_t]
    for unit in range(1, cubes):
        pairs = [(n, (n - unit * GROUP) % nodes) for n in range(nodes)]
        held.append(lax.ppermute(feat_t, "node", pairs))
    before = ()
    for unit in range(cubes):
        received = cube_steps(pack(cubes, unit, words, held[unit]), cubes)
        total = aggregate(cubes, unit, lists, adj_tiles, received, before, feat_t.shape[1])
        before = (pltpu.with_memory_space_constraint(total, pltpu.HBM),)
    summed = jnp.dot(
        weight,
        lax.all_gather(total, "col", axis=0, tiled=True),
        preferred_element_type=jnp.float32,
    )
    return summed + bias[:, None]


def body(x_t, adj_tiles, tile_rows, tile_cols, tile_counts, w_first, b_first, w_second, b_second):
    cubes = lax.axis_size("node") // GROUP
    plan = make_plan(tile_rows, tile_cols, tile_counts, cubes, x_t.shape[1] // BLK)
    z_first = layer(x_t, adj_tiles, plan, w_first, b_first, cubes)
    h_first = jnp.maximum(z_first, 0.0).astype(jnp.bfloat16)
    return layer(h_first, adj_tiles, plan, w_second, b_second, cubes)


def solution(mesh):
    return jax.shard_map(
        body,
        mesh=mesh,
        in_specs=(
            P("col", "node"),
            P("node", None, None),
            P("node"),
            P("node"),
            P("node"),
            P("col", None),
            P("col"),
            P("col", None),
            P("col"),
        ),
        out_specs=P("col", "node"),
        check_vma=False,
    )
```

```python
import functools

import jax
import jax.numpy as jnp
from jax import lax
from jax.experimental import pallas as pl
from jax.experimental.pallas import tpu as pltpu
from jax.sharding import PartitionSpec as P

BLK = 128
CAP = 2
GROUP = 8
NEAR = (0, 1, 2, 4)
STEPS = (7, 3, 6, 5, 1, 2, 4)
PASSED = {1: 2, 2: 4, 4: 1, 7: 0}
DEPTH = 4
SMEM = pl.BlockSpec(memory_space=pltpu.SMEM)
VMEM = pl.BlockSpec(memory_space=pltpu.VMEM)
HBM = pl.BlockSpec(memory_space=pltpu.HBM)
PARAMS = pltpu.CompilerParams(vmem_limit_bytes=24 * 1024 * 1024)


def lowest(mask):
    return jnp.where(mask & 1 != 0, 0, jnp.where(mask & 2 != 0, 1, jnp.where(mask & 4 != 0, 2, 3)))


def highest(mask):
    return jnp.where(mask & 8 != 0, 3, jnp.where(mask & 4 != 0, 2, jnp.where(mask & 2 != 0, 1, 0)))


def owner_mask(words, owner, row_blocks):
    first = owner * row_blocks
    word = words[0]
    for at in range(1, len(words)):
        word = jnp.where(first >> 5 == at, words[at], word)
    return (word >> (first & 31)) & ((1 << row_blocks) - 1)


def words_kernel(count_ref, cols_ref, words_ref):
    live = count_ref[0]
    word_total = words_ref.shape[1]

    def step(slot, found):
        column = cols_ref[slot]
        bit = jnp.where(slot < live, 1 << (column & 31), 0)
        word = column >> 5
        return tuple(one | jnp.where(word == at, bit, 0) for at, one in enumerate(found))

    start = tuple(jnp.int32(0) for _ in range(word_total))
    found = lax.fori_loop(0, cols_ref.shape[0], step, start, unroll=8)
    for member in range(GROUP):
        for at in range(word_total):
            words_ref[member, at] = found[at]


def list_size(tile_total):
    return 1 + 2 * (tile_total + DEPTH)


def list_kernel(cubes, row_blocks, count_ref, rows_ref, cols_ref, words_ref, lists):
    tile_total = cols_ref.shape[0]
    node = lax.axis_index("node")
    cube, member = node // GROUP, node % GROUP
    words = [words_ref[0, at] for at in range(words_ref.shape[1])]
    size = list_size(tile_total)
    for row in range(row_blocks):
        lists[row * size] = 0

    @pl.loop(0, count_ref[0])
    def _(slot):
        column = cols_ref[slot]
        owner = column // row_blocks
        home = owner // GROUP
        unit = jnp.where(home >= cube, home - cube, home - cube + cubes)
        second = column - owner * row_blocks != lowest(owner_mask(words, owner, row_blocks))
        head = rows_ref[slot] * size
        filled = lists[head]
        lists[head] = filled + 1
        lists[head + 1 + 2 * filled] = slot
        step = (owner - home * GROUP) ^ member
        lists[head + 2 + 2 * filled] = (unit * GROUP + step) * CAP + jnp.where(second, 1, 0)

    for row in range(row_blocks):
        filled = lists[row * size]
        for at in range(DEPTH):
            lists[row * size + 1 + 2 * (filled + at)] = 0
            lists[row * size + 2 + 2 * (filled + at)] = cubes * GROUP * CAP


def cube_exchange(packed, cubes):
    return lax.all_to_all(
        packed,
        "node",
        split_axis=0,
        concat_axis=0,
        tiled=True,
        axis_index_groups=[
            [cube * GROUP + member for member in range(GROUP)] for cube in range(cubes)
        ],
    )


def make_plan(tile_rows, tile_cols, tile_counts, cubes, row_blocks):
    tile_total = tile_cols.shape[0]
    word_total = -(-cubes * GROUP * row_blocks // 32)
    own = pl.pallas_call(
        words_kernel,
        out_shape=jax.ShapeDtypeStruct((GROUP, word_total), jnp.int32),
        in_specs=[SMEM] * 2,
        out_specs=SMEM,
    )(tile_counts, tile_cols)
    lists = pl.pallas_call(
        functools.partial(list_kernel, cubes, row_blocks),
        out_shape=jax.ShapeDtypeStruct((row_blocks * list_size(tile_total),), jnp.int32),
        in_specs=[SMEM] * 4,
        out_specs=SMEM,
    )(tile_counts, tile_rows, tile_cols, own)
    return cube_exchange(own, cubes), lists


def named_blocks(words_ref, member, owner, row_blocks):
    words = [words_ref[member, at] for at in range(words_ref.shape[1])]
    mask = owner_mask(words, owner, row_blocks)
    return [pl.multiple_of(block * BLK, BLK) for block in (lowest(mask), highest(mask))]


def pack_kernel(cubes, words_ref, *refs):
    near = dict(zip(NEAR, refs))
    relayed, refs = refs[len(NEAR) : len(NEAR) + cubes - 1], refs[len(NEAR) + cubes - 1 :]
    sent, packed, done = refs[: len(STEPS)], refs[len(STEPS) : -1], refs[-1]
    row_blocks = near[0].shape[1] // BLK
    node = lax.axis_index("node")
    cube, member = node // GROUP, node % GROUP
    copies = []
    for at, step in enumerate(STEPS):
        parts = [(0, PASSED[step], near[PASSED[step]])] if step in PASSED else []
        parts += [(unit, 0, relayed[unit - 1]) for unit in range(1, cubes)]
        for part, (unit, source, held) in enumerate(parts):
            owner = (cube + unit) % cubes * GROUP + (member ^ source)
            lanes = named_blocks(words_ref, member ^ step, owner, row_blocks)
            for slot, lane in enumerate(lanes):
                packed[at][part, slot] = held[:, pl.ds(lane, BLK)]
        copies.append(pltpu.make_async_copy(packed[at], sent[at], done.at[at]))
        copies[-1].start()
    for copy in copies:
        copy.wait()


def pack(cubes, words, near, relayed):
    shapes = [
        (cubes - 1 + (step in PASSED), CAP, near[0].shape[0], BLK) for step in STEPS
    ]
    return pl.pallas_call(
        functools.partial(pack_kernel, cubes),
        out_shape=[pltpu.HBM(shape, jnp.bfloat16) for shape in shapes],
        in_specs=[SMEM] + [VMEM] * (len(near) + len(relayed)),
        out_specs=[HBM] * len(STEPS),
        scratch_shapes=[pltpu.VMEM(shape, jnp.bfloat16) for shape in shapes]
        + [pltpu.SemaphoreType.DMA((len(STEPS),))],
        compiler_params=PARAMS,
    )(words, *near, *relayed)


def aggregate_kernel(cubes, lists, words_ref, tiles, *refs):
    near = dict(zip(NEAR, refs))
    relayed, refs = refs[len(NEAR) : len(NEAR) + cubes - 1], refs[len(NEAR) + cubes - 1 :]
    received, (out_ref, blocks, total) = dict(zip(STEPS, refs)), refs[len(STEPS) :]
    row_blocks = out_ref.shape[1] // BLK
    node = lax.axis_index("node")
    cube, member = node // GROUP, node % GROUP
    blocks[cubes * GROUP, 0] = jnp.zeros_like(blocks[cubes * GROUP, 0])
    whole = [(0, source, near[source]) for source in NEAR]
    whole += [(unit, 0, relayed[unit - 1]) for unit in range(1, cubes)]
    for unit, source, held in whole:
        owner = (cube + unit) % cubes * GROUP + (member ^ source)
        for slot, lane in enumerate(named_blocks(words_ref, member, owner, row_blocks)):
            blocks[unit * GROUP + source, slot] = held[:, pl.ds(lane, BLK)]
    for step in STEPS:
        first = step in PASSED
        if first:
            blocks[step ^ PASSED[step]] = received[step][0]
        for unit in range(1, cubes):
            blocks[unit * GROUP + step] = received[step][unit - 1 + first]

    size = list_size(tiles.shape[0])
    for row in range(row_blocks):
        total[...] = jnp.zeros_like(total)

        @pl.loop(0, (lists[row * size] + DEPTH - 1) // DEPTH)
        def _(group):
            left, right = [], []
            for at in range(DEPTH):
                entry = row * size + 1 + 2 * (group * DEPTH + at)
                place = lists[entry + 1]
                left.append(blocks[place // CAP, place % CAP])
                right.append(tiles[lists[entry]])
            total[...] += lax.dot_general(
                jnp.concatenate(left, axis=1),
                jnp.concatenate(right, axis=1),
                (((1,), (1,)), ((), ())),
                preferred_element_type=jnp.float32,
            )

        out_ref[:, row * BLK : (row + 1) * BLK] = total[...].astype(out_ref.dtype)


def aggregate(cubes, words, lists, adj_tiles, near, relayed, received):
    feat_local, nodes_local = near[0].shape
    operands = [adj_tiles, *near, *relayed, *received]
    return pl.pallas_call(
        functools.partial(aggregate_kernel, cubes),
        out_shape=jax.ShapeDtypeStruct((feat_local, nodes_local), jnp.bfloat16),
        in_specs=[SMEM] * 2 + [VMEM] * len(operands),
        out_specs=VMEM,
        scratch_shapes=[
            pltpu.VMEM((cubes * GROUP + 1, CAP, feat_local, BLK), jnp.bfloat16),
            pltpu.VMEM((feat_local, BLK), jnp.float32),
        ],
        compiler_params=PARAMS,
        cost_estimate=pl.CostEstimate(
            flops=2 * adj_tiles.shape[0] * feat_local * BLK * BLK,
            bytes_accessed=2 * sum(one.size for one in operands),
            transcendentals=0,
        ),
    )(lists, words, *operands)


def layer(feat_t, adj_tiles, plan, weight, bias, cubes):
    words, lists = plan
    nodes = cubes * GROUP

    def to_member(array, step):
        return lax.ppermute(array, "node", [(n, n ^ step) for n in range(nodes)])

    relayed = [
        lax.ppermute(feat_t, "node", [(n, (n - unit * GROUP) % nodes) for n in range(nodes)])
        for unit in range(1, cubes)
    ]
    near = [feat_t] + [to_member(feat_t, step) for step in NEAR[1:]]
    sent = pack(cubes, words, near, relayed)
    received = [to_member(array, step) for array, step in zip(sent, STEPS)]
    summed = jnp.dot(
        weight,
        lax.all_gather(
            aggregate(cubes, words, lists, adj_tiles, near, relayed, received),
            "col",
            axis=0,
            tiled=True,
        ),
        preferred_element_type=jnp.float32,
    )
    return summed + bias[:, None]


def body(x_t, adj_tiles, tile_rows, tile_cols, tile_counts, w_first, b_first, w_second, b_second):
    cubes = lax.axis_size("node") // GROUP
    plan = make_plan(tile_rows, tile_cols, tile_counts, cubes, x_t.shape[1] // BLK)
    z_first = layer(x_t, adj_tiles, plan, w_first, b_first, cubes)
    h_first = jnp.maximum(z_first, 0.0).astype(jnp.bfloat16)
    return layer(h_first, adj_tiles, plan, w_second, b_second, cubes)


def solution(mesh):
    return jax.shard_map(
        body,
        mesh=mesh,
        in_specs=(
            P("col", "node"),
            P("node", None, None),
            P("node"),
            P("node"),
            P("node"),
            P("col", None),
            P("col"),
            P("col", None),
            P("col"),
        ),
        out_specs=P("col", "node"),
        check_vma=False,
    )
```

```python
import functools

import jax
import jax.numpy as jnp
from jax import lax
from jax.experimental import pallas as pl
from jax.experimental.pallas import tpu as pltpu
from jax.sharding import PartitionSpec as P

BLK = 128
CAP = 2
GROUP = 8
NEAR = (0, 1, 2, 4)
STEPS = (7, 6, 5, 4, 3, 1, 2)
PASSED = {1: 2, 2: 4, 4: 1, 7: 0}
DEPTH = 4
WIDTH = 4
SMEM = pl.BlockSpec(memory_space=pltpu.SMEM)
VMEM = pl.BlockSpec(memory_space=pltpu.VMEM)
HBM = pl.BlockSpec(memory_space=pltpu.HBM)
PARAMS = pltpu.CompilerParams(vmem_limit_bytes=24 * 1024 * 1024)


def lowest(mask):
    return jnp.where(mask & 1 != 0, 0, jnp.where(mask & 2 != 0, 1, jnp.where(mask & 4 != 0, 2, 3)))


def highest(mask):
    return jnp.where(mask & 8 != 0, 3, jnp.where(mask & 4 != 0, 2, jnp.where(mask & 2 != 0, 1, 0)))


def owner_mask(words, owner, row_blocks):
    first = owner * row_blocks
    word = words[0]
    for at in range(1, len(words)):
        word = jnp.where(first >> 5 == at, words[at], word)
    return (word >> (first & 31)) & ((1 << row_blocks) - 1)


def words_kernel(count_ref, cols_ref, words_ref):
    live = count_ref[0]
    word_total = words_ref.shape[1]

    def step(slot, found):
        column = cols_ref[slot]
        bit = jnp.where(slot < live, 1 << (column & 31), 0)
        word = column >> 5
        return tuple(one | jnp.where(word == at, bit, 0) for at, one in enumerate(found))

    start = tuple(jnp.int32(0) for _ in range(word_total))
    found = lax.fori_loop(0, cols_ref.shape[0], step, start, unroll=8)
    for at in range(word_total):
        words_ref[0, at] = found[at]


def group_limit(tile_total, row_blocks):
    return -(-(tile_total // DEPTH + row_blocks) // WIDTH) * WIDTH


def list_kernel(cubes, row_blocks, count_ref, rows_ref, cols_ref, words_ref, lists, filled):
    tile_total = cols_ref.shape[0]
    node = lax.axis_index("node")
    cube, member = node // GROUP, node % GROUP
    words = [words_ref[0, at] for at in range(words_ref.shape[1])]
    limit = group_limit(tile_total, row_blocks)

    @pl.loop(0, limit)
    def _(group):
        lists[1 + group] = row_blocks
        for at in range(DEPTH):
            entry = 1 + limit + 2 * (group * DEPTH + at)
            lists[entry] = 0
            lists[entry + 1] = cubes * GROUP * CAP

    for row in range(row_blocks):
        filled[row] = 0

    @pl.loop(0, count_ref[0])
    def _(slot):
        row = rows_ref[slot]
        filled[row] = filled[row] + 1

    start = 0
    for row in range(row_blocks):
        groups = (filled[row] + DEPTH - 1) // DEPTH
        filled[row] = start * DEPTH

        @pl.loop(start, start + groups)
        def _(group):
            lists[1 + group] = row

        start = start + groups
    lists[0] = start

    @pl.loop(0, count_ref[0])
    def _(slot):
        column = cols_ref[slot]
        owner = column // row_blocks
        home = owner // GROUP
        unit = jnp.where(home >= cube, home - cube, home - cube + cubes)
        second = column - owner * row_blocks != lowest(owner_mask(words, owner, row_blocks))
        row = rows_ref[slot]
        entry = 1 + limit + 2 * filled[row]
        filled[row] = filled[row] + 1
        step = (owner - home * GROUP) ^ member
        lists[entry] = slot
        lists[entry + 1] = (unit * GROUP + step) * CAP + jnp.where(second, 1, 0)


def make_plan(tile_rows, tile_cols, tile_counts, cubes, row_blocks):
    tile_total = tile_cols.shape[0]
    word_total = -(-cubes * GROUP * row_blocks // 32)
    list_length = 1 + group_limit(tile_total, row_blocks) * (1 + 2 * DEPTH)
    own = pl.pallas_call(
        words_kernel,
        out_shape=jax.ShapeDtypeStruct((1, word_total), jnp.int32),
        in_specs=[SMEM] * 2,
        out_specs=SMEM,
    )(tile_counts, tile_cols)
    lists = pl.pallas_call(
        functools.partial(list_kernel, cubes, row_blocks),
        out_shape=jax.ShapeDtypeStruct((list_length,), jnp.int32),
        in_specs=[SMEM] * 4,
        out_specs=SMEM,
        scratch_shapes=[pltpu.SMEM((row_blocks,), jnp.int32)],
    )(tile_counts, tile_rows, tile_cols, own)
    groups = [[cube * GROUP + member for member in range(GROUP)] for cube in range(cubes)]
    words = lax.all_gather(own, "node", axis=0, tiled=True, axis_index_groups=groups)
    return words, lists


def named_blocks(words_ref, member, owner, row_blocks):
    words = [words_ref[member, at] for at in range(words_ref.shape[1])]
    mask = owner_mask(words, owner, row_blocks)
    return [pl.multiple_of(block * BLK, BLK) for block in (lowest(mask), highest(mask))]


def pack_kernel(cubes, words_ref, own_hbm, *refs):
    near = dict(zip(NEAR[1:], refs))
    relayed, refs = refs[len(NEAR) - 1 :][: cubes - 1], refs[len(NEAR) + cubes - 2 :]
    sent, packed, (near[0], done) = refs[: len(STEPS)], refs[len(STEPS) : -2], refs[-2:]
    row_blocks = near[0].shape[1] // BLK
    node = lax.axis_index("node")
    cube, member = node // GROUP, node % GROUP
    fetch = pltpu.make_async_copy(own_hbm, near[0], done.at[len(STEPS)])
    fetch.start()
    copies = []
    for at, step in sorted(enumerate(STEPS), key=lambda pair: PASSED.get(pair[1]) == 0):
        parts = [(unit, 0, relayed[unit - 1]) for unit in range(1, cubes)]
        if step in PASSED:
            if PASSED[step] == 0:
                fetch.wait()
            parts.append((0, PASSED[step], near[PASSED[step]]))
        for part, (unit, source, held) in enumerate(parts):
            owner = (cube + unit) % cubes * GROUP + (member ^ source)
            lanes = named_blocks(words_ref, member ^ step, owner, row_blocks)
            for slot, lane in enumerate(lanes):
                packed[at][part, slot] = held[:, pl.ds(lane, BLK)]
        copies.append(pltpu.make_async_copy(packed[at], sent[at], done.at[at]))
        copies[-1].start()
    for copy in copies:
        copy.wait()


def pack(cubes, words, near, relayed):
    shapes = [
        (cubes - 1 + (step in PASSED), CAP, near[0].shape[0], BLK) for step in STEPS
    ]
    return pl.pallas_call(
        functools.partial(pack_kernel, cubes),
        out_shape=[pltpu.HBM(shape, jnp.bfloat16) for shape in shapes],
        in_specs=[SMEM, HBM] + [VMEM] * (len(near) - 1 + len(relayed)),
        out_specs=[HBM] * len(STEPS),
        scratch_shapes=[pltpu.VMEM(shape, jnp.bfloat16) for shape in shapes]
        + [pltpu.VMEM(near[0].shape, jnp.bfloat16)]
        + [pltpu.SemaphoreType.DMA((len(STEPS) + 1,))],
        compiler_params=PARAMS,
    )(words, in_hbm(near[0]), *near[1:], *relayed)


def in_hbm(array):
    return pltpu.with_memory_space_constraint(array, pltpu.HBM)


def kept_sources(cubes):
    return [(unit, 0) for unit in range(1, cubes)] + [(0, source) for source in NEAR]


def keep_kernel(cubes, words_ref, *refs):
    held, kept = refs[:-1], refs[-1]
    row_blocks = held[0].shape[1] // BLK
    node = lax.axis_index("node")
    cube, member = node // GROUP, node % GROUP
    for at, (unit, source) in enumerate(kept_sources(cubes)):
        owner = (cube + unit) % cubes * GROUP + (member ^ source)
        for slot, lane in enumerate(named_blocks(words_ref, member, owner, row_blocks)):
            kept[at, slot] = held[at][:, pl.ds(lane, BLK)]


def keep(cubes, words, held):
    shape = (len(held), CAP, held[0].shape[0], BLK)
    return pl.pallas_call(
        functools.partial(keep_kernel, cubes),
        out_shape=jax.ShapeDtypeStruct(shape, jnp.bfloat16),
        in_specs=[SMEM] + [VMEM] * len(held),
        out_specs=VMEM,
        compiler_params=PARAMS,
    )(words, *held)


def aggregate_kernel(cubes, limit, lists_hbm, tiles_hbm, kept, *refs):
    received, refs = dict(zip(STEPS, refs)), refs[len(STEPS) :]
    out_ref, lists, tiles, blocks, total, done = refs
    copies = [
        pltpu.make_async_copy(lists_hbm, lists, done.at[0]),
        pltpu.make_async_copy(tiles_hbm, tiles, done.at[1]),
    ]
    for copy in copies:
        copy.start()
    total[...] = jnp.zeros_like(total)
    blocks[cubes * GROUP, 0] = jnp.zeros_like(blocks[cubes * GROUP, 0])
    for at, (unit, source) in enumerate(kept_sources(cubes)):
        blocks[unit * GROUP + source] = kept[at]
    for step in STEPS:
        for unit in range(1, cubes):
            blocks[unit * GROUP + step] = received[step][unit - 1]
        if step in PASSED:
            blocks[step ^ PASSED[step]] = received[step][cubes - 1]
    for copy in copies:
        copy.wait()

    @pl.loop(0, (lists[0] + WIDTH - 1) // WIDTH)
    def _(loop_step):
        sums = []
        for wide in range(WIDTH):
            group = loop_step * WIDTH + wide
            left, right = [], []
            for at in range(DEPTH):
                entry = 1 + limit + 2 * (group * DEPTH + at)
                place = lists[entry + 1]
                left.append(blocks[place // CAP, place % CAP])
                right.append(tiles[lists[entry]])
            summed = lax.dot_general(
                jnp.concatenate(left, axis=1),
                jnp.concatenate(right, axis=1),
                (((1,), (1,)), ((), ())),
                preferred_element_type=jnp.float32,
            )
            sums.append((lists[1 + group], summed))
        for row, summed in sums:
            total[row] += summed

    for row in range(out_ref.shape[1] // BLK):
        out_ref[:, row * BLK : (row + 1) * BLK] = total[row].astype(out_ref.dtype)


def aggregate(cubes, lists, adj_tiles, kept, received, nodes_local):
    feat_local = kept.shape[2]
    row_blocks = nodes_local // BLK
    operands = [adj_tiles, kept, *received]
    return pl.pallas_call(
        functools.partial(
            aggregate_kernel, cubes, group_limit(adj_tiles.shape[0], row_blocks)
        ),
        out_shape=jax.ShapeDtypeStruct((feat_local, nodes_local), jnp.bfloat16),
        in_specs=[HBM] * 2 + [VMEM] * (1 + len(received)),
        out_specs=VMEM,
        scratch_shapes=[
            pltpu.SMEM(lists.shape, jnp.int32),
            pltpu.VMEM(adj_tiles.shape, jnp.bfloat16),
            pltpu.VMEM((cubes * GROUP + 1, CAP, feat_local, BLK), jnp.bfloat16),
            pltpu.VMEM((row_blocks + 1, feat_local, BLK), jnp.float32),
            pltpu.SemaphoreType.DMA((2,)),
        ],
        compiler_params=PARAMS,
        cost_estimate=pl.CostEstimate(
            flops=2 * adj_tiles.shape[0] * feat_local * BLK * BLK,
            bytes_accessed=2 * sum(one.size for one in operands),
            transcendentals=0,
        ),
    )(in_hbm(lists), in_hbm(adj_tiles), kept, *received)


def gather_sums(feat_t, adj_tiles, plan, cubes):
    words, lists = plan
    nodes = cubes * GROUP

    def to_member(array, step):
        return lax.ppermute(array, "node", [(n, n ^ step) for n in range(nodes)])

    relayed = [
        lax.ppermute(feat_t, "node", [(n, (n - unit * GROUP) % nodes) for n in range(nodes)])
        for unit in range(1, cubes)
    ]
    near = [feat_t] + [to_member(feat_t, step) for step in NEAR[1:]]
    sent = pack(cubes, words, near, relayed)
    received = [to_member(array, step) for array, step in zip(sent, STEPS)]
    kept = keep(cubes, words, relayed + near)
    local = aggregate(cubes, lists, adj_tiles, kept, received, feat_t.shape[1])
    return lax.all_gather(local, "col", axis=0, tiled=True)


def dense_kernel(weight, aggregated, bias, out_ref):
    out_ref[...] = (
        jnp.dot(weight[...], aggregated[...], preferred_element_type=jnp.float32) + bias[...]
    )


def dense(weight, aggregated, bias):
    return pl.pallas_call(
        dense_kernel,
        out_shape=jax.ShapeDtypeStruct((weight.shape[0], aggregated.shape[1]), jnp.float32),
        in_specs=[VMEM] * 3,
        out_specs=VMEM,
        compiler_params=PARAMS,
        cost_estimate=pl.CostEstimate(
            flops=2 * weight.size * aggregated.shape[1],
            bytes_accessed=2 * (weight.size + 3 * aggregated.size),
            transcendentals=0,
        ),
    )(weight, aggregated, bias[:, None])


def body(x_t, adj_tiles, tile_rows, tile_cols, tile_counts, w_first, b_first, w_second, b_second):
    cubes = lax.axis_size("node") // GROUP
    plan = make_plan(tile_rows, tile_cols, tile_counts, cubes, x_t.shape[1] // BLK)
    y_first = gather_sums(x_t, adj_tiles, plan, cubes)
    z_first = jnp.dot(w_first, y_first, preferred_element_type=jnp.float32) + b_first[:, None]
    h_first = jnp.maximum(z_first, 0.0).astype(jnp.bfloat16)
    y_second = gather_sums(h_first, adj_tiles, plan, cubes)
    return dense(w_second, y_second, b_second)


def solution(mesh):
    return jax.shard_map(
        body,
        mesh=mesh,
        in_specs=(
            P("col", "node"),
            P("node", None, None),
            P("node"),
            P("node"),
            P("node"),
            P("col", None),
            P("col"),
            P("col", None),
            P("col"),
        ),
        out_specs=P("col", "node"),
        check_vma=False,
    )
```

```python
import functools

import jax
import jax.numpy as jnp
from jax import lax
from jax.experimental import pallas as pl
from jax.experimental.pallas import tpu as pltpu
from jax.sharding import PartitionSpec as P

BLK = 128
CAP = 2
GROUP = 8
NEAR = (0, 1, 2, 4)
PASSED = {7: 0, 4: 1, 1: 2, 2: 4}
EVEN = (0, 3, 5, 6)
DEPTH = 4
WIDTH = 4
SMEM = pl.BlockSpec(memory_space=pltpu.SMEM)
VMEM = pl.BlockSpec(memory_space=pltpu.VMEM)
HBM = pl.BlockSpec(memory_space=pltpu.HBM)
PARAMS = pltpu.CompilerParams(vmem_limit_bytes=24 * 1024 * 1024)


def lowest(mask):
    return jnp.where(mask & 1 != 0, 0, jnp.where(mask & 2 != 0, 1, jnp.where(mask & 4 != 0, 2, 3)))


def highest(mask):
    return jnp.where(mask & 8 != 0, 3, jnp.where(mask & 4 != 0, 2, jnp.where(mask & 2 != 0, 1, 0)))


def owner_mask(words, owner, row_blocks):
    first = owner * row_blocks
    word = words[0]
    for at in range(1, len(words)):
        word = jnp.where(first >> 5 == at, words[at], word)
    return (word >> (first & 31)) & ((1 << row_blocks) - 1)


def words_kernel(count_ref, cols_ref, words_ref):
    live = count_ref[0]
    word_total = words_ref.shape[1]

    def step(slot, found):
        column = cols_ref[slot]
        bit = jnp.where(slot < live, 1 << (column & 31), 0)
        word = column >> 5
        return tuple(one | jnp.where(word == at, bit, 0) for at, one in enumerate(found))

    start = tuple(jnp.int32(0) for _ in range(word_total))
    found = lax.fori_loop(0, cols_ref.shape[0], step, start, unroll=8)
    for at in range(word_total):
        words_ref[0, at] = found[at]


def group_limit(tile_total, row_blocks):
    return -(-(tile_total // DEPTH + row_blocks) // WIDTH) * WIDTH


def list_kernel(cubes, row_blocks, count_ref, rows_ref, cols_ref, words_ref, lists, filled):
    tile_total = cols_ref.shape[0]
    node = lax.axis_index("node")
    cube, member = node // GROUP, node % GROUP
    words = [words_ref[0, at] for at in range(words_ref.shape[1])]
    limit = group_limit(tile_total, row_blocks)

    @pl.loop(0, limit)
    def _(group):
        lists[1 + group] = row_blocks
        for at in range(DEPTH):
            entry = 1 + limit + 2 * (group * DEPTH + at)
            lists[entry] = 0
            lists[entry + 1] = cubes * GROUP * CAP

    for row in range(row_blocks):
        filled[row] = 0

    @pl.loop(0, count_ref[0])
    def _(slot):
        row = rows_ref[slot]
        filled[row] = filled[row] + 1

    start = 0
    for row in range(row_blocks):
        groups = (filled[row] + DEPTH - 1) // DEPTH
        filled[row] = start * DEPTH

        @pl.loop(start, start + groups)
        def _(group):
            lists[1 + group] = row

        start = start + groups
    lists[0] = start

    @pl.loop(0, count_ref[0])
    def _(slot):
        column = cols_ref[slot]
        owner = column // row_blocks
        home = owner // GROUP
        unit = jnp.where(home >= cube, home - cube, home - cube + cubes)
        second = column - owner * row_blocks != lowest(owner_mask(words, owner, row_blocks))
        row = rows_ref[slot]
        entry = 1 + limit + 2 * filled[row]
        filled[row] = filled[row] + 1
        step = (owner - home * GROUP) ^ member
        lists[entry] = slot
        lists[entry + 1] = (unit * GROUP + step) * CAP + jnp.where(second, 1, 0)


def make_plan(tile_rows, tile_cols, tile_counts, cubes, row_blocks):
    tile_total = tile_cols.shape[0]
    word_total = -(-cubes * GROUP * row_blocks // 32)
    list_length = 1 + group_limit(tile_total, row_blocks) * (1 + 2 * DEPTH)
    own = pl.pallas_call(
        words_kernel,
        out_shape=jax.ShapeDtypeStruct((1, word_total), jnp.int32),
        in_specs=[SMEM] * 2,
        out_specs=SMEM,
    )(tile_counts, tile_cols)
    lists = pl.pallas_call(
        functools.partial(list_kernel, cubes, row_blocks),
        out_shape=jax.ShapeDtypeStruct((list_length,), jnp.int32),
        in_specs=[SMEM] * 4,
        out_specs=SMEM,
        scratch_shapes=[pltpu.SMEM((row_blocks,), jnp.int32)],
    )(tile_counts, tile_rows, tile_cols, own)
    groups = [[cube * GROUP + member for member in range(GROUP)] for cube in range(cubes)]
    words = exchange(jnp.broadcast_to(own, (GROUP, word_total)), groups)
    return words, lists


def exchange(array, groups):
    return lax.all_to_all(
        array, "node", split_axis=0, concat_axis=0, tiled=True, axis_index_groups=groups
    )


def named_blocks(words_ref, member, owner, row_blocks):
    words = [words_ref[member, at] for at in range(words_ref.shape[1])]
    mask = owner_mask(words, owner, row_blocks)
    return [pl.multiple_of(block * BLK, BLK) for block in (lowest(mask), highest(mask))]


def even_member(member):
    parity = (member ^ (member >> 1) ^ (member >> 2)) & 1
    return member ^ parity, parity


def pack_kernel(cubes, fetched, words_ref, *refs):
    relayed, refs = refs[: cubes - 1], refs[cubes - 1 :]
    near, refs = dict(zip(NEAR, refs)), refs[len(NEAR) :]
    total = len(PASSED) + 1
    sent, packed, done = refs[:total], refs[total : 2 * total], refs[2 * total]
    row_blocks = near[0].shape[1] // BLK
    node = lax.axis_index("node")
    cube, member = node // GROUP, node % GROUP
    _, parity = even_member(member)

    def fill(target, other, unit, source, held):
        owner = (cube + unit) % cubes * GROUP + (member ^ source)
        for slot, lane in enumerate(named_blocks(words_ref, other, owner, row_blocks)):
            target[slot] = held[:, pl.ds(lane, BLK)]

    if fetched:
        own, near[0] = near[0], refs[-1]
        fetch = pltpu.make_async_copy(own, near[0], done.at[total])
        fetch.start()
    copies = []
    for at, step in reversed(list(enumerate(PASSED))):
        for unit in range(1, cubes):
            fill(packed[at].at[unit], member ^ step, unit, 0, relayed[unit - 1])
        source = PASSED[step]
        if fetched and source == 0:
            fetch.wait()
        fill(packed[at].at[0], member ^ step, 0, source, near[source])
        copies.append(pltpu.make_async_copy(packed[at], sent[at], done.at[at]))
        copies[-1].start()
    for at, even in enumerate(EVEN):
        for unit in range(1, cubes):
            fill(packed[-1].at[at, unit - 1], even ^ parity, unit, 0, relayed[unit - 1])
    copies.append(pltpu.make_async_copy(packed[-1], sent[-1], done.at[total - 1]))
    copies[-1].start()
    for copy in copies:
        copy.wait()


def pack(cubes, fetched, words, near, relayed):
    shapes = [(cubes, CAP, near[0].shape[0], BLK)] * len(PASSED)
    shapes += [(len(EVEN), cubes - 1, CAP, near[0].shape[0], BLK)]
    scratch = [pltpu.VMEM(shape, jnp.bfloat16) for shape in shapes]
    scratch += [pltpu.SemaphoreType.DMA((len(shapes) + 1,))]
    if fetched:
        scratch += [pltpu.VMEM(near[0].shape, jnp.bfloat16)]
    return pl.pallas_call(
        functools.partial(pack_kernel, cubes, fetched),
        out_shape=[pltpu.HBM(shape, jnp.bfloat16) for shape in shapes],
        in_specs=[SMEM] + [VMEM] * len(relayed) + [HBM if fetched else VMEM] + [VMEM] * 3,
        out_specs=[HBM] * len(shapes),
        scratch_shapes=scratch,
        compiler_params=PARAMS,
    )(words, *relayed, in_hbm(near[0]) if fetched else near[0], *near[1:])


def in_hbm(array):
    return pltpu.with_memory_space_constraint(array, pltpu.HBM)


def keep_kernel(cubes, whole, words_ref, *refs):
    held, kept = refs[:-1], refs[-1]
    row_blocks = held[0].shape[1] // BLK
    node = lax.axis_index("node")
    cube, member = node // GROUP, node % GROUP
    for at, (unit, source) in enumerate(whole):
        owner = (cube + unit) % cubes * GROUP + (member ^ source)
        for slot, lane in enumerate(named_blocks(words_ref, member, owner, row_blocks)):
            kept[at, slot] = held[at][:, pl.ds(lane, BLK)]


def keep(cubes, whole, words, held):
    shape = (len(held), CAP, held[0].shape[0], BLK)
    return pl.pallas_call(
        functools.partial(keep_kernel, cubes, whole),
        out_shape=jax.ShapeDtypeStruct(shape, jnp.bfloat16),
        in_specs=[SMEM] + [VMEM] * len(held),
        out_specs=VMEM,
        compiler_params=PARAMS,
    )(words, *held)


def aggregate_kernel(cubes, limit, whole, lists_hbm, tiles_hbm, kept, *refs):
    received, refs = dict(zip(PASSED, refs)), refs[len(PASSED) :]
    alike, out_ref, lists, tiles, blocks, total, done = refs
    copies = [
        pltpu.make_async_copy(lists_hbm, lists, done.at[0]),
        pltpu.make_async_copy(tiles_hbm, tiles, done.at[1]),
    ]
    for copy in copies:
        copy.start()
    total[...] = jnp.zeros_like(total)
    blocks[cubes * GROUP, 0] = jnp.zeros_like(blocks[cubes * GROUP, 0])
    own, _ = even_member(lax.axis_index("node") % GROUP)
    for unit in range(1, cubes):
        for at, even in enumerate(EVEN):
            blocks[unit * GROUP + (even ^ own)] = alike[at, unit - 1]
    for at, (unit, source) in enumerate(whole):
        blocks[unit * GROUP + source] = kept[at]
    for step, source in PASSED.items():
        blocks[step ^ source] = received[step][0]
        for unit in range(1, cubes):
            blocks[unit * GROUP + step] = received[step][unit]
    for copy in copies:
        copy.wait()

    @pl.loop(0, (lists[0] + WIDTH - 1) // WIDTH)
    def _(loop_step):
        sums = []
        for wide in range(WIDTH):
            group = loop_step * WIDTH + wide
            left, right = [], []
            for at in range(DEPTH):
                entry = 1 + limit + 2 * (group * DEPTH + at)
                place = lists[entry + 1]
                left.append(blocks[place // CAP, place % CAP])
                right.append(tiles[lists[entry]])
            summed = lax.dot_general(
                jnp.concatenate(left, axis=1),
                jnp.concatenate(right, axis=1),
                (((1,), (1,)), ((), ())),
                preferred_element_type=jnp.float32,
            )
            sums.append((lists[1 + group], summed))
        for row, summed in sums:
            total[row] += summed

    for row in range(out_ref.shape[1] // BLK):
        out_ref[:, row * BLK : (row + 1) * BLK] = total[row].astype(out_ref.dtype)


def aggregate(cubes, whole, lists, adj_tiles, kept, received, nodes_local):
    feat_local = kept.shape[2]
    row_blocks = nodes_local // BLK
    operands = [adj_tiles, kept, *received]
    return pl.pallas_call(
        functools.partial(
            aggregate_kernel, cubes, group_limit(adj_tiles.shape[0], row_blocks), whole
        ),
        out_shape=jax.ShapeDtypeStruct((feat_local, nodes_local), jnp.bfloat16),
        in_specs=[HBM] * 2 + [VMEM] * (1 + len(received)),
        out_specs=VMEM,
        scratch_shapes=[
            pltpu.SMEM(lists.shape, jnp.int32),
            pltpu.VMEM(adj_tiles.shape, jnp.bfloat16),
            pltpu.VMEM((cubes * GROUP + 1, CAP, feat_local, BLK), jnp.bfloat16),
            pltpu.VMEM((row_blocks + 1, feat_local, BLK), jnp.float32),
            pltpu.SemaphoreType.DMA((2,)),
        ],
        compiler_params=PARAMS,
        cost_estimate=pl.CostEstimate(
            flops=2 * adj_tiles.shape[0] * feat_local * BLK * BLK,
            bytes_accessed=2 * sum(one.size for one in operands),
            transcendentals=0,
        ),
    )(in_hbm(lists), in_hbm(adj_tiles), kept, *received)


def gather_sums(feat_t, adj_tiles, plan, cubes, fetched):
    words, lists = plan
    nodes = cubes * GROUP

    def to_member(array, step):
        return lax.ppermute(array, "node", [(n, n ^ step) for n in range(nodes)])

    relayed = [
        lax.ppermute(feat_t, "node", [(n, (n - unit * GROUP) % nodes) for n in range(nodes)])
        for unit in range(1, cubes)
    ]
    near = [feat_t] + [to_member(feat_t, step) for step in NEAR[1:]]
    sent = pack(cubes, fetched, words, near, relayed)
    received = [to_member(array, step) for array, step in zip(sent, PASSED)]
    groups = [
        [cube * GROUP + (even ^ parity) for even in EVEN]
        for cube in range(cubes)
        for parity in range(2)
    ]
    received.append(exchange(sent[-1], groups))
    own_cube = [((0, source), array) for source, array in zip(NEAR, near)]
    others = [((unit, 0), array) for unit, array in enumerate(relayed, 1)]
    ahead = 0 if fetched else 3
    whole, held = zip(*(own_cube[:ahead] + others + own_cube[ahead:]))
    kept = keep(cubes, whole, words, held)
    local = aggregate(cubes, whole, lists, adj_tiles, kept, received, feat_t.shape[1])
    return lax.all_gather(local, "col", axis=0, tiled=True)


def dense_kernel(weight, aggregated, bias, out_ref):
    out_ref[...] = (
        jnp.dot(weight[...], aggregated[...], preferred_element_type=jnp.float32) + bias[...]
    )


def dense(weight, aggregated, bias):
    return pl.pallas_call(
        dense_kernel,
        out_shape=jax.ShapeDtypeStruct((weight.shape[0], aggregated.shape[1]), jnp.float32),
        in_specs=[VMEM] * 3,
        out_specs=VMEM,
        compiler_params=PARAMS,
        cost_estimate=pl.CostEstimate(
            flops=2 * weight.size * aggregated.shape[1],
            bytes_accessed=2 * (weight.size + 3 * aggregated.size),
            transcendentals=0,
        ),
    )(weight, aggregated, bias[:, None])


def body(x_t, adj_tiles, tile_rows, tile_cols, tile_counts, w_first, b_first, w_second, b_second):
    cubes = lax.axis_size("node") // GROUP
    plan = make_plan(tile_rows, tile_cols, tile_counts, cubes, x_t.shape[1] // BLK)
    y_first = gather_sums(x_t, adj_tiles, plan, cubes, True)
    z_first = jnp.dot(w_first, y_first, preferred_element_type=jnp.float32) + b_first[:, None]
    h_first = jnp.maximum(z_first, 0.0).astype(jnp.bfloat16)
    y_second = gather_sums(h_first, adj_tiles, plan, cubes, False)
    return dense(w_second, y_second, b_second)


def solution(mesh):
    return jax.shard_map(
        body,
        mesh=mesh,
        in_specs=(
            P("col", "node"),
            P("node", None, None),
            P("node"),
            P("node"),
            P("node"),
            P("col", None),
            P("col"),
            P("col", None),
            P("col"),
        ),
        out_specs=P("col", "node"),
        check_vma=False,
    )
```

```python
import functools

import jax
import jax.numpy as jnp
from jax import lax
from jax.experimental import pallas as pl
from jax.experimental.pallas import tpu as pltpu
from jax.sharding import PartitionSpec as P

BLK = 128
CAP = 2
GROUP = 8
NEAR = (0, 1, 2, 4)
PASSED = {7: 0, 4: 1, 1: 2, 2: 4}
DEPTH = 4
WIDTH = 4
SMEM = pl.BlockSpec(memory_space=pltpu.SMEM)
VMEM = pl.BlockSpec(memory_space=pltpu.VMEM)
HBM = pl.BlockSpec(memory_space=pltpu.HBM)
PARAMS = pltpu.CompilerParams(vmem_limit_bytes=24 * 1024 * 1024)


def lowest(mask):
    return jnp.where(mask & 1 != 0, 0, jnp.where(mask & 2 != 0, 1, jnp.where(mask & 4 != 0, 2, 3)))


def highest(mask):
    return jnp.where(mask & 8 != 0, 3, jnp.where(mask & 4 != 0, 2, jnp.where(mask & 2 != 0, 1, 0)))


def owner_mask(words, owner, row_blocks):
    first = owner * row_blocks
    word = words[0]
    for at in range(1, len(words)):
        word = jnp.where(first >> 5 == at, words[at], word)
    return (word >> (first & 31)) & ((1 << row_blocks) - 1)


def words_kernel(count_ref, cols_ref, words_ref):
    live = count_ref[0]
    word_total = words_ref.shape[1]

    def step(slot, found):
        column = cols_ref[slot]
        bit = jnp.where(slot < live, 1 << (column & 31), 0)
        word = column >> 5
        return tuple(one | jnp.where(word == at, bit, 0) for at, one in enumerate(found))

    start = tuple(jnp.int32(0) for _ in range(word_total))
    found = lax.fori_loop(0, cols_ref.shape[0], step, start, unroll=8)
    for at in range(word_total):
        words_ref[0, at] = found[at]


def group_limit(tile_total, row_blocks):
    return -(-(tile_total // DEPTH + row_blocks) // WIDTH) * WIDTH


def list_kernel(cubes, row_blocks, count_ref, rows_ref, cols_ref, words_ref, lists, filled):
    tile_total = cols_ref.shape[0]
    node = lax.axis_index("node")
    cube, member = node // GROUP, node % GROUP
    words = [words_ref[0, at] for at in range(words_ref.shape[1])]
    limit = group_limit(tile_total, row_blocks)

    @pl.loop(0, limit)
    def _(group):
        lists[1 + group] = row_blocks
        for at in range(DEPTH):
            entry = 1 + limit + 2 * (group * DEPTH + at)
            lists[entry] = 0
            lists[entry + 1] = cubes * GROUP * CAP

    for row in range(row_blocks):
        filled[row] = 0

    @pl.loop(0, count_ref[0])
    def _(slot):
        row = rows_ref[slot]
        filled[row] = filled[row] + 1

    start = 0
    for row in range(row_blocks):
        groups = (filled[row] + DEPTH - 1) // DEPTH
        filled[row] = start * DEPTH

        @pl.loop(start, start + groups)
        def _(group):
            lists[1 + group] = row

        start = start + groups
    lists[0] = start

    @pl.loop(0, count_ref[0])
    def _(slot):
        column = cols_ref[slot]
        owner = column // row_blocks
        home = owner // GROUP
        unit = jnp.where(home >= cube, home - cube, home - cube + cubes)
        second = column - owner * row_blocks != lowest(owner_mask(words, owner, row_blocks))
        row = rows_ref[slot]
        entry = 1 + limit + 2 * filled[row]
        filled[row] = filled[row] + 1
        step = (owner - home * GROUP) ^ member
        lists[entry] = slot
        lists[entry + 1] = (unit * GROUP + step) * CAP + jnp.where(second, 1, 0)


def make_plan(tile_rows, tile_cols, tile_counts, cubes, row_blocks):
    tile_total = tile_cols.shape[0]
    word_total = -(-cubes * GROUP * row_blocks // 32)
    list_length = 1 + group_limit(tile_total, row_blocks) * (1 + 2 * DEPTH)
    own = pl.pallas_call(
        words_kernel,
        out_shape=jax.ShapeDtypeStruct((1, word_total), jnp.int32),
        in_specs=[SMEM] * 2,
        out_specs=SMEM,
    )(tile_counts, tile_cols)
    lists = pl.pallas_call(
        functools.partial(list_kernel, cubes, row_blocks),
        out_shape=jax.ShapeDtypeStruct((list_length,), jnp.int32),
        in_specs=[SMEM] * 4,
        out_specs=SMEM,
        scratch_shapes=[pltpu.SMEM((row_blocks,), jnp.int32)],
    )(tile_counts, tile_rows, tile_cols, own)
    groups = [[cube * GROUP + member for member in range(GROUP)] for cube in range(cubes)]
    words = exchange(jnp.broadcast_to(own, (GROUP, word_total)), groups)
    return words, lists


def exchange(array, groups):
    return lax.all_to_all(
        array, "node", split_axis=0, concat_axis=0, tiled=True, axis_index_groups=groups
    )


def named_blocks(words_ref, member, owner, row_blocks):
    words = [words_ref[member, at] for at in range(words_ref.shape[1])]
    mask = owner_mask(words, owner, row_blocks)
    return [pl.multiple_of(block * BLK, BLK) for block in (lowest(mask), highest(mask))]


def pack_kernel(cubes, whole, fetched, words_ref, *refs):
    held, refs = dict(zip(whole, refs)), refs[len(whole) :]
    total = len(PASSED)
    sent, packed, done = refs[:total], refs[total : 2 * total], refs[2 * total]
    row_blocks = held[0, 0].shape[1] // BLK
    node = lax.axis_index("node")
    cube, member = node // GROUP, node % GROUP
    if fetched:
        own, held[0, 0] = held[0, 0], refs[-1]
        fetch = pltpu.make_async_copy(own, held[0, 0], done.at[total])
        fetch.start()
    copies = []
    for at, (step, source) in reversed(list(enumerate(PASSED.items()))):
        for unit in reversed(range(cubes)):
            if fetched and (unit, source) == (0, 0):
                fetch.wait()
            owner = (cube + unit) % cubes * GROUP + (member ^ source)
            lanes = named_blocks(words_ref, member ^ step, owner, row_blocks)
            for slot, lane in enumerate(lanes):
                packed[at][unit, slot] = held[unit, source][:, pl.ds(lane, BLK)]
        copies.append(pltpu.make_async_copy(packed[at], sent[at], done.at[at]))
        copies[-1].start()
    for copy in copies:
        copy.wait()


def pack(cubes, fetched, words, held):
    feat_local, nodes_local = held[0, 0].shape
    shape = (cubes, CAP, feat_local, BLK)
    scratch = [pltpu.VMEM(shape, jnp.bfloat16)] * len(PASSED)
    scratch += [pltpu.SemaphoreType.DMA((len(PASSED) + 1,))]
    if fetched:
        scratch += [pltpu.VMEM((feat_local, nodes_local), jnp.bfloat16)]
        held = {**held, (0, 0): in_hbm(held[0, 0])}
    return pl.pallas_call(
        functools.partial(pack_kernel, cubes, tuple(held), fetched),
        out_shape=[pltpu.HBM(shape, jnp.bfloat16)] * len(PASSED),
        in_specs=[SMEM] + [HBM if fetched and at == (0, 0) else VMEM for at in held],
        out_specs=[HBM] * len(PASSED),
        scratch_shapes=scratch,
        compiler_params=PARAMS,
    )(words, *held.values())


def in_hbm(array):
    return pltpu.with_memory_space_constraint(array, pltpu.HBM)


def keep_kernel(cubes, whole, words_ref, *refs):
    held, kept = refs[:-1], refs[-1]
    row_blocks = held[0].shape[1] // BLK
    node = lax.axis_index("node")
    cube, member = node // GROUP, node % GROUP
    for at, (unit, source) in enumerate(whole):
        owner = (cube + unit) % cubes * GROUP + (member ^ source)
        for slot, lane in enumerate(named_blocks(words_ref, member, owner, row_blocks)):
            kept[at, slot] = held[at][:, pl.ds(lane, BLK)]


def keep(cubes, words, held):
    shape = (len(held), CAP, held[0, 0].shape[0], BLK)
    return pl.pallas_call(
        functools.partial(keep_kernel, cubes, tuple(held)),
        out_shape=jax.ShapeDtypeStruct(shape, jnp.bfloat16),
        in_specs=[SMEM] + [VMEM] * len(held),
        out_specs=VMEM,
        compiler_params=PARAMS,
    )(words, *held.values())


def aggregate_kernel(cubes, limit, whole, lists_hbm, tiles_hbm, kept, *refs):
    received, refs = dict(zip(PASSED, refs)), refs[len(PASSED) :]
    out_ref, lists, tiles, blocks, total, done = refs
    copies = [
        pltpu.make_async_copy(lists_hbm, lists, done.at[0]),
        pltpu.make_async_copy(tiles_hbm, tiles, done.at[1]),
    ]
    for copy in copies:
        copy.start()
    total[...] = jnp.zeros_like(total)
    blocks[cubes * GROUP, 0] = jnp.zeros_like(blocks[cubes * GROUP, 0])
    for at, (unit, source) in enumerate(whole):
        blocks[unit * GROUP + source] = kept[at]
    for step, source in PASSED.items():
        for unit in range(cubes):
            blocks[unit * GROUP + (step ^ source)] = received[step][unit]
    for copy in copies:
        copy.wait()

    @pl.loop(0, (lists[0] + WIDTH - 1) // WIDTH)
    def _(loop_step):
        sums = []
        for wide in range(WIDTH):
            group = loop_step * WIDTH + wide
            left, right = [], []
            for at in range(DEPTH):
                entry = 1 + limit + 2 * (group * DEPTH + at)
                place = lists[entry + 1]
                left.append(blocks[place // CAP, place % CAP])
                right.append(tiles[lists[entry]])
            summed = lax.dot_general(
                jnp.concatenate(left, axis=1),
                jnp.concatenate(right, axis=1),
                (((1,), (1,)), ((), ())),
                preferred_element_type=jnp.float32,
            )
            sums.append((lists[1 + group], summed))
        for row, summed in sums:
            total[row] += summed

    for row in range(out_ref.shape[1] // BLK):
        out_ref[:, row * BLK : (row + 1) * BLK] = total[row].astype(out_ref.dtype)


def aggregate(cubes, whole, lists, adj_tiles, kept, received, nodes_local):
    feat_local = kept.shape[2]
    row_blocks = nodes_local // BLK
    operands = [adj_tiles, kept, *received]
    return pl.pallas_call(
        functools.partial(
            aggregate_kernel, cubes, group_limit(adj_tiles.shape[0], row_blocks), whole
        ),
        out_shape=jax.ShapeDtypeStruct((feat_local, nodes_local), jnp.bfloat16),
        in_specs=[HBM] * 2 + [VMEM] * (1 + len(received)),
        out_specs=VMEM,
        scratch_shapes=[
            pltpu.SMEM(lists.shape, jnp.int32),
            pltpu.VMEM(adj_tiles.shape, jnp.bfloat16),
            pltpu.VMEM((cubes * GROUP + 1, CAP, feat_local, BLK), jnp.bfloat16),
            pltpu.VMEM((row_blocks + 1, feat_local, BLK), jnp.float32),
            pltpu.SemaphoreType.DMA((2,)),
        ],
        compiler_params=PARAMS,
        cost_estimate=pl.CostEstimate(
            flops=2 * adj_tiles.shape[0] * feat_local * BLK * BLK,
            bytes_accessed=2 * sum(one.size for one in operands),
            transcendentals=0,
        ),
    )(in_hbm(lists), in_hbm(adj_tiles), kept, *received)


def gather_sums(feat_t, adj_tiles, plan, cubes, fetched):
    words, lists = plan
    nodes = cubes * GROUP

    def to_member(array, step):
        return lax.ppermute(array, "node", [(n, n ^ step) for n in range(nodes)])

    relayed = [feat_t] + [
        lax.ppermute(feat_t, "node", [(n, (n - unit * GROUP) % nodes) for n in range(nodes)])
        for unit in range(1, cubes)
    ]
    held = {
        (unit, source): to_member(relayed[unit], source) if source else relayed[unit]
        for unit in range(cubes)
        for source in NEAR
    }
    sent = pack(cubes, fetched, words, held)
    received = [to_member(array, step) for array, step in zip(sent, PASSED)]
    kept = keep(cubes, words, held)
    local = aggregate(cubes, tuple(held), lists, adj_tiles, kept, received, feat_t.shape[1])
    return lax.all_gather(local, "col", axis=0, tiled=True)


def dense_kernel(weight, aggregated, bias, out_ref):
    out_ref[...] = (
        jnp.dot(weight[...], aggregated[...], preferred_element_type=jnp.float32) + bias[...]
    )


def dense(weight, aggregated, bias):
    return pl.pallas_call(
        dense_kernel,
        out_shape=jax.ShapeDtypeStruct((weight.shape[0], aggregated.shape[1]), jnp.float32),
        in_specs=[VMEM] * 3,
        out_specs=VMEM,
        compiler_params=PARAMS,
        cost_estimate=pl.CostEstimate(
            flops=2 * weight.size * aggregated.shape[1],
            bytes_accessed=2 * (weight.size + 3 * aggregated.size),
            transcendentals=0,
        ),
    )(weight, aggregated, bias[:, None])


def body(x_t, adj_tiles, tile_rows, tile_cols, tile_counts, w_first, b_first, w_second, b_second):
    cubes = lax.axis_size("node") // GROUP
    plan = make_plan(tile_rows, tile_cols, tile_counts, cubes, x_t.shape[1] // BLK)
    y_first = gather_sums(x_t, adj_tiles, plan, cubes, True)
    z_first = jnp.dot(w_first, y_first, preferred_element_type=jnp.float32) + b_first[:, None]
    h_first = jnp.maximum(z_first, 0.0).astype(jnp.bfloat16)
    y_second = gather_sums(h_first, adj_tiles, plan, cubes, False)
    return dense(w_second, y_second, b_second)


def solution(mesh):
    return jax.shard_map(
        body,
        mesh=mesh,
        in_specs=(
            P("col", "node"),
            P("node", None, None),
            P("node"),
            P("node"),
            P("node"),
            P("col", None),
            P("col"),
            P("col", None),
            P("col"),
        ),
        out_specs=P("col", "node"),
        check_vma=False,
    )
```

```python
import functools

import jax
import jax.numpy as jnp
from jax import lax
from jax.experimental import pallas as pl
from jax.experimental.pallas import tpu as pltpu
from jax.sharding import PartitionSpec as P

BLK = 128
CAP = 2
GROUP = 8
NEAR = (0, 1, 2, 4)
PASSED = {7: 0, 4: 1, 1: 2, 2: 4}
EVEN = (0, 3, 5, 6)
DEPTH = 4
RELAY_WORK = 50_000_000_000
WIDTH = 4
SMEM = pl.BlockSpec(memory_space=pltpu.SMEM)
VMEM = pl.BlockSpec(memory_space=pltpu.VMEM)
HBM = pl.BlockSpec(memory_space=pltpu.HBM)
PARAMS = pltpu.CompilerParams(vmem_limit_bytes=24 * 1024 * 1024)


def lowest(mask):
    return jnp.where(mask & 1 != 0, 0, jnp.where(mask & 2 != 0, 1, jnp.where(mask & 4 != 0, 2, 3)))


def highest(mask):
    return jnp.where(mask & 8 != 0, 3, jnp.where(mask & 4 != 0, 2, jnp.where(mask & 2 != 0, 1, 0)))


def owner_mask(words, owner, row_blocks):
    first = owner * row_blocks
    word = words[0]
    for at in range(1, len(words)):
        word = jnp.where(first >> 5 == at, words[at], word)
    return (word >> (first & 31)) & ((1 << row_blocks) - 1)


def words_kernel(count_ref, cols_ref, words_ref):
    live = count_ref[0]
    word_total = words_ref.shape[1]

    def step(slot, found):
        column = cols_ref[slot]
        bit = jnp.where(slot < live, 1 << (column & 31), 0)
        word = column >> 5
        return tuple(one | jnp.where(word == at, bit, 0) for at, one in enumerate(found))

    start = tuple(jnp.int32(0) for _ in range(word_total))
    found = lax.fori_loop(0, cols_ref.shape[0], step, start, unroll=8)
    for member in range(GROUP):
        for at in range(word_total):
            words_ref[member, at] = found[at]


def group_limit(tile_total, row_blocks):
    return -(-(tile_total // DEPTH + row_blocks) // WIDTH) * WIDTH


def list_kernel(cubes, row_blocks, count_ref, rows_ref, cols_ref, words_ref, lists, filled):
    tile_total = cols_ref.shape[0]
    node = lax.axis_index("node")
    cube, member = node // GROUP, node % GROUP
    words = [words_ref[0, at] for at in range(words_ref.shape[1])]
    limit = group_limit(tile_total, row_blocks)

    @pl.loop(0, limit)
    def _(group):
        lists[1 + group] = row_blocks
        for at in range(DEPTH):
            entry = 1 + limit + 2 * (group * DEPTH + at)
            lists[entry] = 0
            lists[entry + 1] = cubes * GROUP * CAP

    for row in range(row_blocks):
        filled[row] = 0

    @pl.loop(0, count_ref[0])
    def _(slot):
        row = rows_ref[slot]
        filled[row] = filled[row] + 1

    start = 0
    for row in range(row_blocks):
        groups = (filled[row] + DEPTH - 1) // DEPTH
        filled[row] = start * DEPTH

        @pl.loop(start, start + groups)
        def _(group):
            lists[1 + group] = row

        start = start + groups
    lists[0] = start

    @pl.loop(0, count_ref[0])
    def _(slot):
        column = cols_ref[slot]
        owner = column // row_blocks
        home = owner // GROUP
        unit = jnp.where(home >= cube, home - cube, home - cube + cubes)
        second = column - owner * row_blocks != lowest(owner_mask(words, owner, row_blocks))
        row = rows_ref[slot]
        entry = 1 + limit + 2 * filled[row]
        filled[row] = filled[row] + 1
        step = (owner - home * GROUP) ^ member
        lists[entry] = slot
        lists[entry + 1] = (unit * GROUP + step) * CAP + jnp.where(second, 1, 0)


def make_plan(tile_rows, tile_cols, tile_counts, cubes, row_blocks):
    tile_total = tile_cols.shape[0]
    word_total = -(-cubes * GROUP * row_blocks // 32)
    list_length = 1 + group_limit(tile_total, row_blocks) * (1 + 2 * DEPTH)
    own = pl.pallas_call(
        words_kernel,
        out_shape=jax.ShapeDtypeStruct((GROUP, word_total), jnp.int32),
        in_specs=[SMEM] * 2,
        out_specs=SMEM,
    )(tile_counts, tile_cols)
    lists = pl.pallas_call(
        functools.partial(list_kernel, cubes, row_blocks),
        out_shape=jax.ShapeDtypeStruct((list_length,), jnp.int32),
        in_specs=[SMEM] * 4,
        out_specs=SMEM,
        scratch_shapes=[pltpu.SMEM((row_blocks,), jnp.int32)],
    )(tile_counts, tile_rows, tile_cols, own)
    groups = [[cube * GROUP + member for member in range(GROUP)] for cube in range(cubes)]
    words = exchange(own, groups)
    return words, lists


def exchange(array, groups):
    return lax.all_to_all(
        array, "node", split_axis=0, concat_axis=0, tiled=True, axis_index_groups=groups
    )


def named_blocks(words_ref, member, owner, row_blocks):
    words = [words_ref[member, at] for at in range(words_ref.shape[1])]
    mask = owner_mask(words, owner, row_blocks)
    return [pl.multiple_of(block * BLK, BLK) for block in (lowest(mask), highest(mask))]


def even_member(member):
    parity = (member ^ (member >> 1) ^ (member >> 2)) & 1
    return member ^ parity, parity


def pack_kernel(cubes, whole, messages, alike, fetched, words_ref, *refs):
    held, refs = dict(zip(whole, refs)), refs[len(whole) :]
    total = len(messages) + alike
    sent, packed, done = refs[:total], refs[total : 2 * total], refs[2 * total]
    row_blocks = held[whole[0]].shape[1] // BLK
    node = lax.axis_index("node")
    cube, member = node // GROUP, node % GROUP
    _, parity = even_member(member)

    def fill(target, other, unit, source):
        owner = (cube + unit) % cubes * GROUP + (member ^ source)
        for slot, lane in enumerate(named_blocks(words_ref, other, owner, row_blocks)):
            target[slot] = held[unit, source][:, pl.ds(lane, BLK)]

    if fetched:
        own, held[0, 0] = held[0, 0], refs[-1]
        fetch = pltpu.make_async_copy(own, held[0, 0], done.at[total])
        fetch.start()
    copies = []
    for at, (step, sources) in reversed(list(enumerate(messages))):
        for part, (unit, source) in reversed(list(enumerate(sources))):
            if fetched and (unit, source) == (0, 0):
                fetch.wait()
            fill(packed[at].at[part], member ^ step, unit, source)
        copies.append(pltpu.make_async_copy(packed[at], sent[at], done.at[at]))
        copies[-1].start()
    if alike:
        for at, even in enumerate(EVEN):
            for unit in range(1, cubes):
                fill(packed[-1].at[at, unit - 1], even ^ parity, unit, 0)
        copies.append(pltpu.make_async_copy(packed[-1], sent[-1], done.at[total - 1]))
        copies[-1].start()
    for copy in copies:
        copy.wait()


def pack(cubes, words, held, messages, alike, fetched, work):
    feat_local, nodes_local = next(iter(held.values())).shape
    shapes = [(len(sources), CAP, feat_local, BLK) for _, sources in messages]
    if alike:
        shapes += [(len(EVEN), cubes - 1, CAP, feat_local, BLK)]
    scratch = [pltpu.VMEM(shape, jnp.bfloat16) for shape in shapes]
    scratch += [pltpu.SemaphoreType.DMA((len(shapes) + 1,))]
    if fetched:
        scratch += [pltpu.VMEM((feat_local, nodes_local), jnp.bfloat16)]
        held = {**held, (0, 0): in_hbm(held[0, 0])}
    return pl.pallas_call(
        functools.partial(pack_kernel, cubes, tuple(held), messages, alike, fetched),
        out_shape=[pltpu.HBM(shape, jnp.bfloat16) for shape in shapes],
        in_specs=[SMEM] + [HBM if fetched and at == (0, 0) else VMEM for at in held],
        out_specs=[HBM] * len(shapes),
        scratch_shapes=scratch,
        compiler_params=PARAMS,
        cost_estimate=pl.CostEstimate(flops=work, bytes_accessed=0, transcendentals=0),
    )(words, *held.values())


def in_hbm(array):
    return pltpu.with_memory_space_constraint(array, pltpu.HBM)


def keep_kernel(cubes, whole, words_ref, *refs):
    held, kept = refs[:-1], refs[-1]
    row_blocks = held[0].shape[1] // BLK
    node = lax.axis_index("node")
    cube, member = node // GROUP, node % GROUP
    for at, (unit, source) in enumerate(whole):
        owner = (cube + unit) % cubes * GROUP + (member ^ source)
        for slot, lane in enumerate(named_blocks(words_ref, member, owner, row_blocks)):
            kept[at, slot] = held[at][:, pl.ds(lane, BLK)]


def keep(cubes, words, held):
    shape = (len(held), CAP, held[0, 0].shape[0], BLK)
    return pl.pallas_call(
        functools.partial(keep_kernel, cubes, tuple(held)),
        out_shape=jax.ShapeDtypeStruct(shape, jnp.bfloat16),
        in_specs=[SMEM] + [VMEM] * len(held),
        out_specs=VMEM,
        compiler_params=PARAMS,
    )(words, *held.values())


def aggregate_kernel(cubes, limit, whole, messages, lists_hbm, tiles_hbm, kept, *refs):
    received, refs = refs[: len(messages)], refs[len(messages) :]
    alike, out_ref, lists, tiles, blocks, total, done = refs
    copies = [
        pltpu.make_async_copy(lists_hbm, lists, done.at[0]),
        pltpu.make_async_copy(tiles_hbm, tiles, done.at[1]),
    ]
    for copy in copies:
        copy.start()
    total[...] = jnp.zeros_like(total)
    blocks[cubes * GROUP, 0] = jnp.zeros_like(blocks[cubes * GROUP, 0])
    own, _ = even_member(lax.axis_index("node") % GROUP)
    for unit in range(1, cubes):
        for at, even in enumerate(EVEN):
            blocks[unit * GROUP + (even ^ own)] = alike[at, unit - 1]
    for at, (unit, source) in enumerate(whole):
        blocks[unit * GROUP + source] = kept[at]
    for (step, sources), array in zip(messages, received):
        for part, (unit, source) in enumerate(sources):
            blocks[unit * GROUP + (step ^ source)] = array[part]
    for copy in copies:
        copy.wait()

    @pl.loop(0, (lists[0] + WIDTH - 1) // WIDTH)
    def _(loop_step):
        sums = []
        for wide in range(WIDTH):
            group = loop_step * WIDTH + wide
            left, right = [], []
            for at in range(DEPTH):
                entry = 1 + limit + 2 * (group * DEPTH + at)
                place = lists[entry + 1]
                left.append(blocks[place // CAP, place % CAP])
                right.append(tiles[lists[entry]])
            summed = lax.dot_general(
                jnp.concatenate(left, axis=1),
                jnp.concatenate(right, axis=1),
                (((1,), (1,)), ((), ())),
                preferred_element_type=jnp.float32,
            )
            sums.append((lists[1 + group], summed))
        for row, summed in sums:
            total[row] += summed

    for row in range(out_ref.shape[1] // BLK):
        out_ref[:, row * BLK : (row + 1) * BLK] = total[row].astype(out_ref.dtype)


def aggregate(cubes, whole, messages, lists, adj_tiles, kept, received, nodes_local):
    feat_local = kept.shape[2]
    row_blocks = nodes_local // BLK
    operands = [adj_tiles, kept, *received]
    return pl.pallas_call(
        functools.partial(
            aggregate_kernel,
            cubes,
            group_limit(adj_tiles.shape[0], row_blocks),
            whole,
            messages,
        ),
        out_shape=jax.ShapeDtypeStruct((feat_local, nodes_local), jnp.bfloat16),
        in_specs=[HBM] * 2 + [VMEM] * (1 + len(received)),
        out_specs=VMEM,
        scratch_shapes=[
            pltpu.SMEM(lists.shape, jnp.int32),
            pltpu.VMEM(adj_tiles.shape, jnp.bfloat16),
            pltpu.VMEM((cubes * GROUP + 1, CAP, feat_local, BLK), jnp.bfloat16),
            pltpu.VMEM((row_blocks + 1, feat_local, BLK), jnp.float32),
            pltpu.SemaphoreType.DMA((2,)),
        ],
        compiler_params=PARAMS,
        cost_estimate=pl.CostEstimate(
            flops=2 * adj_tiles.shape[0] * feat_local * BLK * BLK,
            bytes_accessed=2 * sum(one.size for one in operands),
            transcendentals=0,
        ),
    )(in_hbm(lists), in_hbm(adj_tiles), kept, *received)


def gather_sums(feat_t, adj_tiles, plan, cubes, early):
    words, lists = plan
    nodes = cubes * GROUP

    def to_member(array, step):
        return lax.ppermute(array, "node", [(n, n ^ step) for n in range(nodes)])

    relayed = {
        (unit, 0): lax.ppermute(
            feat_t, "node", [(n, (n - unit * GROUP) % nodes) for n in range(nodes)]
        )
        for unit in range(1, cubes)
    }
    near = {(0, step): to_member(feat_t, step) if step else feat_t for step in NEAR}
    messages = [(step, [(0, source)] + list(relayed)) for step, source in PASSED.items()]
    held = {**near, **relayed}
    sent = []
    if early:
        messages = [(7, [(0, 0)]), (7, list(relayed))] + messages[1:]
        own = {(0, 0): held.pop((0, 0))}
        sent += pack(cubes, words, own, messages[:1], False, False, RELAY_WORK)
        sent += pack(cubes, words, held, messages[1:], True, False, 0)
    else:
        sent += pack(cubes, words, held, messages, True, True, 0)
    received = [to_member(array, step) for array, (step, _) in zip(sent, messages)]
    groups = [
        [cube * GROUP + (even ^ parity) for even in EVEN]
        for cube in range(cubes)
        for parity in range(2)
    ]
    received.append(exchange(sent[-1], groups))
    held = {**relayed, **near}
    kept = keep(cubes, words, held)
    local = aggregate(
        cubes, tuple(held), messages, lists, adj_tiles, kept, received, feat_t.shape[1]
    )
    return lax.all_gather(local, "col", axis=0, tiled=True)


def dense_kernel(weight, aggregated, bias, out_ref):
    out_ref[...] = (
        jnp.dot(weight[...], aggregated[...], preferred_element_type=jnp.float32) + bias[...]
    )


def dense(weight, aggregated, bias):
    return pl.pallas_call(
        dense_kernel,
        out_shape=jax.ShapeDtypeStruct((weight.shape[0], aggregated.shape[1]), jnp.float32),
        in_specs=[VMEM] * 3,
        out_specs=VMEM,
        compiler_params=PARAMS,
        cost_estimate=pl.CostEstimate(
            flops=2 * weight.size * aggregated.shape[1],
            bytes_accessed=2 * (weight.size + 3 * aggregated.size),
            transcendentals=0,
        ),
    )(weight, aggregated, bias[:, None])


def body(x_t, adj_tiles, tile_rows, tile_cols, tile_counts, w_first, b_first, w_second, b_second):
    cubes = lax.axis_size("node") // GROUP
    plan = make_plan(tile_rows, tile_cols, tile_counts, cubes, x_t.shape[1] // BLK)
    y_first = gather_sums(x_t, adj_tiles, plan, cubes, False)
    z_first = jnp.dot(w_first, y_first, preferred_element_type=jnp.float32) + b_first[:, None]
    h_first = jnp.maximum(z_first, 0.0).astype(jnp.bfloat16)
    y_second = gather_sums(h_first, adj_tiles, plan, cubes, True)
    return dense(w_second, y_second, b_second)


def solution(mesh):
    return jax.shard_map(
        body,
        mesh=mesh,
        in_specs=(
            P("col", "node"),
            P("node", None, None),
            P("node"),
            P("node"),
            P("node"),
            P("col", None),
            P("col"),
            P("col", None),
            P("col"),
        ),
        out_specs=P("col", "node"),
        check_vma=False,
    )
```

```python
import functools

import jax
import jax.numpy as jnp
from jax import lax
from jax.experimental import pallas as pl
from jax.experimental.pallas import tpu as pltpu
from jax.sharding import PartitionSpec as P

BLK = 128
CAP = 2
GROUP = 8
NEAR = (0, 1, 2, 4)
PASSED = {7: 0, 4: 1, 1: 2, 2: 4}
EVEN = (0, 3, 5, 6)
DEPTH = 4
WIDTH = 4
SMEM = pl.BlockSpec(memory_space=pltpu.SMEM)
VMEM = pl.BlockSpec(memory_space=pltpu.VMEM)
HBM = pl.BlockSpec(memory_space=pltpu.HBM)
PARAMS = pltpu.CompilerParams(vmem_limit_bytes=24 * 1024 * 1024)


def lowest(mask):
    return jnp.where(mask & 1 != 0, 0, jnp.where(mask & 2 != 0, 1, jnp.where(mask & 4 != 0, 2, 3)))


def highest(mask):
    return jnp.where(mask & 8 != 0, 3, jnp.where(mask & 4 != 0, 2, jnp.where(mask & 2 != 0, 1, 0)))


def owner_mask(words, owner, row_blocks):
    first = owner * row_blocks
    word = words[0]
    for at in range(1, len(words)):
        word = jnp.where(first >> 5 == at, words[at], word)
    return (word >> (first & 31)) & ((1 << row_blocks) - 1)


def words_kernel(count_ref, cols_ref, words_ref):
    live = count_ref[0]
    word_total = words_ref.shape[1]

    def step(slot, found):
        column = cols_ref[slot]
        bit = jnp.where(slot < live, 1 << (column & 31), 0)
        word = column >> 5
        return tuple(one | jnp.where(word == at, bit, 0) for at, one in enumerate(found))

    start = tuple(jnp.int32(0) for _ in range(word_total))
    found = lax.fori_loop(0, cols_ref.shape[0], step, start, unroll=8)
    for member in range(GROUP):
        for at in range(word_total):
            words_ref[member, at] = found[at]


def group_limit(tile_total, row_blocks):
    return -(-(tile_total // DEPTH + row_blocks) // WIDTH) * WIDTH


def list_kernel(cubes, row_blocks, count_ref, rows_ref, cols_ref, words_ref, lists, filled):
    tile_total = cols_ref.shape[0]
    node = lax.axis_index("node")
    cube, member = node // GROUP, node % GROUP
    words = [words_ref[0, at] for at in range(words_ref.shape[1])]
    limit = group_limit(tile_total, row_blocks)

    @pl.loop(0, limit)
    def _(group):
        lists[1 + group] = row_blocks
        for at in range(DEPTH):
            entry = 1 + limit + 2 * (group * DEPTH + at)
            lists[entry] = -1
            lists[entry + 1] = 0

    for row in range(row_blocks):
        filled[row] = 0

    @pl.loop(0, count_ref[0])
    def _(slot):
        row = rows_ref[slot]
        filled[row] = filled[row] + 1

    start = 0
    for row in range(row_blocks):
        groups = (filled[row] + DEPTH - 1) // DEPTH
        filled[row] = start * DEPTH

        @pl.loop(start, start + groups)
        def _(group):
            lists[1 + group] = row

        start = start + groups
    lists[0] = start

    @pl.loop(0, count_ref[0])
    def _(slot):
        column = cols_ref[slot]
        owner = column // row_blocks
        home = owner // GROUP
        unit = jnp.where(home >= cube, home - cube, home - cube + cubes)
        second = column - owner * row_blocks != lowest(owner_mask(words, owner, row_blocks))
        row = rows_ref[slot]
        entry = 1 + limit + 2 * filled[row]
        filled[row] = filled[row] + 1
        step = (owner - home * GROUP) ^ member
        lists[entry] = slot
        lists[entry + 1] = (unit * GROUP + step) * CAP + jnp.where(second, 1, 0)


def make_plan(tile_rows, tile_cols, tile_counts, cubes, row_blocks):
    tile_total = tile_cols.shape[0]
    word_total = -(-cubes * GROUP * row_blocks // 32)
    list_length = 1 + group_limit(tile_total, row_blocks) * (1 + 2 * DEPTH)
    own = pl.pallas_call(
        words_kernel,
        out_shape=jax.ShapeDtypeStruct((GROUP, word_total), jnp.int32),
        in_specs=[SMEM] * 2,
        out_specs=SMEM,
    )(tile_counts, tile_cols)
    lists = pl.pallas_call(
        functools.partial(list_kernel, cubes, row_blocks),
        out_shape=jax.ShapeDtypeStruct((list_length,), jnp.int32),
        in_specs=[SMEM] * 4,
        out_specs=SMEM,
        scratch_shapes=[pltpu.SMEM((row_blocks,), jnp.int32)],
    )(tile_counts, tile_rows, tile_cols, own)
    groups = [[cube * GROUP + member for member in range(GROUP)] for cube in range(cubes)]
    words = exchange(own, groups)
    return words, lists


def exchange(array, groups):
    return lax.all_to_all(
        array, "node", split_axis=0, concat_axis=0, tiled=True, axis_index_groups=groups
    )


def named_blocks(words_ref, member, owner, row_blocks):
    words = [words_ref[member, at] for at in range(words_ref.shape[1])]
    mask = owner_mask(words, owner, row_blocks)
    return [pl.multiple_of(block * BLK, BLK) for block in (lowest(mask), highest(mask))]


def even_member(member):
    parity = (member ^ (member >> 1) ^ (member >> 2)) & 1
    return member ^ parity, parity


def pack_kernel(cubes, whole, messages, alike, fetched, words_ref, *refs):
    held, refs = dict(zip(whole, refs)), refs[len(whole) :]
    total = len(messages) + alike
    sent, packed, done = refs[:total], refs[total : 2 * total], refs[2 * total]
    row_blocks = held[whole[0]].shape[1] // BLK
    node = lax.axis_index("node")
    cube, member = node // GROUP, node % GROUP
    _, parity = even_member(member)

    def fill(target, other, unit, source):
        owner = (cube + unit) % cubes * GROUP + (member ^ source)
        for slot, lane in enumerate(named_blocks(words_ref, other, owner, row_blocks)):
            target[slot] = held[unit, source][:, pl.ds(lane, BLK)]

    if fetched:
        own, held[0, 0] = held[0, 0], refs[-1]
        fetch = pltpu.make_async_copy(own, held[0, 0], done.at[total])
        fetch.start()
    copies = []
    for at, (step, sources) in reversed(list(enumerate(messages))):
        for part, (unit, source) in reversed(list(enumerate(sources))):
            if fetched and (unit, source) == (0, 0):
                fetch.wait()
            fill(packed[at].at[part], member ^ step, unit, source)
        copies.append(pltpu.make_async_copy(packed[at], sent[at], done.at[at]))
        copies[-1].start()
    if alike:
        for at, even in enumerate(EVEN):
            for unit in range(1, cubes):
                fill(packed[-1].at[at, unit - 1], even ^ parity, unit, 0)
        copies.append(pltpu.make_async_copy(packed[-1], sent[-1], done.at[total - 1]))
        copies[-1].start()
    for copy in copies:
        copy.wait()


def pack(cubes, words, held, messages, alike, fetched, work):
    feat_local, nodes_local = next(iter(held.values())).shape
    shapes = [(len(sources), CAP, feat_local, BLK) for _, sources in messages]
    if alike:
        shapes += [(len(EVEN), cubes - 1, CAP, feat_local, BLK)]
    scratch = [pltpu.VMEM(shape, jnp.bfloat16) for shape in shapes]
    scratch += [pltpu.SemaphoreType.DMA((len(shapes) + 1,))]
    if fetched:
        scratch += [pltpu.VMEM((feat_local, nodes_local), jnp.bfloat16)]
        held = {**held, (0, 0): in_hbm(held[0, 0])}
    return pl.pallas_call(
        functools.partial(pack_kernel, cubes, tuple(held), messages, alike, fetched),
        out_shape=[pltpu.HBM(shape, jnp.bfloat16) for shape in shapes],
        in_specs=[SMEM] + [HBM if fetched and at == (0, 0) else VMEM for at in held],
        out_specs=[HBM] * len(shapes),
        scratch_shapes=scratch,
        compiler_params=PARAMS,
        cost_estimate=pl.CostEstimate(flops=work, bytes_accessed=0, transcendentals=0),
    )(words, *held.values())


def in_hbm(array):
    return pltpu.with_memory_space_constraint(array, pltpu.HBM)


def keep_kernel(cubes, whole, words_ref, *refs):
    held, kept = refs[:-1], refs[-1]
    row_blocks = held[0].shape[1] // BLK
    node = lax.axis_index("node")
    cube, member = node // GROUP, node % GROUP
    for at, (unit, source) in enumerate(whole):
        owner = (cube + unit) % cubes * GROUP + (member ^ source)
        for slot, lane in enumerate(named_blocks(words_ref, member, owner, row_blocks)):
            kept[at, slot] = held[at][:, pl.ds(lane, BLK)]


def keep(cubes, words, held):
    shape = (len(held), CAP, held[0, 0].shape[0], BLK)
    return pl.pallas_call(
        functools.partial(keep_kernel, cubes, tuple(held)),
        out_shape=jax.ShapeDtypeStruct(shape, jnp.bfloat16),
        in_specs=[SMEM] + [VMEM] * len(held),
        out_specs=VMEM,
        compiler_params=PARAMS,
    )(words, *held.values())


def sort_kernel(limit, lists, tiles, out_ref):
    @pl.loop(0, (lists[0] + WIDTH - 1) // WIDTH * WIDTH)
    def _(group):
        for at in range(DEPTH):
            entry = 1 + limit + 2 * (group * DEPTH + at)
            slot = lists[entry]
            tile = tiles[jnp.maximum(slot, 0)].T
            tile = jnp.where(slot < 0, jnp.zeros_like(tile), tile)
            out_ref[group, at * BLK : (at + 1) * BLK] = tile


def sort_tiles(lists, adj_tiles, row_blocks):
    limit = group_limit(adj_tiles.shape[0], row_blocks)
    return pl.pallas_call(
        functools.partial(sort_kernel, limit),
        out_shape=pltpu.HBM((limit, DEPTH * BLK, BLK), jnp.bfloat16),
        in_specs=[SMEM, VMEM],
        out_specs=VMEM,
        compiler_params=PARAMS,
    )(lists, adj_tiles)


def aggregate_kernel(cubes, limit, whole, messages, lists_hbm, tiles_hbm, kept, *refs):
    received, refs = refs[: len(messages)], refs[len(messages) :]
    alike, out_ref, lists, tiles, blocks, total, done = refs
    steps = limit // WIDTH

    def fetch(step):
        groups = pl.ds(step * WIDTH, WIDTH)
        return pltpu.make_async_copy(tiles_hbm.at[groups], tiles.at[groups], done.at[step])

    listed = pltpu.make_async_copy(lists_hbm, lists, done.at[steps])
    listed.start()
    fetch(0).start()
    total[...] = jnp.zeros_like(total)
    listed.wait()
    used = (lists[0] + WIDTH - 1) // WIDTH

    @pl.loop(1, used)
    def _(step):
        fetch(step).start()

    own, _ = even_member(lax.axis_index("node") % GROUP)
    for unit in range(1, cubes):
        for at, even in enumerate(EVEN):
            blocks[unit * GROUP + (even ^ own)] = alike[at, unit - 1]
    for at, (unit, source) in enumerate(whole):
        blocks[unit * GROUP + source] = kept[at]
    for (step, sources), array in zip(messages, received):
        for part, (unit, source) in enumerate(sources):
            blocks[unit * GROUP + (step ^ source)] = array[part]
    @pl.when(used == 0)
    def _():
        fetch(0).wait()

    @pl.loop(0, used)
    def _(step):
        fetch(step).wait()
        sums = []
        for wide in range(WIDTH):
            group = step * WIDTH + wide
            left = []
            for at in range(DEPTH):
                place = lists[2 + limit + 2 * (group * DEPTH + at)]
                left.append(blocks[place // CAP, place % CAP])
            summed = jnp.dot(
                jnp.concatenate(left, axis=1), tiles[group], preferred_element_type=jnp.float32
            )
            sums.append((lists[1 + group], summed))
        for row, summed in sums:
            total[row] += summed

    for row in range(out_ref.shape[1] // BLK):
        out_ref[:, row * BLK : (row + 1) * BLK] = total[row].astype(out_ref.dtype)


def aggregate(cubes, whole, messages, lists, tiles, kept, received, nodes_local):
    feat_local = kept.shape[2]
    row_blocks = nodes_local // BLK
    limit = tiles.shape[0]
    operands = [tiles, kept, *received]
    return pl.pallas_call(
        functools.partial(
            aggregate_kernel,
            cubes,
            limit,
            whole,
            messages,
        ),
        out_shape=jax.ShapeDtypeStruct((feat_local, nodes_local), jnp.bfloat16),
        in_specs=[HBM] * 2 + [VMEM] * (1 + len(received)),
        out_specs=VMEM,
        scratch_shapes=[
            pltpu.SMEM(lists.shape, jnp.int32),
            pltpu.VMEM(tiles.shape, jnp.bfloat16),
            pltpu.VMEM((cubes * GROUP, CAP, feat_local, BLK), jnp.bfloat16),
            pltpu.VMEM((row_blocks + 1, feat_local, BLK), jnp.float32),
            pltpu.SemaphoreType.DMA((limit // WIDTH + 1,)),
        ],
        compiler_params=PARAMS,
        cost_estimate=pl.CostEstimate(
            flops=2 * limit * DEPTH * feat_local * BLK * BLK,
            bytes_accessed=2 * sum(one.size for one in operands),
            transcendentals=0,
        ),
    )(in_hbm(lists), in_hbm(tiles), kept, *received)


def gather_sums(feat_t, tiles, plan, cubes, early):
    words, lists = plan
    nodes = cubes * GROUP

    def to_member(array, step):
        return lax.ppermute(array, "node", [(n, n ^ step) for n in range(nodes)])

    relayed = {
        (unit, 0): lax.ppermute(
            feat_t, "node", [(n, (n - unit * GROUP) % nodes) for n in range(nodes)]
        )
        for unit in range(1, cubes)
    }
    near = {(0, step): to_member(feat_t, step) if step else feat_t for step in NEAR}
    messages = [(step, [(0, source)] + list(relayed)) for step, source in PASSED.items()]
    held = {**near, **relayed}
    if early:
        messages = [(7, [(0, 0)]), (7, list(relayed))] + messages[1:]
        own = {(0, 0): held.pop((0, 0))}
        first = pack(cubes, words, own, messages[:1], False, False, 0)
        passed = to_member(first[0], 7)
        held, passed = lax.optimization_barrier((held, passed))
        sent = pack(cubes, words, held, messages[1:], True, False, 0)
        received = [passed]
    else:
        sent = list(pack(cubes, words, held, messages, True, True, 0))
        received = []
        sent[0], tiles = lax.optimization_barrier((sent[0], tiles))
        tiles = sort_tiles(lists, tiles, feat_t.shape[1] // BLK)
    steps = [step for step, _ in messages[len(received) :]]
    received += [to_member(array, step) for array, step in zip(sent, steps)]
    groups = [
        [cube * GROUP + (even ^ parity) for even in EVEN]
        for cube in range(cubes)
        for parity in range(2)
    ]
    received.append(exchange(sent[-1], groups))
    held = {**relayed, **near}
    kept = keep(cubes, words, held)
    local = aggregate(
        cubes, tuple(held), messages, lists, tiles, kept, received, feat_t.shape[1]
    )
    return lax.all_gather(local, "col", axis=0, tiled=True), tiles


def dense_kernel(weight, aggregated, bias, out_ref):
    out_ref[...] = (
        jnp.dot(weight[...], aggregated[...], preferred_element_type=jnp.float32) + bias[...]
    )


def dense(weight, aggregated, bias):
    return pl.pallas_call(
        dense_kernel,
        out_shape=jax.ShapeDtypeStruct((weight.shape[0], aggregated.shape[1]), jnp.float32),
        in_specs=[VMEM] * 3,
        out_specs=VMEM,
        compiler_params=PARAMS,
        cost_estimate=pl.CostEstimate(
            flops=2 * weight.size * aggregated.shape[1],
            bytes_accessed=2 * (weight.size + 3 * aggregated.size),
            transcendentals=0,
        ),
    )(weight, aggregated, bias[:, None])


def body(x_t, adj_tiles, tile_rows, tile_cols, tile_counts, w_first, b_first, w_second, b_second):
    cubes = lax.axis_size("node") // GROUP
    plan = make_plan(tile_rows, tile_cols, tile_counts, cubes, x_t.shape[1] // BLK)
    y_first, tiles = gather_sums(x_t, adj_tiles, plan, cubes, False)
    z_first = jnp.dot(w_first, y_first, preferred_element_type=jnp.float32) + b_first[:, None]
    h_first = jnp.maximum(z_first, 0.0).astype(jnp.bfloat16)
    y_second, _ = gather_sums(h_first, tiles, plan, cubes, True)
    return dense(w_second, y_second, b_second)


def solution(mesh):
    return jax.shard_map(
        body,
        mesh=mesh,
        in_specs=(
            P("col", "node"),
            P("node", None, None),
            P("node"),
            P("node"),
            P("node"),
            P("col", None),
            P("col"),
            P("col", None),
            P("col"),
        ),
        out_specs=P("col", "node"),
        check_vma=False,
    )
```

```python
import functools

import jax
import jax.numpy as jnp
from jax import lax
from jax.experimental import pallas as pl
from jax.experimental.pallas import tpu as pltpu
from jax.sharding import PartitionSpec as P

BLK = 128
CAP = 2
GROUP = 8
NEAR = (0, 1, 2, 4)
PASSED = {7: 0, 4: 1, 1: 2, 2: 4}
EVEN = (0, 3, 5, 6)
DEPTH = 4
RELAY_WORK = 50_000_000_000
WIDTH = 4
SMEM = pl.BlockSpec(memory_space=pltpu.SMEM)
VMEM = pl.BlockSpec(memory_space=pltpu.VMEM)
HBM = pl.BlockSpec(memory_space=pltpu.HBM)
PARAMS = pltpu.CompilerParams(vmem_limit_bytes=24 * 1024 * 1024)


def lowest(mask):
    return jnp.where(mask & 1 != 0, 0, jnp.where(mask & 2 != 0, 1, jnp.where(mask & 4 != 0, 2, 3)))


def highest(mask):
    return jnp.where(mask & 8 != 0, 3, jnp.where(mask & 4 != 0, 2, jnp.where(mask & 2 != 0, 1, 0)))


def owner_mask(words, owner, row_blocks):
    first = owner * row_blocks
    word = words[0]
    for at in range(1, len(words)):
        word = jnp.where(first >> 5 == at, words[at], word)
    return (word >> (first & 31)) & ((1 << row_blocks) - 1)


def words_kernel(count_ref, cols_ref, words_ref):
    live = count_ref[0]
    word_total = words_ref.shape[1]

    def step(slot, found):
        column = cols_ref[slot]
        bit = jnp.where(slot < live, 1 << (column & 31), 0)
        word = column >> 5
        return tuple(one | jnp.where(word == at, bit, 0) for at, one in enumerate(found))

    start = tuple(jnp.int32(0) for _ in range(word_total))
    found = lax.fori_loop(0, cols_ref.shape[0], step, start, unroll=8)
    for member in range(GROUP):
        for at in range(word_total):
            words_ref[member, at] = found[at]


def group_limit(tile_total, row_blocks):
    return -(-(tile_total // DEPTH + row_blocks) // WIDTH) * WIDTH


def list_kernel(cubes, row_blocks, count_ref, rows_ref, cols_ref, words_ref, lists, filled):
    tile_total = cols_ref.shape[0]
    node = lax.axis_index("node")
    cube, member = node // GROUP, node % GROUP
    words = [words_ref[0, at] for at in range(words_ref.shape[1])]
    limit = group_limit(tile_total, row_blocks)

    @pl.loop(0, limit)
    def _(group):
        lists[1 + group] = row_blocks
        for at in range(DEPTH):
            entry = 1 + limit + 2 * (group * DEPTH + at)
            lists[entry] = 0
            lists[entry + 1] = cubes * GROUP * CAP

    for row in range(row_blocks):
        filled[row] = 0

    @pl.loop(0, count_ref[0])
    def _(slot):
        row = rows_ref[slot]
        filled[row] = filled[row] + 1

    start = 0
    for row in range(row_blocks):
        groups = (filled[row] + DEPTH - 1) // DEPTH
        filled[row] = start * DEPTH

        @pl.loop(start, start + groups)
        def _(group):
            lists[1 + group] = row

        start = start + groups
    lists[0] = start

    @pl.loop(0, count_ref[0])
    def _(slot):
        column = cols_ref[slot]
        owner = column // row_blocks
        home = owner // GROUP
        unit = jnp.where(home >= cube, home - cube, home - cube + cubes)
        second = column - owner * row_blocks != lowest(owner_mask(words, owner, row_blocks))
        row = rows_ref[slot]
        entry = 1 + limit + 2 * filled[row]
        filled[row] = filled[row] + 1
        step = (owner - home * GROUP) ^ member
        lists[entry] = slot
        lists[entry + 1] = (unit * GROUP + step) * CAP + jnp.where(second, 1, 0)


def make_plan(tile_rows, tile_cols, tile_counts, cubes, row_blocks):
    tile_total = tile_cols.shape[0]
    word_total = -(-cubes * GROUP * row_blocks // 32)
    list_length = 1 + group_limit(tile_total, row_blocks) * (1 + 2 * DEPTH)
    own = pl.pallas_call(
        words_kernel,
        out_shape=jax.ShapeDtypeStruct((GROUP, word_total), jnp.int32),
        in_specs=[SMEM] * 2,
        out_specs=SMEM,
    )(tile_counts, tile_cols)
    lists = pl.pallas_call(
        functools.partial(list_kernel, cubes, row_blocks),
        out_shape=jax.ShapeDtypeStruct((list_length,), jnp.int32),
        in_specs=[SMEM] * 4,
        out_specs=SMEM,
        scratch_shapes=[pltpu.SMEM((row_blocks,), jnp.int32)],
    )(tile_counts, tile_rows, tile_cols, own)
    groups = [[cube * GROUP + member for member in range(GROUP)] for cube in range(cubes)]
    words = exchange(own, groups)
    return words, lists


def exchange(array, groups):
    return lax.all_to_all(
        array, "node", split_axis=0, concat_axis=0, tiled=True, axis_index_groups=groups
    )


def named_blocks(words_ref, member, owner, row_blocks):
    words = [words_ref[member, at] for at in range(words_ref.shape[1])]
    mask = owner_mask(words, owner, row_blocks)
    return [pl.multiple_of(block * BLK, BLK) for block in (lowest(mask), highest(mask))]


def even_member(member):
    parity = (member ^ (member >> 1) ^ (member >> 2)) & 1
    return member ^ parity, parity


def pack_kernel(cubes, whole, messages, alike, fetched, words_ref, *refs):
    held, refs = dict(zip(whole, refs)), refs[len(whole) :]
    total = len(messages) + alike
    sent, packed, done = refs[:total], refs[total : 2 * total], refs[2 * total]
    row_blocks = held[whole[0]].shape[1] // BLK
    node = lax.axis_index("node")
    cube, member = node // GROUP, node % GROUP
    _, parity = even_member(member)

    def fill(target, other, unit, source):
        owner = (cube + unit) % cubes * GROUP + (member ^ source)
        for slot, lane in enumerate(named_blocks(words_ref, other, owner, row_blocks)):
            target[slot] = held[unit, source][:, pl.ds(lane, BLK)]

    if fetched:
        own, held[0, 0] = held[0, 0], refs[-1]
        fetch = pltpu.make_async_copy(own, held[0, 0], done.at[total])
        fetch.start()
    copies = []
    for at, (step, sources) in reversed(list(enumerate(messages))):
        for part, (unit, source) in reversed(list(enumerate(sources))):
            if fetched and (unit, source) == (0, 0):
                fetch.wait()
            fill(packed[at].at[part], member ^ step, unit, source)
        copies.append(pltpu.make_async_copy(packed[at], sent[at], done.at[at]))
        copies[-1].start()
    if alike:
        for at, even in enumerate(EVEN):
            for unit in range(1, cubes):
                fill(packed[-1].at[at, unit - 1], even ^ parity, unit, 0)
        copies.append(pltpu.make_async_copy(packed[-1], sent[-1], done.at[total - 1]))
        copies[-1].start()
    for copy in copies:
        copy.wait()


def pack(cubes, words, held, messages, alike, fetched, work):
    feat_local, nodes_local = next(iter(held.values())).shape
    shapes = [(len(sources), CAP, feat_local, BLK) for _, sources in messages]
    if alike:
        shapes += [(len(EVEN), cubes - 1, CAP, feat_local, BLK)]
    scratch = [pltpu.VMEM(shape, jnp.bfloat16) for shape in shapes]
    scratch += [pltpu.SemaphoreType.DMA((len(shapes) + 1,))]
    if fetched:
        scratch += [pltpu.VMEM((feat_local, nodes_local), jnp.bfloat16)]
        held = {**held, (0, 0): in_hbm(held[0, 0])}
    return pl.pallas_call(
        functools.partial(pack_kernel, cubes, tuple(held), messages, alike, fetched),
        out_shape=[pltpu.HBM(shape, jnp.bfloat16) for shape in shapes],
        in_specs=[SMEM] + [HBM if fetched and at == (0, 0) else VMEM for at in held],
        out_specs=[HBM] * len(shapes),
        scratch_shapes=scratch,
        compiler_params=PARAMS,
        cost_estimate=pl.CostEstimate(flops=work, bytes_accessed=0, transcendentals=0),
    )(words, *held.values())


def in_hbm(array):
    return pltpu.with_memory_space_constraint(array, pltpu.HBM)


def keep_kernel(cubes, whole, words_ref, *refs):
    held, kept = refs[:-1], refs[-1]
    row_blocks = held[0].shape[1] // BLK
    node = lax.axis_index("node")
    cube, member = node // GROUP, node % GROUP
    for at, (unit, source) in enumerate(whole):
        owner = (cube + unit) % cubes * GROUP + (member ^ source)
        for slot, lane in enumerate(named_blocks(words_ref, member, owner, row_blocks)):
            kept[at, slot] = held[at][:, pl.ds(lane, BLK)]


def keep(cubes, words, held):
    shape = (len(held), CAP, held[0, 0].shape[0], BLK)
    return pl.pallas_call(
        functools.partial(keep_kernel, cubes, tuple(held)),
        out_shape=jax.ShapeDtypeStruct(shape, jnp.bfloat16),
        in_specs=[SMEM] + [VMEM] * len(held),
        out_specs=VMEM,
        compiler_params=PARAMS,
    )(words, *held.values())


def aggregate_kernel(cubes, limit, whole, messages, alike, lists_hbm, tiles, kept, *refs):
    received, refs = refs[: len(messages)], refs[len(messages) :]
    if alike:
        alike_hbm, out_ref, lists, blocks, total, done, fetched = refs
    else:
        out_ref, lists, blocks, total, done = refs
    copies = [pltpu.make_async_copy(lists_hbm, lists, done.at[0])]
    if alike:
        copies.append(pltpu.make_async_copy(tiles, fetched, done.at[1]))
        tiles = fetched
        own, _ = even_member(lax.axis_index("node") % GROUP)
        for at, even in enumerate(EVEN):
            for unit in range(1, cubes):
                place = blocks.at[unit * GROUP + (even ^ own)]
                sem = done.at[2 + at * (cubes - 1) + unit - 1]
                copies.append(pltpu.make_async_copy(alike_hbm.at[at, unit - 1], place, sem))
    for copy in copies:
        copy.start()
    total[...] = jnp.zeros_like(total)
    blocks[cubes * GROUP, 0] = jnp.zeros_like(blocks[cubes * GROUP, 0])
    for (step, sources), array in zip(messages, received):
        for part, (unit, source) in enumerate(sources):
            blocks[unit * GROUP + (step ^ source)] = array[part]
    for at, (unit, source) in enumerate(whole):
        if not alike or unit == 0:
            blocks[unit * GROUP + source] = kept[at]
    for copy in copies:
        copy.wait()

    @pl.loop(0, (lists[0] + WIDTH - 1) // WIDTH)
    def _(loop_step):
        sums = []
        for wide in range(WIDTH):
            group = loop_step * WIDTH + wide
            left, right = [], []
            for at in range(DEPTH):
                entry = 1 + limit + 2 * (group * DEPTH + at)
                place = lists[entry + 1]
                left.append(blocks[place // CAP, place % CAP])
                right.append(tiles[lists[entry]])
            summed = lax.dot_general(
                jnp.concatenate(left, axis=1),
                jnp.concatenate(right, axis=1),
                (((1,), (1,)), ((), ())),
                preferred_element_type=jnp.float32,
            )
            sums.append((lists[1 + group], summed))
        for row, summed in sums:
            total[row] += summed

    for row in range(out_ref.shape[1] // BLK):
        out_ref[:, row * BLK : (row + 1) * BLK] = total[row].astype(out_ref.dtype)


def aggregate(cubes, whole, messages, alike, lists, adj_tiles, kept, received, nodes_local):
    feat_local = kept.shape[2]
    row_blocks = nodes_local // BLK
    limit = group_limit(adj_tiles.shape[0], row_blocks)
    operands = [in_hbm(adj_tiles) if alike else adj_tiles, kept, *received]
    spaces = [HBM if alike else VMEM] + [VMEM] * (1 + len(messages))
    scratch = [
        pltpu.SMEM(lists.shape, jnp.int32),
        pltpu.VMEM((cubes * GROUP + 1, CAP, feat_local, BLK), jnp.bfloat16),
        pltpu.VMEM((row_blocks + 1, feat_local, BLK), jnp.float32),
        pltpu.SemaphoreType.DMA((2 + len(EVEN) * (cubes - 1),)),
    ]
    if alike:
        operands[-1] = in_hbm(operands[-1])
        spaces.append(HBM)
        scratch.append(pltpu.VMEM(adj_tiles.shape, jnp.bfloat16))
    return pl.pallas_call(
        functools.partial(aggregate_kernel, cubes, limit, whole, messages, alike),
        out_shape=jax.ShapeDtypeStruct((feat_local, nodes_local), jnp.bfloat16),
        in_specs=[HBM] + spaces,
        out_specs=VMEM,
        scratch_shapes=scratch,
        compiler_params=PARAMS,
        cost_estimate=pl.CostEstimate(
            flops=2 * adj_tiles.shape[0] * feat_local * BLK * BLK,
            bytes_accessed=2 * sum(one.size for one in operands),
            transcendentals=0,
        ),
    )(in_hbm(lists), *operands)


def gather_sums(feat_t, adj_tiles, plan, cubes, by_planes):
    words, lists = plan
    nodes = cubes * GROUP

    def to_member(array, step):
        return lax.ppermute(array, "node", [(n, n ^ step) for n in range(nodes)])

    relayed = {
        (unit, 0): lax.ppermute(
            feat_t, "node", [(n, (n - unit * GROUP) % nodes) for n in range(nodes)]
        )
        for unit in range(1, cubes)
    }
    if by_planes:
        held = {(0, 0): feat_t, **relayed}
        held.update({(unit, 4): to_member(array, 4) for (unit, _), array in held.items()})
        batches = [
            ([(0, 0)], 0),
            ([(0, 4)] + list(relayed), RELAY_WORK),
            ([(unit, 4) for unit, _ in relayed], RELAY_WORK),
        ]
        messages, received = [], []
        for sources, work in batches:
            batch = [(step, sources) for step in (3, 1, 2)]
            array = {at: held[at] for at in sources}
            sent = pack(cubes, words, array, batch, False, False, work)
            messages += batch
            received += [to_member(array, step) for array, (step, _) in zip(sent, batch)]
    else:
        near = {(0, step): to_member(feat_t, step) if step else feat_t for step in NEAR}
        messages = [(step, [(0, source)] + list(relayed)) for step, source in PASSED.items()]
        held = {**relayed, **near}
        sent = pack(cubes, words, {**near, **relayed}, messages, True, True, 0)
        received = [to_member(array, step) for array, (step, _) in zip(sent, messages)]
        groups = [
            [cube * GROUP + (even ^ parity) for even in EVEN]
            for cube in range(cubes)
            for parity in range(2)
        ]
        received.append(exchange(sent[-1], groups))
    kept = keep(cubes, words, held)
    local = aggregate(
        cubes,
        tuple(held),
        messages,
        not by_planes,
        lists,
        adj_tiles,
        kept,
        received,
        feat_t.shape[1],
    )
    return lax.all_gather(local, "col", axis=0, tiled=True)


def dense_kernel(weight, aggregated, bias, out_ref):
    out_ref[...] = (
        jnp.dot(weight[...], aggregated[...], preferred_element_type=jnp.float32) + bias[...]
    )


def dense(weight, aggregated, bias):
    return pl.pallas_call(
        dense_kernel,
        out_shape=jax.ShapeDtypeStruct((weight.shape[0], aggregated.shape[1]), jnp.float32),
        in_specs=[VMEM] * 3,
        out_specs=VMEM,
        compiler_params=PARAMS,
        cost_estimate=pl.CostEstimate(
            flops=2 * weight.size * aggregated.shape[1],
            bytes_accessed=2 * (weight.size + 3 * aggregated.size),
            transcendentals=0,
        ),
    )(weight, aggregated, bias[:, None])


def body(x_t, adj_tiles, tile_rows, tile_cols, tile_counts, w_first, b_first, w_second, b_second):
    cubes = lax.axis_size("node") // GROUP
    plan = make_plan(tile_rows, tile_cols, tile_counts, cubes, x_t.shape[1] // BLK)
    y_first = gather_sums(x_t, adj_tiles, plan, cubes, False)
    z_first = jnp.dot(w_first, y_first, preferred_element_type=jnp.float32) + b_first[:, None]
    h_first = jnp.maximum(z_first, 0.0).astype(jnp.bfloat16)
    y_second = gather_sums(h_first, adj_tiles, plan, cubes, True)
    return dense(w_second, y_second, b_second)


def solution(mesh):
    return jax.shard_map(
        body,
        mesh=mesh,
        in_specs=(
            P("col", "node"),
            P("node", None, None),
            P("node"),
            P("node"),
            P("node"),
            P("col", None),
            P("col"),
            P("col", None),
            P("col"),
        ),
        out_specs=P("col", "node"),
        check_vma=False,
    )
```

```python
import functools

import jax
import jax.numpy as jnp
from jax import lax
from jax.experimental import pallas as pl
from jax.experimental.pallas import tpu as pltpu
from jax.sharding import PartitionSpec as P

BLK = 128
CAP = 2
GROUP = 8
NEAR = (0, 1, 2, 4)
PASSED = {7: 0, 4: 1, 1: 2, 2: 4}
EVEN = (0, 3, 5, 6)
DEPTH = 4
RELAY_WORK = 50_000_000_000
WIDTH = 4
SMEM = pl.BlockSpec(memory_space=pltpu.SMEM)
VMEM = pl.BlockSpec(memory_space=pltpu.VMEM)
HBM = pl.BlockSpec(memory_space=pltpu.HBM)
PARAMS = pltpu.CompilerParams(vmem_limit_bytes=24 * 1024 * 1024)


def lowest(mask):
    return jnp.where(mask & 1 != 0, 0, jnp.where(mask & 2 != 0, 1, jnp.where(mask & 4 != 0, 2, 3)))


def highest(mask):
    return jnp.where(mask & 8 != 0, 3, jnp.where(mask & 4 != 0, 2, jnp.where(mask & 2 != 0, 1, 0)))


def owner_mask(words, owner, row_blocks):
    first = owner * row_blocks
    word = words[0]
    for at in range(1, len(words)):
        word = jnp.where(first >> 5 == at, words[at], word)
    return (word >> (first & 31)) & ((1 << row_blocks) - 1)


def words_kernel(count_ref, cols_ref, words_ref):
    live = count_ref[0]
    word_total = words_ref.shape[1]

    def step(slot, found):
        column = cols_ref[slot]
        bit = jnp.where(slot < live, 1 << (column & 31), 0)
        word = column >> 5
        return tuple(one | jnp.where(word == at, bit, 0) for at, one in enumerate(found))

    start = tuple(jnp.int32(0) for _ in range(word_total))
    found = lax.fori_loop(0, cols_ref.shape[0], step, start, unroll=8)
    for member in range(GROUP):
        for at in range(word_total):
            words_ref[member, at] = found[at]


def group_limit(tile_total, row_blocks):
    return -(-(tile_total // DEPTH + row_blocks) // WIDTH) * WIDTH


def list_kernel(cubes, row_blocks, count_ref, rows_ref, cols_ref, words_ref, lists, filled):
    tile_total = cols_ref.shape[0]
    node = lax.axis_index("node")
    cube, member = node // GROUP, node % GROUP
    words = [words_ref[0, at] for at in range(words_ref.shape[1])]
    limit = group_limit(tile_total, row_blocks)

    @pl.loop(0, limit)
    def _(group):
        lists[1 + group] = row_blocks
        for at in range(DEPTH):
            entry = 1 + limit + 2 * (group * DEPTH + at)
            lists[entry] = 0
            lists[entry + 1] = cubes * GROUP * CAP

    for row in range(row_blocks):
        filled[row] = 0

    @pl.loop(0, count_ref[0])
    def _(slot):
        row = rows_ref[slot]
        filled[row] = filled[row] + 1

    start = 0
    for row in range(row_blocks):
        groups = (filled[row] + DEPTH - 1) // DEPTH
        filled[row] = start * DEPTH

        @pl.loop(start, start + groups)
        def _(group):
            lists[1 + group] = row

        start = start + groups
    lists[0] = start

    @pl.loop(0, count_ref[0])
    def _(slot):
        column = cols_ref[slot]
        owner = column // row_blocks
        home = owner // GROUP
        unit = jnp.where(home >= cube, home - cube, home - cube + cubes)
        second = column - owner * row_blocks != lowest(owner_mask(words, owner, row_blocks))
        row = rows_ref[slot]
        entry = 1 + limit + 2 * filled[row]
        filled[row] = filled[row] + 1
        step = (owner - home * GROUP) ^ member
        lists[entry] = slot
        lists[entry + 1] = (unit * GROUP + step) * CAP + jnp.where(second, 1, 0)


def make_plan(tile_rows, tile_cols, tile_counts, cubes, row_blocks):
    tile_total = tile_cols.shape[0]
    word_total = -(-cubes * GROUP * row_blocks // 32)
    list_length = 1 + group_limit(tile_total, row_blocks) * (1 + 2 * DEPTH)
    own = pl.pallas_call(
        words_kernel,
        out_shape=jax.ShapeDtypeStruct((GROUP, word_total), jnp.int32),
        in_specs=[SMEM] * 2,
        out_specs=SMEM,
    )(tile_counts, tile_cols)
    lists = pl.pallas_call(
        functools.partial(list_kernel, cubes, row_blocks),
        out_shape=jax.ShapeDtypeStruct((list_length,), jnp.int32),
        in_specs=[SMEM] * 4,
        out_specs=SMEM,
        scratch_shapes=[pltpu.SMEM((row_blocks,), jnp.int32)],
    )(tile_counts, tile_rows, tile_cols, own)
    groups = [[cube * GROUP + member for member in range(GROUP)] for cube in range(cubes)]
    words = exchange(own, groups)
    return words, lists


def exchange(array, groups):
    return lax.all_to_all(
        array, "node", split_axis=0, concat_axis=0, tiled=True, axis_index_groups=groups
    )


def named_blocks(words_ref, member, owner, row_blocks):
    words = [words_ref[member, at] for at in range(words_ref.shape[1])]
    mask = owner_mask(words, owner, row_blocks)
    return [pl.multiple_of(block * BLK, BLK) for block in (lowest(mask), highest(mask))]


def even_member(member):
    parity = (member ^ (member >> 1) ^ (member >> 2)) & 1
    return member ^ parity, parity


def pack_kernel(cubes, whole, messages, alike, fetched, words_ref, *refs):
    held, refs = dict(zip(whole, refs)), refs[len(whole) :]
    total = len(messages) + alike
    sent, packed, done = refs[:total], refs[total : 2 * total], refs[2 * total]
    row_blocks = held[whole[0]].shape[1] // BLK
    node = lax.axis_index("node")
    cube, member = node // GROUP, node % GROUP
    _, parity = even_member(member)

    def fill(target, other, unit, source):
        owner = (cube + unit) % cubes * GROUP + (member ^ source)
        for slot, lane in enumerate(named_blocks(words_ref, other, owner, row_blocks)):
            target[slot] = held[unit, source][:, pl.ds(lane, BLK)]

    if fetched:
        own, held[0, 0] = held[0, 0], refs[-1]
        fetch = pltpu.make_async_copy(own, held[0, 0], done.at[total])
        fetch.start()
    copies = []
    for at, (step, sources) in reversed(list(enumerate(messages))):
        target = packed[at] if step else sent[at]
        for part, (unit, source) in reversed(list(enumerate(sources))):
            if fetched and (unit, source) == (0, 0):
                fetch.wait()
            fill(target.at[part], member ^ step, unit, source)
        if not step:
            continue
        copies.append(pltpu.make_async_copy(packed[at], sent[at], done.at[at]))
        copies[-1].start()
    if alike:
        for at, even in enumerate(EVEN):
            for unit in range(1, cubes):
                fill(packed[-1].at[at, unit - 1], even ^ parity, unit, 0)
        copies.append(pltpu.make_async_copy(packed[-1], sent[-1], done.at[total - 1]))
        copies[-1].start()
    for copy in copies:
        copy.wait()


def pack(cubes, words, held, messages, alike, fetched, work):
    feat_local, nodes_local = next(iter(held.values())).shape
    shapes = [(len(sources), CAP, feat_local, BLK) for _, sources in messages]
    away = [step != 0 for step, _ in messages]
    if alike:
        shapes += [(len(EVEN), cubes - 1, CAP, feat_local, BLK)]
        away += [True]
    scratch = [pltpu.VMEM(shape, jnp.bfloat16) for shape in shapes]
    scratch += [pltpu.SemaphoreType.DMA((len(shapes) + 1,))]
    if fetched:
        scratch += [pltpu.VMEM((feat_local, nodes_local), jnp.bfloat16)]
        held = {**held, (0, 0): in_hbm(held[0, 0])}
    return pl.pallas_call(
        functools.partial(pack_kernel, cubes, tuple(held), messages, alike, fetched),
        out_shape=[
            (pltpu.HBM if far else pltpu.VMEM)(shape, jnp.bfloat16)
            for shape, far in zip(shapes, away)
        ],
        in_specs=[SMEM] + [HBM if fetched and at == (0, 0) else VMEM for at in held],
        out_specs=[HBM if far else VMEM for far in away],
        scratch_shapes=scratch,
        compiler_params=PARAMS,
        cost_estimate=pl.CostEstimate(flops=work, bytes_accessed=0, transcendentals=0),
    )(words, *held.values())


def in_hbm(array):
    return pltpu.with_memory_space_constraint(array, pltpu.HBM)


def keep_kernel(cubes, whole, words_ref, *refs):
    held, kept = refs[:-1], refs[-1]
    row_blocks = held[0].shape[1] // BLK
    node = lax.axis_index("node")
    cube, member = node // GROUP, node % GROUP
    for at, (unit, source) in enumerate(whole):
        owner = (cube + unit) % cubes * GROUP + (member ^ source)
        for slot, lane in enumerate(named_blocks(words_ref, member, owner, row_blocks)):
            kept[at, slot] = held[at][:, pl.ds(lane, BLK)]


def keep(cubes, words, held):
    shape = (len(held), CAP, held[0, 0].shape[0], BLK)
    return pl.pallas_call(
        functools.partial(keep_kernel, cubes, tuple(held)),
        out_shape=jax.ShapeDtypeStruct(shape, jnp.bfloat16),
        in_specs=[SMEM] + [VMEM] * len(held),
        out_specs=VMEM,
        compiler_params=PARAMS,
    )(words, *held.values())


def aggregate_kernel(cubes, limit, whole, messages, alike, lists_hbm, tiles, *refs):
    received, refs = refs[: len(messages)], refs[len(messages) :]
    if alike:
        kept, alike_hbm, out_ref, lists, blocks, total, done, fetched = refs
    else:
        out_ref, lists, blocks, total, done = refs
    pairs = [(lists_hbm, lists)]
    if alike:
        pairs.append((tiles, fetched))
        tiles = fetched
        own, _ = even_member(lax.axis_index("node") % GROUP)
        for at, even in enumerate(EVEN):
            for unit in range(1, cubes):
                place = unit * GROUP + (even ^ own)
                pairs.append((alike_hbm.at[at, unit - 1], blocks.at[place]))
    copies = [pltpu.make_async_copy(*pair, done.at[at]) for at, pair in enumerate(pairs)]
    for copy in copies:
        copy.start()
    total[...] = jnp.zeros_like(total)
    blocks[cubes * GROUP, 0] = jnp.zeros_like(blocks[cubes * GROUP, 0])
    for (step, sources), array in zip(messages, received):
        for part, (unit, source) in enumerate(sources):
            blocks[unit * GROUP + (step ^ source)] = array[part]
    if alike:
        for at, (unit, source) in enumerate(whole):
            if unit == 0:
                blocks[source] = kept[at]
    for copy in copies:
        copy.wait()

    @pl.loop(0, (lists[0] + WIDTH - 1) // WIDTH)
    def _(loop_step):
        sums = []
        for wide in range(WIDTH):
            group = loop_step * WIDTH + wide
            left, right = [], []
            for at in range(DEPTH):
                entry = 1 + limit + 2 * (group * DEPTH + at)
                place = lists[entry + 1]
                left.append(blocks[place // CAP, place % CAP])
                right.append(tiles[lists[entry]])
            summed = lax.dot_general(
                jnp.concatenate(left, axis=1),
                jnp.concatenate(right, axis=1),
                (((1,), (1,)), ((), ())),
                preferred_element_type=jnp.float32,
            )
            sums.append((lists[1 + group], summed))
        for row, summed in sums:
            total[row] += summed

    for row in range(out_ref.shape[1] // BLK):
        out_ref[:, row * BLK : (row + 1) * BLK] = total[row].astype(out_ref.dtype)


def aggregate(cubes, whole, messages, alike, lists, adj_tiles, received, nodes_local):
    feat_local = received[0].shape[2]
    row_blocks = nodes_local // BLK
    limit = group_limit(adj_tiles.shape[0], row_blocks)
    scratch = [
        pltpu.SMEM(lists.shape, jnp.int32),
        pltpu.VMEM((cubes * GROUP + 1, CAP, feat_local, BLK), jnp.bfloat16),
        pltpu.VMEM((row_blocks + 1, feat_local, BLK), jnp.float32),
        pltpu.SemaphoreType.DMA((1 + cubes * GROUP,)),
    ]
    if alike:
        operands = [in_hbm(adj_tiles), *received[:-1], in_hbm(received[-1])]
        spaces = [HBM] + [VMEM] * (len(received) - 1) + [HBM]
        scratch.append(pltpu.VMEM(adj_tiles.shape, jnp.bfloat16))
    else:
        operands = [adj_tiles]
        operands += [pltpu.with_memory_space_constraint(one, pltpu.VMEM) for one in received]
        spaces = [VMEM] * len(operands)
    return pl.pallas_call(
        functools.partial(aggregate_kernel, cubes, limit, whole, messages, alike),
        out_shape=jax.ShapeDtypeStruct((feat_local, nodes_local), jnp.bfloat16),
        in_specs=[HBM] + spaces,
        out_specs=VMEM,
        scratch_shapes=scratch,
        compiler_params=PARAMS,
        cost_estimate=pl.CostEstimate(
            flops=2 * adj_tiles.shape[0] * feat_local * BLK * BLK,
            bytes_accessed=2 * sum(one.size for one in operands),
            transcendentals=0,
        ),
    )(in_hbm(lists), *operands)


def gather_sums(feat_t, adj_tiles, plan, cubes, by_planes):
    words, lists = plan
    nodes = cubes * GROUP

    def to_member(array, step):
        return lax.ppermute(array, "node", [(n, n ^ step) for n in range(nodes)])

    relayed = {
        (unit, 0): lax.ppermute(
            feat_t, "node", [(n, (n - unit * GROUP) % nodes) for n in range(nodes)]
        )
        for unit in range(1, cubes)
    }
    if by_planes:
        held = {(0, 0): feat_t, **relayed}
        held.update({(unit, 4): to_member(array, 4) for (unit, _), array in held.items()})
        batches = [
            ([(0, 0)], 0),
            ([(0, 4)] + list(relayed), RELAY_WORK),
            ([(unit, 4) for unit, _ in relayed], RELAY_WORK),
        ]
        messages, received = [], []
        for sources, work in batches:
            batch = [(step, sources) for step in (3, 1, 2, 0)]
            array = {at: held[at] for at in sources}
            sent = pack(cubes, words, array, batch, False, False, work)
            messages += batch
            received += [
                to_member(array, step) if step else array
                for array, (step, _) in zip(sent, batch)
            ]
    else:
        near = {(0, step): to_member(feat_t, step) if step else feat_t for step in NEAR}
        messages = [(step, [(0, source)] + list(relayed)) for step, source in PASSED.items()]
        held = {**relayed, **near}
        sent = pack(cubes, words, held, messages, True, True, 0)
        received = [to_member(array, step) for array, (step, _) in zip(sent, messages)]
        groups = [
            [cube * GROUP + (even ^ parity) for even in EVEN]
            for cube in range(cubes)
            for parity in range(2)
        ]
        received += [keep(cubes, words, held), exchange(sent[-1], groups)]
    local = aggregate(
        cubes, tuple(held), messages, not by_planes, lists, adj_tiles, received, feat_t.shape[1]
    )
    return lax.all_gather(local, "col", axis=0, tiled=True)


def dense_kernel(weight, aggregated, bias, out_ref):
    out_ref[...] = (
        jnp.dot(weight[...], aggregated[...], preferred_element_type=jnp.float32) + bias[...]
    )


def dense(weight, aggregated, bias):
    return pl.pallas_call(
        dense_kernel,
        out_shape=jax.ShapeDtypeStruct((weight.shape[0], aggregated.shape[1]), jnp.float32),
        in_specs=[VMEM] * 3,
        out_specs=VMEM,
        compiler_params=PARAMS,
        cost_estimate=pl.CostEstimate(
            flops=2 * weight.size * aggregated.shape[1],
            bytes_accessed=2 * (weight.size + 3 * aggregated.size),
            transcendentals=0,
        ),
    )(weight, aggregated, bias[:, None])


def body(x_t, adj_tiles, tile_rows, tile_cols, tile_counts, w_first, b_first, w_second, b_second):
    cubes = lax.axis_size("node") // GROUP
    plan = make_plan(tile_rows, tile_cols, tile_counts, cubes, x_t.shape[1] // BLK)
    y_first = gather_sums(x_t, adj_tiles, plan, cubes, False)
    z_first = jnp.dot(w_first, y_first, preferred_element_type=jnp.float32) + b_first[:, None]
    h_first = jnp.maximum(z_first, 0.0).astype(jnp.bfloat16)
    y_second = gather_sums(h_first, adj_tiles, plan, cubes, True)
    return dense(w_second, y_second, b_second)


def solution(mesh):
    return jax.shard_map(
        body,
        mesh=mesh,
        in_specs=(
            P("col", "node"),
            P("node", None, None),
            P("node"),
            P("node"),
            P("node"),
            P("col", None),
            P("col"),
            P("col", None),
            P("col"),
        ),
        out_specs=P("col", "node"),
        check_vma=False,
    )
```

```python
import functools

import jax
import jax.numpy as jnp
from jax import lax
from jax.experimental import pallas as pl
from jax.experimental.pallas import tpu as pltpu
from jax.sharding import PartitionSpec as P

BLK = 128
CAP = 2
GROUP = 8
NEAR = (0, 1, 2, 4)
PASSED = {7: 0, 4: 1, 1: 2, 2: 4}
STEPS = (7, 6, 5, 4, 3, 1, 2)
DEPTH = 4
RELAY_WORK = 50_000_000_000
WIDTH = 4
SMEM = pl.BlockSpec(memory_space=pltpu.SMEM)
VMEM = pl.BlockSpec(memory_space=pltpu.VMEM)
HBM = pl.BlockSpec(memory_space=pltpu.HBM)
PARAMS = pltpu.CompilerParams(vmem_limit_bytes=24 * 1024 * 1024)


def lowest(mask):
    return jnp.where(mask & 1 != 0, 0, jnp.where(mask & 2 != 0, 1, jnp.where(mask & 4 != 0, 2, 3)))


def highest(mask):
    return jnp.where(mask & 8 != 0, 3, jnp.where(mask & 4 != 0, 2, jnp.where(mask & 2 != 0, 1, 0)))


def owner_mask(words, owner, row_blocks):
    first = owner * row_blocks
    word = words[0]
    for at in range(1, len(words)):
        word = jnp.where(first >> 5 == at, words[at], word)
    return (word >> (first & 31)) & ((1 << row_blocks) - 1)


def words_kernel(count_ref, cols_ref, words_ref):
    live = count_ref[0]
    word_total = words_ref.shape[1]

    def step(slot, found):
        column = cols_ref[slot]
        bit = jnp.where(slot < live, 1 << (column & 31), 0)
        word = column >> 5
        return tuple(one | jnp.where(word == at, bit, 0) for at, one in enumerate(found))

    start = tuple(jnp.int32(0) for _ in range(word_total))
    found = lax.fori_loop(0, cols_ref.shape[0], step, start, unroll=8)
    for member in range(GROUP):
        for at in range(word_total):
            words_ref[member, at] = found[at]


def group_limit(tile_total, row_blocks):
    return -(-(tile_total // DEPTH + row_blocks) // WIDTH) * WIDTH


def list_kernel(cubes, row_blocks, count_ref, rows_ref, cols_ref, words_ref, lists, filled):
    tile_total = cols_ref.shape[0]
    node = lax.axis_index("node")
    cube, member = node // GROUP, node % GROUP
    words = [words_ref[0, at] for at in range(words_ref.shape[1])]
    limit = group_limit(tile_total, row_blocks)

    @pl.loop(0, limit)
    def _(group):
        lists[1 + group] = row_blocks
        for at in range(DEPTH):
            entry = 1 + limit + 2 * (group * DEPTH + at)
            lists[entry] = 0
            lists[entry + 1] = cubes * GROUP * CAP

    for row in range(row_blocks):
        filled[row] = 0

    @pl.loop(0, count_ref[0])
    def _(slot):
        row = rows_ref[slot]
        filled[row] = filled[row] + 1

    start = 0
    for row in range(row_blocks):
        groups = (filled[row] + DEPTH - 1) // DEPTH
        filled[row] = start * DEPTH

        @pl.loop(start, start + groups)
        def _(group):
            lists[1 + group] = row

        start = start + groups
    lists[0] = start

    @pl.loop(0, count_ref[0])
    def _(slot):
        column = cols_ref[slot]
        owner = column // row_blocks
        home = owner // GROUP
        unit = jnp.where(home >= cube, home - cube, home - cube + cubes)
        second = column - owner * row_blocks != lowest(owner_mask(words, owner, row_blocks))
        row = rows_ref[slot]
        entry = 1 + limit + 2 * filled[row]
        filled[row] = filled[row] + 1
        step = (owner - home * GROUP) ^ member
        lists[entry] = slot
        lists[entry + 1] = (unit * GROUP + step) * CAP + jnp.where(second, 1, 0)


def make_plan(tile_rows, tile_cols, tile_counts, cubes, row_blocks):
    tile_total = tile_cols.shape[0]
    word_total = -(-cubes * GROUP * row_blocks // 32)
    list_length = 1 + group_limit(tile_total, row_blocks) * (1 + 2 * DEPTH)
    own = pl.pallas_call(
        words_kernel,
        out_shape=jax.ShapeDtypeStruct((GROUP, word_total), jnp.int32),
        in_specs=[SMEM] * 2,
        out_specs=SMEM,
    )(tile_counts, tile_cols)
    lists = pl.pallas_call(
        functools.partial(list_kernel, cubes, row_blocks),
        out_shape=jax.ShapeDtypeStruct((list_length,), jnp.int32),
        in_specs=[SMEM] * 4,
        out_specs=SMEM,
        scratch_shapes=[pltpu.SMEM((row_blocks,), jnp.int32)],
    )(tile_counts, tile_rows, tile_cols, own)
    groups = [[cube * GROUP + member for member in range(GROUP)] for cube in range(cubes)]
    words = exchange(own, groups)
    return words, lists


def exchange(array, groups):
    return lax.all_to_all(
        array, "node", split_axis=0, concat_axis=0, tiled=True, axis_index_groups=groups
    )


def named_blocks(words_ref, member, owner, row_blocks):
    words = [words_ref[member, at] for at in range(words_ref.shape[1])]
    mask = owner_mask(words, owner, row_blocks)
    return [pl.multiple_of(block * BLK, BLK) for block in (lowest(mask), highest(mask))]


def pack_kernel(cubes, whole, messages, fetched, words_ref, *refs):
    held, refs = dict(zip(whole, refs)), refs[len(whole) :]
    total = len(messages)
    sent, packed, done = refs[:total], refs[total : 2 * total], refs[2 * total]
    row_blocks = held[whole[0]].shape[1] // BLK
    node = lax.axis_index("node")
    cube, member = node // GROUP, node % GROUP

    def fill(target, other, unit, source):
        owner = (cube + unit) % cubes * GROUP + (member ^ source)
        for slot, lane in enumerate(named_blocks(words_ref, other, owner, row_blocks)):
            target[slot] = held[unit, source][:, pl.ds(lane, BLK)]

    if fetched:
        own, held[0, 0] = held[0, 0], refs[-1]
        fetch = pltpu.make_async_copy(own, held[0, 0], done.at[total])
        fetch.start()
    copies = []
    for at, (step, sources) in reversed(list(enumerate(messages))):
        for part, (unit, source) in reversed(list(enumerate(sources))):
            if fetched and (unit, source) == (0, 0):
                fetch.wait()
            fill(packed[at].at[part], member ^ step, unit, source)
        copies.append(pltpu.make_async_copy(packed[at], sent[at], done.at[at]))
        copies[-1].start()
    for copy in copies:
        copy.wait()


def pack(cubes, words, held, messages, fetched, work):
    feat_local, nodes_local = next(iter(held.values())).shape
    shapes = [(len(sources), CAP, feat_local, BLK) for _, sources in messages]
    scratch = [pltpu.VMEM(shape, jnp.bfloat16) for shape in shapes]
    scratch += [pltpu.SemaphoreType.DMA((len(shapes) + 1,))]
    if fetched:
        scratch += [pltpu.VMEM((feat_local, nodes_local), jnp.bfloat16)]
        held = {**held, (0, 0): in_hbm(held[0, 0])}
    return pl.pallas_call(
        functools.partial(pack_kernel, cubes, tuple(held), messages, fetched),
        out_shape=[pltpu.HBM(shape, jnp.bfloat16) for shape in shapes],
        in_specs=[SMEM] + [HBM if fetched and at == (0, 0) else VMEM for at in held],
        out_specs=[HBM] * len(shapes),
        scratch_shapes=scratch,
        compiler_params=PARAMS,
        cost_estimate=pl.CostEstimate(flops=work, bytes_accessed=0, transcendentals=0),
    )(words, *held.values())


def in_hbm(array):
    return pltpu.with_memory_space_constraint(array, pltpu.HBM)


def keep_kernel(cubes, whole, words_ref, *refs):
    held, kept = refs[:-1], refs[-1]
    row_blocks = held[0].shape[1] // BLK
    node = lax.axis_index("node")
    cube, member = node // GROUP, node % GROUP
    for at, (unit, source) in enumerate(whole):
        owner = (cube + unit) % cubes * GROUP + (member ^ source)
        for slot, lane in enumerate(named_blocks(words_ref, member, owner, row_blocks)):
            kept[at, slot] = held[at][:, pl.ds(lane, BLK)]


def keep(cubes, words, held):
    shape = (len(held), CAP, held[0, 0].shape[0], BLK)
    return pl.pallas_call(
        functools.partial(keep_kernel, cubes, tuple(held)),
        out_shape=jax.ShapeDtypeStruct(shape, jnp.bfloat16),
        in_specs=[SMEM] + [VMEM] * len(held),
        out_specs=VMEM,
        compiler_params=PARAMS,
    )(words, *held.values())


def aggregate_kernel(cubes, limit, messages, fetched, lists_hbm, tiles, *refs):
    received, refs = refs[: len(messages)], refs[len(messages) :]
    out_ref, lists, blocks, total, done = refs[:5]
    pairs = [(lists_hbm, lists)]
    if fetched:
        pairs.append((tiles, refs[5]))
        tiles = refs[5]
    for (step, sources, far), array in zip(messages, received):
        for part, (unit, source) in enumerate(sources if far else ()):
            pairs.append((array.at[part], blocks.at[unit * GROUP + (step ^ source)]))
    copies = [pltpu.make_async_copy(*pair, done.at[at]) for at, pair in enumerate(pairs)]
    for copy in copies:
        copy.start()
    total[...] = jnp.zeros_like(total)
    blocks[cubes * GROUP, 0] = jnp.zeros_like(blocks[cubes * GROUP, 0])
    for (step, sources, far), array in zip(messages, received):
        for part, (unit, source) in enumerate(() if far else sources):
            blocks[unit * GROUP + (step ^ source)] = array[part]
    for copy in copies:
        copy.wait()

    @pl.loop(0, (lists[0] + WIDTH - 1) // WIDTH)
    def _(loop_step):
        sums = []
        for wide in range(WIDTH):
            group = loop_step * WIDTH + wide
            left, right = [], []
            for at in range(DEPTH):
                entry = 1 + limit + 2 * (group * DEPTH + at)
                place = lists[entry + 1]
                left.append(blocks[place // CAP, place % CAP])
                right.append(tiles[lists[entry]])
            summed = lax.dot_general(
                jnp.concatenate(left, axis=1),
                jnp.concatenate(right, axis=1),
                (((1,), (1,)), ((), ())),
                preferred_element_type=jnp.float32,
            )
            sums.append((lists[1 + group], summed))
        for row, summed in sums:
            total[row] += summed

    for row in range(out_ref.shape[1] // BLK):
        out_ref[:, row * BLK : (row + 1) * BLK] = total[row].astype(out_ref.dtype)


def aggregate(cubes, messages, fetched, lists, adj_tiles, received, nodes_local):
    feat_local = received[0].shape[2]
    row_blocks = nodes_local // BLK
    limit = group_limit(adj_tiles.shape[0], row_blocks)
    operands = [in_hbm(adj_tiles) if fetched else adj_tiles]
    operands += [in_hbm(one) if far else one for one, (_, _, far) in zip(received, messages)]
    spaces = [HBM if fetched else VMEM] + [HBM if far else VMEM for _, _, far in messages]
    scratch = [
        pltpu.SMEM(lists.shape, jnp.int32),
        pltpu.VMEM((cubes * GROUP + 1, CAP, feat_local, BLK), jnp.bfloat16),
        pltpu.VMEM((row_blocks + 1, feat_local, BLK), jnp.float32),
        pltpu.SemaphoreType.DMA((2 + cubes * GROUP,)),
    ]
    if fetched:
        scratch.append(pltpu.VMEM(adj_tiles.shape, jnp.bfloat16))
    return pl.pallas_call(
        functools.partial(aggregate_kernel, cubes, limit, messages, fetched),
        out_shape=jax.ShapeDtypeStruct((feat_local, nodes_local), jnp.bfloat16),
        in_specs=[HBM] + spaces,
        out_specs=VMEM,
        scratch_shapes=scratch,
        compiler_params=PARAMS,
        cost_estimate=pl.CostEstimate(
            flops=2 * adj_tiles.shape[0] * feat_local * BLK * BLK,
            bytes_accessed=2 * sum(one.size for one in operands),
            transcendentals=0,
        ),
    )(in_hbm(lists), *operands)


def gather_sums(feat_t, adj_tiles, plan, cubes, by_planes):
    words, lists = plan
    nodes = cubes * GROUP

    def to_member(array, step):
        return lax.ppermute(array, "node", [(n, n ^ step) for n in range(nodes)])

    relayed = {
        (unit, 0): lax.ppermute(
            feat_t, "node", [(n, (n - unit * GROUP) % nodes) for n in range(nodes)]
        )
        for unit in range(1, cubes)
    }
    if by_planes:
        held = {(0, 0): feat_t, **relayed}
        held.update({(unit, 4): to_member(array, 4) for (unit, _), array in held.items()})
        batches = [
            ([(0, 0)], 0),
            ([(0, 4)] + list(relayed), RELAY_WORK),
            ([(unit, 4) for unit, _ in relayed], RELAY_WORK),
        ]
        messages, received = [], []
        for number, (sources, work) in enumerate(batches):
            batch = [(step, sources) for step in (3, 1, 2, 0)]
            array = {at: held[at] for at in sources}
            sent = pack(cubes, words, array, batch, False, work)
            for one, (step, _) in zip(sent, batch):
                messages.append((step, sources, number == 0 or step == 0))
                received.append(to_member(one, step) if step else one)
    else:
        near = {(0, step): to_member(feat_t, step) if step else feat_t for step in NEAR}
        held = {**relayed, **near}
        batch = [
            (step, ([(0, PASSED[step])] if step in PASSED else []) + list(relayed))
            for step in STEPS
        ]
        sent = pack(cubes, words, held, batch, True, 0)
        received = [to_member(one, step) for one, (step, _) in zip(sent, batch)]
        received.append(keep(cubes, words, held))
        messages = [(*one, False) for one in batch] + [(0, list(held), False)]
    local = aggregate(
        cubes, messages, not by_planes, lists, adj_tiles, received, feat_t.shape[1]
    )
    return lax.all_gather(local, "col", axis=0, tiled=True)


def dense_kernel(weight, aggregated, bias, out_ref):
    out_ref[...] = (
        jnp.dot(weight[...], aggregated[...], preferred_element_type=jnp.float32) + bias[...]
    )


def dense(weight, aggregated, bias):
    return pl.pallas_call(
        dense_kernel,
        out_shape=jax.ShapeDtypeStruct((weight.shape[0], aggregated.shape[1]), jnp.float32),
        in_specs=[VMEM] * 3,
        out_specs=VMEM,
        compiler_params=PARAMS,
        cost_estimate=pl.CostEstimate(
            flops=2 * weight.size * aggregated.shape[1],
            bytes_accessed=2 * (weight.size + 3 * aggregated.size),
            transcendentals=0,
        ),
    )(weight, aggregated, bias[:, None])


def body(x_t, adj_tiles, tile_rows, tile_cols, tile_counts, w_first, b_first, w_second, b_second):
    cubes = lax.axis_size("node") // GROUP
    plan = make_plan(tile_rows, tile_cols, tile_counts, cubes, x_t.shape[1] // BLK)
    y_first = gather_sums(x_t, adj_tiles, plan, cubes, False)
    z_first = jnp.dot(w_first, y_first, preferred_element_type=jnp.float32) + b_first[:, None]
    h_first = jnp.maximum(z_first, 0.0).astype(jnp.bfloat16)
    y_second = gather_sums(h_first, adj_tiles, plan, cubes, True)
    return dense(w_second, y_second, b_second)


def solution(mesh):
    return jax.shard_map(
        body,
        mesh=mesh,
        in_specs=(
            P("col", "node"),
            P("node", None, None),
            P("node"),
            P("node"),
            P("node"),
            P("col", None),
            P("col"),
            P("col", None),
            P("col"),
        ),
        out_specs=P("col", "node"),
        check_vma=False,
    )
```

```python
import functools

import jax
import jax.numpy as jnp
from jax import lax
from jax.experimental import pallas as pl
from jax.experimental.pallas import tpu as pltpu
from jax.sharding import PartitionSpec as P

BLK = 128
CAP = 2
GROUP = 8
NEAR = (0, 1, 2, 4)
PASSED = {7: 0, 4: 1, 1: 2, 2: 4}
STEPS = (7, 6, 3, 4, 5, 1, 2)
DEPTH = 4
RELAY_WORK = 50_000_000_000
WIDTH = 4
SMEM = pl.BlockSpec(memory_space=pltpu.SMEM)
VMEM = pl.BlockSpec(memory_space=pltpu.VMEM)
HBM = pl.BlockSpec(memory_space=pltpu.HBM)
PARAMS = pltpu.CompilerParams(vmem_limit_bytes=24 * 1024 * 1024)


def split(value, size):
    shift = size.bit_length() - 1
    if size == 1 << shift:
        return value >> shift, value & (size - 1)
    return lax.div(value, size), lax.rem(value, size)


def lowest(mask):
    return jnp.where(mask & 1 != 0, 0, jnp.where(mask & 2 != 0, 1, jnp.where(mask & 4 != 0, 2, 3)))


def highest(mask):
    return jnp.where(mask & 8 != 0, 3, jnp.where(mask & 4 != 0, 2, jnp.where(mask & 2 != 0, 1, 0)))


def owner_mask(words, owner, row_blocks):
    first = owner * row_blocks
    word = words[0]
    for at in range(1, len(words)):
        word = jnp.where(first >> 5 == at, words[at], word)
    return (word >> (first & 31)) & ((1 << row_blocks) - 1)


def words_kernel(count_ref, cols_ref, words_ref):
    live = count_ref[0]
    word_total = words_ref.shape[1]

    def step(slot, found):
        column = cols_ref[slot]
        bit = jnp.where(slot < live, 1 << (column & 31), 0)
        word = column >> 5
        return tuple(one | jnp.where(word == at, bit, 0) for at, one in enumerate(found))

    start = tuple(jnp.int32(0) for _ in range(word_total))
    found = lax.fori_loop(0, cols_ref.shape[0], step, start, unroll=8)
    for member in range(GROUP):
        for at in range(word_total):
            words_ref[member, at] = found[at]


def group_limit(tile_total, row_blocks):
    return -(-(tile_total // DEPTH + row_blocks) // WIDTH) * WIDTH


def list_kernel(cubes, row_blocks, count_ref, rows_ref, cols_ref, words_ref, lists, filled):
    tile_total = cols_ref.shape[0]
    node = lax.axis_index("node")
    cube, member = split(node, GROUP)
    words = [words_ref[0, at] for at in range(words_ref.shape[1])]
    limit = group_limit(tile_total, row_blocks)

    @pl.loop(0, limit)
    def _(group):
        lists[1 + group] = row_blocks
        for at in range(DEPTH):
            entry = 1 + limit + 2 * (group * DEPTH + at)
            lists[entry] = 0
            lists[entry + 1] = cubes * GROUP * CAP

    for row in range(row_blocks):
        filled[row] = 0

    @pl.loop(0, count_ref[0])
    def _(slot):
        row = rows_ref[slot]
        filled[row] = filled[row] + 1

    start = 0
    for row in range(row_blocks):
        groups, _ = split(filled[row] + DEPTH - 1, DEPTH)
        filled[row] = start * DEPTH

        @pl.loop(start, start + groups)
        def _(group):
            lists[1 + group] = row

        start = start + groups
    lists[0] = start

    @pl.loop(0, count_ref[0])
    def _(slot):
        owner, block = split(cols_ref[slot], row_blocks)
        home, other = split(owner, GROUP)
        unit = jnp.where(home >= cube, home - cube, home - cube + cubes)
        second = block != lowest(owner_mask(words, owner, row_blocks))
        row = rows_ref[slot]
        entry = 1 + limit + 2 * filled[row]
        filled[row] = filled[row] + 1
        lists[entry] = slot
        lists[entry + 1] = (unit * GROUP + (other ^ member)) * CAP + jnp.where(second, 1, 0)


def make_plan(tile_rows, tile_cols, tile_counts, cubes, row_blocks):
    tile_total = tile_cols.shape[0]
    word_total = -(-cubes * GROUP * row_blocks // 32)
    list_length = 1 + group_limit(tile_total, row_blocks) * (1 + 2 * DEPTH)
    own = pl.pallas_call(
        words_kernel,
        out_shape=jax.ShapeDtypeStruct((GROUP, word_total), jnp.int32),
        in_specs=[SMEM] * 2,
        out_specs=SMEM,
    )(tile_counts, tile_cols)
    lists = pl.pallas_call(
        functools.partial(list_kernel, cubes, row_blocks),
        out_shape=jax.ShapeDtypeStruct((list_length,), jnp.int32),
        in_specs=[SMEM] * 4,
        out_specs=SMEM,
        scratch_shapes=[pltpu.SMEM((row_blocks,), jnp.int32)],
    )(tile_counts, tile_rows, tile_cols, own)
    groups = [[cube * GROUP + member for member in range(GROUP)] for cube in range(cubes)]
    words = exchange(own, groups)
    return words, lists


def exchange(array, groups):
    return lax.all_to_all(
        array, "node", split_axis=0, concat_axis=0, tiled=True, axis_index_groups=groups
    )


def named_blocks(words_ref, member, owner, row_blocks):
    words = [words_ref[member, at] for at in range(words_ref.shape[1])]
    mask = owner_mask(words, owner, row_blocks)
    return [pl.multiple_of(block * BLK, BLK) for block in (lowest(mask), highest(mask))]


def pack_kernel(cubes, whole, messages, fetched, words_ref, *refs):
    held, refs = dict(zip(whole, refs)), refs[len(whole) :]
    total = len(messages)
    sent, packed, done = refs[:total], refs[total : 2 * total], refs[2 * total]
    row_blocks = held[whole[0]].shape[1] // BLK
    node = lax.axis_index("node")
    cube, member = split(node, GROUP)

    def fill(target, other, unit, source):
        owner = split(cube + unit, cubes)[1] * GROUP + (member ^ source)
        for slot, lane in enumerate(named_blocks(words_ref, other, owner, row_blocks)):
            target[slot] = held[unit, source][:, pl.ds(lane, BLK)]

    if fetched:
        own, held[0, 0] = held[0, 0], refs[-1]
        fetch = pltpu.make_async_copy(own, held[0, 0], done.at[total])
        fetch.start()
    copies = []
    for at, (step, sources) in reversed(list(enumerate(messages))):
        for part, (unit, source) in reversed(list(enumerate(sources))):
            if fetched and (unit, source) == (0, 0):
                fetch.wait()
            fill(packed[at].at[part], member ^ step, unit, source)
        copies.append(pltpu.make_async_copy(packed[at], sent[at], done.at[at]))
        copies[-1].start()
    for copy in copies:
        copy.wait()


def pack(cubes, words, held, messages, fetched, work):
    feat_local, nodes_local = next(iter(held.values())).shape
    shapes = [(len(sources), CAP, feat_local, BLK) for _, sources in messages]
    scratch = [pltpu.VMEM(shape, jnp.bfloat16) for shape in shapes]
    scratch += [pltpu.SemaphoreType.DMA((len(shapes) + 1,))]
    if fetched:
        scratch += [pltpu.VMEM((feat_local, nodes_local), jnp.bfloat16)]
        held = {**held, (0, 0): in_hbm(held[0, 0])}
    return pl.pallas_call(
        functools.partial(pack_kernel, cubes, tuple(held), messages, fetched),
        out_shape=[pltpu.HBM(shape, jnp.bfloat16) for shape in shapes],
        in_specs=[SMEM] + [HBM if fetched and at == (0, 0) else VMEM for at in held],
        out_specs=[HBM] * len(shapes),
        scratch_shapes=scratch,
        compiler_params=PARAMS,
        cost_estimate=pl.CostEstimate(flops=work, bytes_accessed=0, transcendentals=0),
    )(words, *held.values())


def in_hbm(array):
    return pltpu.with_memory_space_constraint(array, pltpu.HBM)


def keep_kernel(cubes, whole, words_ref, *refs):
    held, kept = refs[:-1], refs[-1]
    row_blocks = held[0].shape[1] // BLK
    node = lax.axis_index("node")
    cube, member = split(node, GROUP)
    for at, (unit, source) in enumerate(whole):
        owner = split(cube + unit, cubes)[1] * GROUP + (member ^ source)
        for slot, lane in enumerate(named_blocks(words_ref, member, owner, row_blocks)):
            kept[at, slot] = held[at][:, pl.ds(lane, BLK)]


def keep(cubes, words, held):
    shape = (len(held), CAP, held[0, 0].shape[0], BLK)
    return pl.pallas_call(
        functools.partial(keep_kernel, cubes, tuple(held)),
        out_shape=jax.ShapeDtypeStruct(shape, jnp.bfloat16),
        in_specs=[SMEM] + [VMEM] * len(held),
        out_specs=VMEM,
        compiler_params=PARAMS,
    )(words, *held.values())


def aggregate_kernel(cubes, limit, messages, fetched, lists_hbm, tiles, *refs):
    received, refs = refs[: len(messages)], refs[len(messages) :]
    out_ref, lists, blocks, total, done = refs[:5]
    pairs = [(lists_hbm, lists)]
    if fetched:
        pairs.append((tiles, refs[5]))
        tiles = refs[5]
    for (step, sources, far), array in zip(messages, received):
        for part, (unit, source) in enumerate(sources if far else ()):
            place = (unit * GROUP + (step ^ source)) * CAP
            pairs.append((array.at[part], blocks.at[place : place + CAP]))
    copies = [pltpu.make_async_copy(*pair, done.at[at]) for at, pair in enumerate(pairs)]
    for copy in copies:
        copy.start()
    total[...] = jnp.zeros_like(total)
    blocks[cubes * GROUP * CAP] = jnp.zeros_like(blocks[cubes * GROUP * CAP])
    for (step, sources, far), array in zip(messages, received):
        for part, (unit, source) in enumerate(() if far else sources):
            place = (unit * GROUP + (step ^ source)) * CAP
            blocks[place : place + CAP] = array[part]
    for copy in copies:
        copy.wait()

    @pl.loop(0, split(lists[0] + WIDTH - 1, WIDTH)[0])
    def _(loop_step):
        sums = []
        for wide in range(WIDTH):
            group = loop_step * WIDTH + wide
            left, right = [], []
            for at in range(DEPTH):
                entry = 1 + limit + 2 * (group * DEPTH + at)
                left.append(blocks[lists[entry + 1]])
                right.append(tiles[lists[entry]])
            summed = lax.dot_general(
                jnp.concatenate(left, axis=1),
                jnp.concatenate(right, axis=1),
                (((1,), (1,)), ((), ())),
                preferred_element_type=jnp.float32,
            )
            sums.append((lists[1 + group], summed))
        for row, summed in sums:
            total[row] += summed

    for row in range(out_ref.shape[1] // BLK):
        out_ref[:, row * BLK : (row + 1) * BLK] = total[row].astype(out_ref.dtype)


def aggregate(cubes, messages, fetched, lists, adj_tiles, received, nodes_local):
    feat_local = received[0].shape[2]
    row_blocks = nodes_local // BLK
    limit = group_limit(adj_tiles.shape[0], row_blocks)
    operands = [in_hbm(adj_tiles) if fetched else adj_tiles]
    operands += [in_hbm(one) if far else one for one, (_, _, far) in zip(received, messages)]
    spaces = [HBM if fetched else VMEM] + [HBM if far else VMEM for _, _, far in messages]
    scratch = [
        pltpu.SMEM(lists.shape, jnp.int32),
        pltpu.VMEM((cubes * GROUP * CAP + 1, feat_local, BLK), jnp.bfloat16),
        pltpu.VMEM((row_blocks + 1, feat_local, BLK), jnp.float32),
        pltpu.SemaphoreType.DMA((2 + cubes * GROUP,)),
    ]
    if fetched:
        scratch.append(pltpu.VMEM(adj_tiles.shape, jnp.bfloat16))
    return pl.pallas_call(
        functools.partial(aggregate_kernel, cubes, limit, messages, fetched),
        out_shape=jax.ShapeDtypeStruct((feat_local, nodes_local), jnp.bfloat16),
        in_specs=[HBM] + spaces,
        out_specs=VMEM,
        scratch_shapes=scratch,
        compiler_params=PARAMS,
        cost_estimate=pl.CostEstimate(
            flops=2 * adj_tiles.shape[0] * feat_local * BLK * BLK,
            bytes_accessed=2 * sum(one.size for one in operands),
            transcendentals=0,
        ),
    )(in_hbm(lists), *operands)


def gather_sums(feat_t, adj_tiles, plan, cubes, by_planes):
    words, lists = plan
    nodes = cubes * GROUP

    def to_member(array, step):
        return lax.ppermute(array, "node", [(n, n ^ step) for n in range(nodes)])

    relayed = {
        (unit, 0): lax.ppermute(
            feat_t, "node", [(n, (n - unit * GROUP) % nodes) for n in range(nodes)]
        )
        for unit in range(1, cubes)
    }
    if by_planes:
        held = {(0, 0): feat_t, **relayed}
        held.update({(unit, 4): to_member(array, 4) for (unit, _), array in held.items()})
        batches = [
            ([(0, 0)], 0),
            ([(0, 4)] + list(relayed), RELAY_WORK),
            ([(unit, 4) for unit, _ in relayed], RELAY_WORK),
        ]
        messages, received = [], []
        for number, (sources, work) in enumerate(batches):
            batch = [(step, sources) for step in (3, 1, 2, 0)]
            array = {at: held[at] for at in sources}
            sent = pack(cubes, words, array, batch, False, work)
            for one, (step, _) in zip(sent, batch):
                messages.append((step, sources, number == 0 or step == 0))
                received.append(to_member(one, step) if step else one)
    else:
        near = {(0, step): to_member(feat_t, step) if step else feat_t for step in NEAR}
        held = {**relayed, **near}
        batch = [
            (step, ([(0, PASSED[step])] if step in PASSED else []) + list(relayed))
            for step in STEPS
        ]
        sent = pack(cubes, words, held, batch, True, 0)
        received = [to_member(one, step) for one, (step, _) in zip(sent, batch)]
        received.append(keep(cubes, words, held))
        messages = [(*one, False) for one in batch] + [(0, list(held), False)]
    local = aggregate(
        cubes, messages, not by_planes, lists, adj_tiles, received, feat_t.shape[1]
    )
    return lax.all_gather(local, "col", axis=0, tiled=True)


def dense_kernel(weight, aggregated, bias, out_ref):
    out_ref[...] = (
        jnp.dot(weight[...], aggregated[...], preferred_element_type=jnp.float32) + bias[...]
    )


def dense(weight, aggregated, bias):
    return pl.pallas_call(
        dense_kernel,
        out_shape=jax.ShapeDtypeStruct((weight.shape[0], aggregated.shape[1]), jnp.float32),
        in_specs=[VMEM] * 3,
        out_specs=VMEM,
        compiler_params=PARAMS,
        cost_estimate=pl.CostEstimate(
            flops=2 * weight.size * aggregated.shape[1],
            bytes_accessed=2 * (weight.size + 3 * aggregated.size),
            transcendentals=0,
        ),
    )(weight, aggregated, bias[:, None])


def body(x_t, adj_tiles, tile_rows, tile_cols, tile_counts, w_first, b_first, w_second, b_second):
    cubes = lax.axis_size("node") // GROUP
    plan = make_plan(tile_rows, tile_cols, tile_counts, cubes, x_t.shape[1] // BLK)
    y_first = gather_sums(x_t, adj_tiles, plan, cubes, False)
    z_first = jnp.dot(w_first, y_first, preferred_element_type=jnp.float32) + b_first[:, None]
    h_first = jnp.maximum(z_first, 0.0).astype(jnp.bfloat16)
    y_second = gather_sums(h_first, adj_tiles, plan, cubes, True)
    return dense(w_second, y_second, b_second)


def solution(mesh):
    return jax.shard_map(
        body,
        mesh=mesh,
        in_specs=(
            P("col", "node"),
            P("node", None, None),
            P("node"),
            P("node"),
            P("node"),
            P("col", None),
            P("col"),
            P("col", None),
            P("col"),
        ),
        out_specs=P("col", "node"),
        check_vma=False,
    )
```

```python
import functools

import jax
import jax.numpy as jnp
from jax import lax
from jax.experimental import pallas as pl
from jax.experimental.pallas import tpu as pltpu
from jax.sharding import PartitionSpec as P

BLK = 128
CAP = 2
GROUP = 8
NEAR = (0, 1, 2, 4)
PASSED = {7: 0, 4: 1, 1: 2, 2: 4}
STEPS = (7, 6, 3, 4, 5, 1, 2)
DEPTH = 4
RELAY_WORK = 50_000_000_000
WIDTH = 4
SMEM = pl.BlockSpec(memory_space=pltpu.SMEM)
VMEM = pl.BlockSpec(memory_space=pltpu.VMEM)
HBM = pl.BlockSpec(memory_space=pltpu.HBM)
PARAMS = pltpu.CompilerParams(vmem_limit_bytes=24 * 1024 * 1024)


def split(value, size):
    shift = size.bit_length() - 1
    if size == 1 << shift:
        return value >> shift, value & (size - 1)
    return lax.div(value, size), lax.rem(value, size)


def lowest(mask):
    return jnp.where(mask & 1 != 0, 0, jnp.where(mask & 2 != 0, 1, jnp.where(mask & 4 != 0, 2, 3)))


def highest(mask):
    return jnp.where(mask & 8 != 0, 3, jnp.where(mask & 4 != 0, 2, jnp.where(mask & 2 != 0, 1, 0)))


def owner_mask(words, owner, row_blocks):
    first = owner * row_blocks
    word = words[0]
    for at in range(1, len(words)):
        word = jnp.where(first >> 5 == at, words[at], word)
    return (word >> (first & 31)) & ((1 << row_blocks) - 1)


def words_kernel(count_ref, cols_ref, words_ref):
    live = count_ref[0]
    word_total = words_ref.shape[1]

    def step(slot, found):
        column = cols_ref[slot]
        bit = jnp.where(slot < live, 1 << (column & 31), 0)
        word = column >> 5
        return tuple(one | jnp.where(word == at, bit, 0) for at, one in enumerate(found))

    start = tuple(jnp.int32(0) for _ in range(word_total))
    found = lax.fori_loop(0, cols_ref.shape[0], step, start, unroll=8)
    for member in range(GROUP):
        for at in range(word_total):
            words_ref[member, at] = found[at]


def group_limit(tile_total, row_blocks):
    return -(-(tile_total // DEPTH + row_blocks) // WIDTH) * WIDTH


def list_kernel(cubes, row_blocks, count_ref, rows_ref, cols_ref, words_ref, lists, filled):
    tile_total = cols_ref.shape[0]
    node = lax.axis_index("node")
    cube, member = split(node, GROUP)
    words = [words_ref[0, at] for at in range(words_ref.shape[1])]
    limit = group_limit(tile_total, row_blocks)

    @pl.loop(0, limit)
    def _(group):
        lists[1 + group] = row_blocks
        for at in range(DEPTH):
            entry = 1 + limit + 2 * (group * DEPTH + at)
            lists[entry] = 0
            lists[entry + 1] = cubes * GROUP * CAP

    for row in range(row_blocks):
        filled[row] = 0

    @pl.loop(0, count_ref[0])
    def _(slot):
        row = rows_ref[slot]
        filled[row] = filled[row] + 1

    start = 0
    for row in range(row_blocks):
        groups, _ = split(filled[row] + DEPTH - 1, DEPTH)
        filled[row] = start * DEPTH

        @pl.loop(start, start + groups)
        def _(group):
            lists[1 + group] = row

        start = start + groups
    lists[0] = start

    @pl.loop(0, count_ref[0])
    def _(slot):
        owner, block = split(cols_ref[slot], row_blocks)
        home, other = split(owner, GROUP)
        unit = jnp.where(home >= cube, home - cube, home - cube + cubes)
        second = block != lowest(owner_mask(words, owner, row_blocks))
        row = rows_ref[slot]
        entry = 1 + limit + 2 * filled[row]
        filled[row] = filled[row] + 1
        lists[entry] = slot
        lists[entry + 1] = (unit * GROUP + (other ^ member)) * CAP + jnp.where(second, 1, 0)


def make_plan(tile_rows, tile_cols, tile_counts, cubes, row_blocks):
    tile_total = tile_cols.shape[0]
    word_total = -(-cubes * GROUP * row_blocks // 32)
    list_length = 1 + group_limit(tile_total, row_blocks) * (1 + 2 * DEPTH)
    own = pl.pallas_call(
        words_kernel,
        out_shape=jax.ShapeDtypeStruct((GROUP, word_total), jnp.int32),
        in_specs=[SMEM] * 2,
        out_specs=SMEM,
    )(tile_counts, tile_cols)
    lists = pl.pallas_call(
        functools.partial(list_kernel, cubes, row_blocks),
        out_shape=jax.ShapeDtypeStruct((list_length,), jnp.int32),
        in_specs=[SMEM] * 4,
        out_specs=SMEM,
        scratch_shapes=[pltpu.SMEM((row_blocks,), jnp.int32)],
    )(tile_counts, tile_rows, tile_cols, own)
    groups = [[cube * GROUP + member for member in range(GROUP)] for cube in range(cubes)]
    words = exchange(own, groups)
    return words, lists


def exchange(array, groups):
    return lax.all_to_all(
        array, "node", split_axis=0, concat_axis=0, tiled=True, axis_index_groups=groups
    )


def named_blocks(words_ref, member, owner, row_blocks):
    words = [words_ref[member, at] for at in range(words_ref.shape[1])]
    mask = owner_mask(words, owner, row_blocks)
    return [pl.multiple_of(block * BLK, BLK) for block in (lowest(mask), highest(mask))]


def pack_kernel(cubes, whole, messages, fetched, words_ref, *refs):
    held, refs = dict(zip(whole, refs)), refs[len(whole) :]
    total = len(messages)
    sent, packed, done = refs[:total], refs[total : 2 * total], refs[2 * total]
    row_blocks = held[whole[0]].shape[1] // BLK
    node = lax.axis_index("node")
    cube, member = split(node, GROUP)

    def fill(target, other, unit, source):
        owner = split(cube + unit, cubes)[1] * GROUP + (member ^ source)
        for slot, lane in enumerate(named_blocks(words_ref, other, owner, row_blocks)):
            target[slot] = held[unit, source][:, pl.ds(lane, BLK)]

    if fetched:
        own, held[0, 0] = held[0, 0], refs[-1]
        fetch = pltpu.make_async_copy(own, held[0, 0], done.at[total])
        fetch.start()
    copies = []
    for at, (step, sources) in reversed(list(enumerate(messages))):
        for part, (unit, source) in reversed(list(enumerate(sources))):
            if fetched and (unit, source) == (0, 0):
                fetch.wait()
            fill(packed[at].at[part], member ^ step, unit, source)
        copies.append(pltpu.make_async_copy(packed[at], sent[at], done.at[at]))
        copies[-1].start()
    for copy in copies:
        copy.wait()


def pack(cubes, words, held, messages, fetched, work):
    feat_local, nodes_local = next(iter(held.values())).shape
    shapes = [(len(sources), CAP, feat_local, BLK) for _, sources in messages]
    scratch = [pltpu.VMEM(shape, jnp.bfloat16) for shape in shapes]
    scratch += [pltpu.SemaphoreType.DMA((len(shapes) + 1,))]
    if fetched:
        scratch += [pltpu.VMEM((feat_local, nodes_local), jnp.bfloat16)]
        held = {**held, (0, 0): in_hbm(held[0, 0])}
    return pl.pallas_call(
        functools.partial(pack_kernel, cubes, tuple(held), messages, fetched),
        out_shape=[pltpu.HBM(shape, jnp.bfloat16) for shape in shapes],
        in_specs=[SMEM] + [HBM if fetched and at == (0, 0) else VMEM for at in held],
        out_specs=[HBM] * len(shapes),
        scratch_shapes=scratch,
        compiler_params=PARAMS,
        cost_estimate=pl.CostEstimate(flops=work, bytes_accessed=0, transcendentals=0),
    )(words, *held.values())


def in_hbm(array):
    return pltpu.with_memory_space_constraint(array, pltpu.HBM)


def keep_kernel(cubes, whole, words_ref, *refs):
    held, kept = refs[:-1], refs[-1]
    row_blocks = held[0].shape[1] // BLK
    node = lax.axis_index("node")
    cube, member = split(node, GROUP)
    for at, (unit, source) in enumerate(whole):
        owner = split(cube + unit, cubes)[1] * GROUP + (member ^ source)
        for slot, lane in enumerate(named_blocks(words_ref, member, owner, row_blocks)):
            kept[at, slot] = held[at][:, pl.ds(lane, BLK)]


def keep(cubes, words, held):
    shape = (len(held), CAP, held[0, 0].shape[0], BLK)
    return pl.pallas_call(
        functools.partial(keep_kernel, cubes, tuple(held)),
        out_shape=jax.ShapeDtypeStruct(shape, jnp.bfloat16),
        in_specs=[SMEM] + [VMEM] * len(held),
        out_specs=VMEM,
        compiler_params=PARAMS,
    )(words, *held.values())


def aggregate_kernel(cubes, limit, messages, fetched, lists_hbm, tiles, *refs):
    received, refs = refs[: len(messages)], refs[len(messages) :]
    out_ref, lists, blocks, total, done = refs[:5]
    pairs = [(lists_hbm, lists)]
    if fetched:
        pairs.append((tiles, refs[5]))
        tiles = refs[5]
    for (step, sources, far), array in zip(messages, received):
        for part, (unit, source) in enumerate(sources if far else ()):
            place = (unit * GROUP + (step ^ source)) * CAP
            pairs.append((array.at[part], blocks.at[place : place + CAP]))
    copies = [pltpu.make_async_copy(*pair, done.at[at]) for at, pair in enumerate(pairs)]
    for copy in copies:
        copy.start()
    total[...] = jnp.zeros_like(total)
    blocks[cubes * GROUP * CAP] = jnp.zeros_like(blocks[cubes * GROUP * CAP])
    for (step, sources, far), array in zip(messages, received):
        for part, (unit, source) in enumerate(() if far else sources):
            place = (unit * GROUP + (step ^ source)) * CAP
            blocks[place : place + CAP] = array[part]
    for copy in copies:
        copy.wait()

    @pl.loop(0, split(lists[0] + WIDTH - 1, WIDTH)[0])
    def _(loop_step):
        sums = []
        for wide in range(WIDTH):
            group = loop_step * WIDTH + wide
            left, right = [], []
            for at in range(DEPTH):
                entry = 1 + limit + 2 * (group * DEPTH + at)
                left.append(blocks[lists[entry + 1]])
                right.append(tiles[lists[entry]])
            summed = lax.dot_general(
                jnp.concatenate(left, axis=1),
                jnp.concatenate(right, axis=1),
                (((1,), (1,)), ((), ())),
                preferred_element_type=jnp.float32,
            )
            sums.append((lists[1 + group], summed))
        for row, summed in sums:
            total[row] += summed

    for row in range(out_ref.shape[1] // BLK):
        out_ref[:, row * BLK : (row + 1) * BLK] = total[row].astype(out_ref.dtype)


def aggregate(cubes, messages, fetched, lists, adj_tiles, received, nodes_local):
    feat_local = received[0].shape[2]
    row_blocks = nodes_local // BLK
    limit = group_limit(adj_tiles.shape[0], row_blocks)
    operands = [in_hbm(adj_tiles) if fetched else adj_tiles]
    operands += [in_hbm(one) if far else one for one, (_, _, far) in zip(received, messages)]
    spaces = [HBM if fetched else VMEM] + [HBM if far else VMEM for _, _, far in messages]
    scratch = [
        pltpu.SMEM(lists.shape, jnp.int32),
        pltpu.VMEM((cubes * GROUP * CAP + 1, feat_local, BLK), jnp.bfloat16),
        pltpu.VMEM((row_blocks + 1, feat_local, BLK), jnp.float32),
        pltpu.SemaphoreType.DMA((2 + cubes * GROUP,)),
    ]
    if fetched:
        scratch.append(pltpu.VMEM(adj_tiles.shape, jnp.bfloat16))
    return pl.pallas_call(
        functools.partial(aggregate_kernel, cubes, limit, messages, fetched),
        out_shape=jax.ShapeDtypeStruct((feat_local, nodes_local), jnp.bfloat16),
        in_specs=[HBM] + spaces,
        out_specs=VMEM,
        scratch_shapes=scratch,
        compiler_params=PARAMS,
        cost_estimate=pl.CostEstimate(
            flops=2 * adj_tiles.shape[0] * feat_local * BLK * BLK,
            bytes_accessed=2 * sum(one.size for one in operands),
            transcendentals=0,
        ),
    )(in_hbm(lists), *operands)


def gather_sums(feat_t, adj_tiles, plan, cubes, by_planes):
    words, lists = plan
    nodes = cubes * GROUP

    def to_member(array, step):
        return lax.ppermute(array, "node", [(n, n ^ step) for n in range(nodes)])

    relayed = {
        (unit, 0): lax.ppermute(
            feat_t, "node", [(n, (n - unit * GROUP) % nodes) for n in range(nodes)]
        )
        for unit in range(1, cubes)
    }
    if by_planes:
        held = {(0, 0): feat_t, **relayed}
        held.update({(unit, 4): to_member(array, 4) for (unit, _), array in held.items()})
        batches = [
            ([(0, 0)], 0),
            ([(0, 4)] + list(relayed), RELAY_WORK),
            ([(unit, 4) for unit, _ in relayed], RELAY_WORK),
        ]
        messages, received = [], []
        for number, (sources, work) in enumerate(batches):
            batch = [(step, sources) for step in (3, 1, 2, 0)]
            array = {at: held[at] for at in sources}
            sent = pack(cubes, words, array, batch, False, work)
            for one, (step, _) in zip(sent, batch):
                far = number == 0 or step == 0 or (number, step) == (2, 2)
                messages.append((step, sources, far))
                received.append(to_member(one, step) if step else one)
    else:
        near = {(0, step): to_member(feat_t, step) if step else feat_t for step in NEAR}
        held = {**relayed, **near}
        batch = [
            (step, ([(0, PASSED[step])] if step in PASSED else []) + list(relayed))
            for step in STEPS
        ]
        sent = list(pack(cubes, words, held, batch, True, 0))
        kept = keep(cubes, words, held)
        sent[4], kept, lists = lax.optimization_barrier((sent[4], kept, lists))
        received = [to_member(one, step) for one, (step, _) in zip(sent, batch)]
        received.append(kept)
        messages = [(*one, False) for one in batch] + [(0, list(held), False)]
    local = aggregate(
        cubes, messages, not by_planes, lists, adj_tiles, received, feat_t.shape[1]
    )
    return lax.all_gather(local, "col", axis=0, tiled=True)


def dense_kernel(weight, aggregated, bias, out_ref):
    out_ref[...] = (
        jnp.dot(weight[...], aggregated[...], preferred_element_type=jnp.float32) + bias[...]
    )


def dense(weight, aggregated, bias):
    return pl.pallas_call(
        dense_kernel,
        out_shape=jax.ShapeDtypeStruct((weight.shape[0], aggregated.shape[1]), jnp.float32),
        in_specs=[VMEM] * 3,
        out_specs=VMEM,
        compiler_params=PARAMS,
        cost_estimate=pl.CostEstimate(
            flops=2 * weight.size * aggregated.shape[1],
            bytes_accessed=2 * (weight.size + 3 * aggregated.size),
            transcendentals=0,
        ),
    )(weight, aggregated, bias[:, None])


def body(x_t, adj_tiles, tile_rows, tile_cols, tile_counts, w_first, b_first, w_second, b_second):
    cubes = lax.axis_size("node") // GROUP
    plan = make_plan(tile_rows, tile_cols, tile_counts, cubes, x_t.shape[1] // BLK)
    y_first = gather_sums(x_t, adj_tiles, plan, cubes, False)
    z_first = jnp.dot(w_first, y_first, preferred_element_type=jnp.float32) + b_first[:, None]
    h_first = jnp.maximum(z_first, 0.0).astype(jnp.bfloat16)
    y_second = gather_sums(h_first, adj_tiles, plan, cubes, True)
    return dense(w_second, y_second, b_second)


def solution(mesh):
    return jax.shard_map(
        body,
        mesh=mesh,
        in_specs=(
            P("col", "node"),
            P("node", None, None),
            P("node"),
            P("node"),
            P("node"),
            P("col", None),
            P("col"),
            P("col", None),
            P("col"),
        ),
        out_specs=P("col", "node"),
        check_vma=False,
    )
```

```python
import functools

import jax
import jax.numpy as jnp
from jax import lax
from jax.experimental import pallas as pl
from jax.experimental.pallas import tpu as pltpu
from jax.sharding import PartitionSpec as P

BLK = 128
CAP = 2
GROUP = 8
NEAR = (0, 1, 2, 4)
PAIRED = 5
PASSED = {7: 0, 4: 1, 1: 2, 2: 4}
STEPS = (7, 6, 3, 4, 5, 1, 2)
DEPTH = 4
RELAY_WORK = 50_000_000_000
WIDTH = 4
SMEM = pl.BlockSpec(memory_space=pltpu.SMEM)
VMEM = pl.BlockSpec(memory_space=pltpu.VMEM)
HBM = pl.BlockSpec(memory_space=pltpu.HBM)
PARAMS = pltpu.CompilerParams(vmem_limit_bytes=24 * 1024 * 1024)


def split(value, size):
    shift = size.bit_length() - 1
    if size == 1 << shift:
        return value >> shift, value & (size - 1)
    return lax.div(value, size), lax.rem(value, size)


def lowest(mask):
    return jnp.where(mask & 1 != 0, 0, jnp.where(mask & 2 != 0, 1, jnp.where(mask & 4 != 0, 2, 3)))


def highest(mask):
    return jnp.where(mask & 8 != 0, 3, jnp.where(mask & 4 != 0, 2, jnp.where(mask & 2 != 0, 1, 0)))


def owner_mask(words, owner, row_blocks):
    first = owner * row_blocks
    word = words[0]
    for at in range(1, len(words)):
        word = jnp.where(first >> 5 == at, words[at], word)
    return (word >> (first & 31)) & ((1 << row_blocks) - 1)


def words_kernel(count_ref, cols_ref, words_ref):
    live = count_ref[0]
    word_total = words_ref.shape[1]

    def step(slot, found):
        column = cols_ref[slot]
        bit = jnp.where(slot < live, 1 << (column & 31), 0)
        word = column >> 5
        return tuple(one | jnp.where(word == at, bit, 0) for at, one in enumerate(found))

    start = tuple(jnp.int32(0) for _ in range(word_total))
    found = lax.fori_loop(0, cols_ref.shape[0], step, start, unroll=8)
    for member in range(GROUP):
        for at in range(word_total):
            words_ref[member, at] = found[at]


def group_limit(tile_total, row_blocks):
    return -(-(tile_total // DEPTH + row_blocks) // WIDTH) * WIDTH


def list_kernel(cubes, row_blocks, count_ref, rows_ref, cols_ref, words_ref, lists, filled):
    tile_total = cols_ref.shape[0]
    node = lax.axis_index("node")
    cube, member = split(node, GROUP)
    words = [words_ref[0, at] for at in range(words_ref.shape[1])]
    limit = group_limit(tile_total, row_blocks)

    @pl.loop(0, limit)
    def _(group):
        lists[1 + group] = row_blocks
        for at in range(DEPTH):
            entry = 1 + limit + 2 * (group * DEPTH + at)
            lists[entry] = 0
            lists[entry + 1] = cubes * GROUP * CAP

    for row in range(row_blocks):
        filled[row] = 0

    @pl.loop(0, count_ref[0])
    def _(slot):
        row = rows_ref[slot]
        filled[row] = filled[row] + 1

    start = 0
    for row in range(row_blocks):
        groups, _ = split(filled[row] + DEPTH - 1, DEPTH)
        filled[row] = start * DEPTH

        @pl.loop(start, start + groups)
        def _(group):
            lists[1 + group] = row

        start = start + groups
    lists[0] = start

    @pl.loop(0, count_ref[0])
    def _(slot):
        owner, block = split(cols_ref[slot], row_blocks)
        home, other = split(owner, GROUP)
        unit = jnp.where(home >= cube, home - cube, home - cube + cubes)
        second = block != lowest(owner_mask(words, owner, row_blocks))
        row = rows_ref[slot]
        entry = 1 + limit + 2 * filled[row]
        filled[row] = filled[row] + 1
        lists[entry] = slot
        lists[entry + 1] = (unit * GROUP + (other ^ member)) * CAP + jnp.where(second, 1, 0)


def make_plan(tile_rows, tile_cols, tile_counts, cubes, row_blocks):
    tile_total = tile_cols.shape[0]
    word_total = -(-cubes * GROUP * row_blocks // 32)
    list_length = 1 + group_limit(tile_total, row_blocks) * (1 + 2 * DEPTH)
    own = pl.pallas_call(
        words_kernel,
        out_shape=jax.ShapeDtypeStruct((GROUP, word_total), jnp.int32),
        in_specs=[SMEM] * 2,
        out_specs=SMEM,
    )(tile_counts, tile_cols)
    make_lists = pl.pallas_call(
        functools.partial(list_kernel, cubes, row_blocks),
        out_shape=jax.ShapeDtypeStruct((list_length,), jnp.int32),
        in_specs=[SMEM] * 4,
        out_specs=SMEM,
        scratch_shapes=[pltpu.SMEM((row_blocks,), jnp.int32)],
    )
    groups = [[cube * GROUP + member for member in range(GROUP)] for cube in range(cubes)]
    words = exchange(own, groups)
    return words, lambda rows: make_lists(tile_counts, rows, tile_cols, own)


def exchange(array, groups):
    return lax.all_to_all(
        array, "node", split_axis=0, concat_axis=0, tiled=True, axis_index_groups=groups
    )


def named_blocks(words_ref, member, owner, row_blocks):
    words = [words_ref[member, at] for at in range(words_ref.shape[1])]
    mask = owner_mask(words, owner, row_blocks)
    return [pl.multiple_of(block * BLK, BLK) for block in (lowest(mask), highest(mask))]


def pack_kernel(cubes, whole, messages, fetched, words_ref, *refs):
    held, refs = dict(zip(whole, refs)), refs[len(whole) :]
    total = len(messages)
    sent, packed, done = refs[:total], refs[total : 2 * total], refs[2 * total]
    row_blocks = held[whole[0]].shape[1] // BLK
    node = lax.axis_index("node")
    cube, member = split(node, GROUP)

    def fill(target, other, unit, source):
        owner = split(cube + unit, cubes)[1] * GROUP + (member ^ source)
        for slot, lane in enumerate(named_blocks(words_ref, other, owner, row_blocks)):
            target[slot] = held[unit, source][:, pl.ds(lane, BLK)]

    if fetched:
        own, held[0, 0] = held[0, 0], refs[-1]
        fetch = pltpu.make_async_copy(own, held[0, 0], done.at[total])
        fetch.start()
    copies = []
    for at, (step, sources) in reversed(list(enumerate(messages))):
        for part, (unit, source) in reversed(list(enumerate(sources))):
            if fetched and (unit, source) == (0, 0):
                fetch.wait()
            if step == PAIRED:
                for place in range(2):
                    fill(packed[at].at[place, part], member ^ step, unit, source)
            else:
                fill(packed[at].at[part], member ^ step, unit, source)
        copies.append(pltpu.make_async_copy(packed[at], sent[at], done.at[at]))
        copies[-1].start()
    for copy in copies:
        copy.wait()


def pack(cubes, words, held, messages, fetched, work):
    feat_local, nodes_local = next(iter(held.values())).shape
    shapes = [
        (2,) * (step == PAIRED) + (len(sources), CAP, feat_local, BLK)
        for step, sources in messages
    ]
    scratch = [pltpu.VMEM(shape, jnp.bfloat16) for shape in shapes]
    scratch += [pltpu.SemaphoreType.DMA((len(shapes) + 1,))]
    if fetched:
        scratch += [pltpu.VMEM((feat_local, nodes_local), jnp.bfloat16)]
        held = {**held, (0, 0): in_hbm(held[0, 0])}
    return pl.pallas_call(
        functools.partial(pack_kernel, cubes, tuple(held), messages, fetched),
        out_shape=[pltpu.HBM(shape, jnp.bfloat16) for shape in shapes],
        in_specs=[SMEM] + [HBM if fetched and at == (0, 0) else VMEM for at in held],
        out_specs=[HBM] * len(shapes),
        scratch_shapes=scratch,
        compiler_params=PARAMS,
        cost_estimate=pl.CostEstimate(flops=work, bytes_accessed=0, transcendentals=0),
    )(words, *held.values())


def in_hbm(array):
    return pltpu.with_memory_space_constraint(array, pltpu.HBM)


def keep_kernel(cubes, whole, words_ref, *refs):
    held, kept = refs[:-1], refs[-1]
    row_blocks = held[0].shape[1] // BLK
    node = lax.axis_index("node")
    cube, member = split(node, GROUP)
    for at, (unit, source) in enumerate(whole):
        owner = split(cube + unit, cubes)[1] * GROUP + (member ^ source)
        for slot, lane in enumerate(named_blocks(words_ref, member, owner, row_blocks)):
            kept[at, slot] = held[at][:, pl.ds(lane, BLK)]


def keep(cubes, words, held):
    shape = (len(held), CAP, held[0, 0].shape[0], BLK)
    return pl.pallas_call(
        functools.partial(keep_kernel, cubes, tuple(held)),
        out_shape=jax.ShapeDtypeStruct(shape, jnp.bfloat16),
        in_specs=[SMEM] + [VMEM] * len(held),
        out_specs=VMEM,
        compiler_params=PARAMS,
    )(words, *held.values())


def aggregate_kernel(cubes, limit, messages, fetched, lists_hbm, tiles, *refs):
    received, refs = refs[: len(messages)], refs[len(messages) :]
    out_ref, lists, blocks, total, done = refs[:5]
    pairs = [(lists_hbm, lists)]
    if fetched:
        pairs.append((tiles, refs[5]))
        tiles = refs[5]
    for (step, sources, far), array in zip(messages, received):
        for part, (unit, source) in enumerate(sources if far else ()):
            place = (unit * GROUP + (step ^ source)) * CAP
            pairs.append((array.at[part], blocks.at[place : place + CAP]))
    copies = [pltpu.make_async_copy(*pair, done.at[at]) for at, pair in enumerate(pairs)]
    for copy in copies:
        copy.start()
    other = 1 - (lax.axis_index("node") & (GROUP - 1)) // (GROUP // 2)
    total[...] = jnp.zeros_like(total)
    blocks[cubes * GROUP * CAP] = jnp.zeros_like(blocks[cubes * GROUP * CAP])
    for (step, sources, far), array in zip(messages, received):
        for part, (unit, source) in enumerate(() if far else sources):
            place = (unit * GROUP + (step ^ source)) * CAP
            blocks[place : place + CAP] = array[other, part] if step == PAIRED else array[part]
    for copy in copies:
        copy.wait()

    @pl.loop(0, split(lists[0] + WIDTH - 1, WIDTH)[0])
    def _(loop_step):
        sums = []
        for wide in range(WIDTH):
            group = loop_step * WIDTH + wide
            left, right = [], []
            for at in range(DEPTH):
                entry = 1 + limit + 2 * (group * DEPTH + at)
                left.append(blocks[lists[entry + 1]])
                right.append(tiles[lists[entry]])
            summed = lax.dot_general(
                jnp.concatenate(left, axis=1),
                jnp.concatenate(right, axis=1),
                (((1,), (1,)), ((), ())),
                preferred_element_type=jnp.float32,
            )
            sums.append((lists[1 + group], summed))
        for row, summed in sums:
            total[row] += summed

    for row in range(out_ref.shape[1] // BLK):
        out_ref[:, row * BLK : (row + 1) * BLK] = total[row].astype(out_ref.dtype)


def aggregate(cubes, messages, fetched, lists, adj_tiles, received, nodes_local):
    feat_local = received[0].shape[-2]
    row_blocks = nodes_local // BLK
    limit = group_limit(adj_tiles.shape[0], row_blocks)
    operands = [in_hbm(adj_tiles) if fetched else adj_tiles]
    operands += [in_hbm(one) if far else one for one, (_, _, far) in zip(received, messages)]
    spaces = [HBM if fetched else VMEM] + [HBM if far else VMEM for _, _, far in messages]
    scratch = [
        pltpu.SMEM(lists.shape, jnp.int32),
        pltpu.VMEM((cubes * GROUP * CAP + 1, feat_local, BLK), jnp.bfloat16),
        pltpu.VMEM((row_blocks + 1, feat_local, BLK), jnp.float32),
        pltpu.SemaphoreType.DMA((2 + cubes * GROUP,)),
    ]
    if fetched:
        scratch.append(pltpu.VMEM(adj_tiles.shape, jnp.bfloat16))
    return pl.pallas_call(
        functools.partial(aggregate_kernel, cubes, limit, messages, fetched),
        out_shape=jax.ShapeDtypeStruct((feat_local, nodes_local), jnp.bfloat16),
        in_specs=[HBM] + spaces,
        out_specs=VMEM,
        scratch_shapes=scratch,
        compiler_params=PARAMS,
        cost_estimate=pl.CostEstimate(
            flops=2 * adj_tiles.shape[0] * feat_local * BLK * BLK,
            bytes_accessed=2 * sum(one.size for one in operands),
            transcendentals=0,
        ),
    )(in_hbm(lists), *operands)


def gather_sums(feat_t, adj_tiles, plan, cubes, by_planes):
    words, make_lists, lists = plan
    nodes = cubes * GROUP

    def to_member(array, step):
        return lax.ppermute(array, "node", [(n, n ^ step) for n in range(nodes)])

    relayed = {
        (unit, 0): lax.ppermute(
            feat_t, "node", [(n, (n - unit * GROUP) % nodes) for n in range(nodes)]
        )
        for unit in range(1, cubes)
    }
    if by_planes:
        held = {(0, 0): feat_t, **relayed}
        held.update({(unit, 4): to_member(array, 4) for (unit, _), array in held.items()})
        batches = [
            ([(0, 0)], 0),
            ([(0, 4)] + list(relayed), RELAY_WORK),
            ([(unit, 4) for unit, _ in relayed], RELAY_WORK),
        ]
        messages, received = [], []
        for number, (sources, work) in enumerate(batches):
            batch = [(step, sources) for step in (3, 1, 2, 0)]
            array = {at: held[at] for at in sources}
            sent = pack(cubes, words, array, batch, False, work)
            for one, (step, _) in zip(sent, batch):
                far = number == 0 or step == 0 or (number, step) == (2, 2)
                messages.append((step, sources, far))
                received.append(to_member(one, step) if step else one)
    else:
        near = {(0, step): to_member(feat_t, step) if step else feat_t for step in NEAR}
        held = {**relayed, **near}
        batch = [
            (step, ([(0, PASSED[step])] if step in PASSED else []) + list(relayed))
            for step in STEPS
        ]
        sent = list(pack(cubes, words, held, batch, True, 0))
        kept = keep(cubes, words, held)
        pairs = [[n, n ^ PAIRED] for n in range(nodes) if n < n ^ PAIRED]
        received = [
            exchange(one, pairs) if step == PAIRED else to_member(one, step)
            for one, (step, _) in zip(sent, batch)
        ]
        received.append(kept)
        rows, received[1] = lax.optimization_barrier((lists, received[1]))
        lists = make_lists(rows)
        messages = [(*one, False) for one in batch] + [(0, list(held), False)]
    local = aggregate(
        cubes, messages, not by_planes, lists, adj_tiles, received, feat_t.shape[1]
    )
    return lax.all_gather(local, "col", axis=0, tiled=True), lists


def dense_kernel(weight, aggregated, bias, out_ref):
    out_ref[...] = (
        jnp.dot(weight[...], aggregated[...], preferred_element_type=jnp.float32) + bias[...]
    )


def dense(weight, aggregated, bias):
    return pl.pallas_call(
        dense_kernel,
        out_shape=jax.ShapeDtypeStruct((weight.shape[0], aggregated.shape[1]), jnp.float32),
        in_specs=[VMEM] * 3,
        out_specs=VMEM,
        compiler_params=PARAMS,
        cost_estimate=pl.CostEstimate(
            flops=2 * weight.size * aggregated.shape[1],
            bytes_accessed=2 * (weight.size + 3 * aggregated.size),
            transcendentals=0,
        ),
    )(weight, aggregated, bias[:, None])


def body(x_t, adj_tiles, tile_rows, tile_cols, tile_counts, w_first, b_first, w_second, b_second):
    cubes = lax.axis_size("node") // GROUP
    plan = make_plan(tile_rows, tile_cols, tile_counts, cubes, x_t.shape[1] // BLK)
    y_first, lists = gather_sums(x_t, adj_tiles, (*plan, tile_rows), cubes, False)
    z_first = jnp.dot(w_first, y_first, preferred_element_type=jnp.float32) + b_first[:, None]
    h_first = jnp.maximum(z_first, 0.0).astype(jnp.bfloat16)
    y_second, _ = gather_sums(h_first, adj_tiles, (*plan, lists), cubes, True)
    return dense(w_second, y_second, b_second)


def solution(mesh):
    return jax.shard_map(
        body,
        mesh=mesh,
        in_specs=(
            P("col", "node"),
            P("node", None, None),
            P("node"),
            P("node"),
            P("node"),
            P("col", None),
            P("col"),
            P("col", None),
            P("col"),
        ),
        out_specs=P("col", "node"),
        check_vma=False,
    )
```

```python
import functools

import jax
import jax.numpy as jnp
from jax import lax
from jax.experimental import pallas as pl
from jax.experimental.pallas import tpu as pltpu
from jax.sharding import PartitionSpec as P

BLK = 128
CAP = 2
GROUP = 8
NEAR = (0, 4, 1, 2)
PASSED = {7: 0, 4: 1, 1: 2, 2: 4}
STEPS = (7, 6, 3, 4, 5, 1, 2)
DEPTH = 4
RELAY_WORK = 50_000_000_000
WIDTH = 4
SMEM = pl.BlockSpec(memory_space=pltpu.SMEM)
VMEM = pl.BlockSpec(memory_space=pltpu.VMEM)
HBM = pl.BlockSpec(memory_space=pltpu.HBM)
PARAMS = pltpu.CompilerParams(vmem_limit_bytes=24 * 1024 * 1024)


def split(value, size):
    shift = size.bit_length() - 1
    if size == 1 << shift:
        return value >> shift, value & (size - 1)
    return lax.div(value, size), lax.rem(value, size)


def lowest(mask):
    return jnp.where(mask & 1 != 0, 0, jnp.where(mask & 2 != 0, 1, jnp.where(mask & 4 != 0, 2, 3)))


def highest(mask):
    return jnp.where(mask & 8 != 0, 3, jnp.where(mask & 4 != 0, 2, jnp.where(mask & 2 != 0, 1, 0)))


def owner_mask(words, owner, row_blocks):
    first = owner * row_blocks
    word = words[0]
    for at in range(1, len(words)):
        word = jnp.where(first >> 5 == at, words[at], word)
    return (word >> (first & 31)) & ((1 << row_blocks) - 1)


def words_kernel(count_ref, cols_ref, words_ref):
    live = count_ref[0]
    word_total = words_ref.shape[1]

    def step(slot, found):
        column = cols_ref[slot]
        bit = jnp.where(slot < live, 1 << (column & 31), 0)
        word = column >> 5
        return tuple(one | jnp.where(word == at, bit, 0) for at, one in enumerate(found))

    start = tuple(jnp.int32(0) for _ in range(word_total))
    found = lax.fori_loop(0, cols_ref.shape[0], step, start, unroll=8)
    for member in range(GROUP):
        for at in range(word_total):
            words_ref[member, at] = found[at]


def group_limit(tile_total, row_blocks):
    return -(-(tile_total // DEPTH + row_blocks) // WIDTH) * WIDTH


def list_kernel(cubes, row_blocks, count_ref, rows_ref, cols_ref, words_ref, lists, filled):
    tile_total = cols_ref.shape[0]
    node = lax.axis_index("node")
    cube, member = split(node, GROUP)
    words = [words_ref[0, at] for at in range(words_ref.shape[1])]
    limit = group_limit(tile_total, row_blocks)

    @pl.loop(0, limit)
    def _(group):
        lists[1 + group] = row_blocks
        for at in range(DEPTH):
            entry = 1 + limit + 2 * (group * DEPTH + at)
            lists[entry] = 0
            lists[entry + 1] = cubes * GROUP * CAP

    for row in range(row_blocks):
        filled[row] = 0

    @pl.loop(0, count_ref[0])
    def _(slot):
        row = rows_ref[slot]
        filled[row] = filled[row] + 1

    start = 0
    for row in range(row_blocks):
        groups, _ = split(filled[row] + DEPTH - 1, DEPTH)
        filled[row] = start * DEPTH

        @pl.loop(start, start + groups)
        def _(group):
            lists[1 + group] = row

        start = start + groups
    lists[0] = start

    @pl.loop(0, count_ref[0])
    def _(slot):
        owner, block = split(cols_ref[slot], row_blocks)
        home, other = split(owner, GROUP)
        unit = jnp.where(home >= cube, home - cube, home - cube + cubes)
        second = block != lowest(owner_mask(words, owner, row_blocks))
        row = rows_ref[slot]
        entry = 1 + limit + 2 * filled[row]
        filled[row] = filled[row] + 1
        lists[entry] = slot
        lists[entry + 1] = (unit * GROUP + (other ^ member)) * CAP + jnp.where(second, 1, 0)


def make_plan(tile_rows, tile_cols, tile_counts, cubes, row_blocks):
    tile_total = tile_cols.shape[0]
    word_total = -(-cubes * GROUP * row_blocks // 32)
    list_length = 1 + group_limit(tile_total, row_blocks) * (1 + 2 * DEPTH)
    own = pl.pallas_call(
        words_kernel,
        out_shape=jax.ShapeDtypeStruct((GROUP, word_total), jnp.int32),
        in_specs=[SMEM] * 2,
        out_specs=SMEM,
    )(tile_counts, tile_cols)
    lists = pl.pallas_call(
        functools.partial(list_kernel, cubes, row_blocks),
        out_shape=jax.ShapeDtypeStruct((list_length,), jnp.int32),
        in_specs=[SMEM] * 4,
        out_specs=SMEM,
        scratch_shapes=[pltpu.SMEM((row_blocks,), jnp.int32)],
    )(tile_counts, tile_rows, tile_cols, own)
    groups = [[cube * GROUP + member for member in range(GROUP)] for cube in range(cubes)]
    words = exchange(own, groups)
    return words, lists


def exchange(array, groups):
    return lax.all_to_all(
        array, "node", split_axis=0, concat_axis=0, tiled=True, axis_index_groups=groups
    )


def named_blocks(words_ref, member, owner, row_blocks):
    words = [words_ref[member, at] for at in range(words_ref.shape[1])]
    mask = owner_mask(words, owner, row_blocks)
    return [pl.multiple_of(block * BLK, BLK) for block in (lowest(mask), highest(mask))]


def pack_kernel(cubes, whole, messages, fetched, words_ref, *refs):
    held, refs = dict(zip(whole, refs)), refs[len(whole) :]
    total = len(messages)
    sent, packed, done = refs[:total], refs[total : 2 * total], refs[2 * total]
    row_blocks = held[whole[0]].shape[1] // BLK
    node = lax.axis_index("node")
    cube, member = split(node, GROUP)

    def fill(target, other, unit, source):
        owner = split(cube + unit, cubes)[1] * GROUP + (member ^ source)
        for slot, lane in enumerate(named_blocks(words_ref, other, owner, row_blocks)):
            target[slot] = held[unit, source][:, pl.ds(lane, BLK)]

    if fetched:
        own, held[0, 0] = held[0, 0], refs[-1]
        fetch = pltpu.make_async_copy(own, held[0, 0], done.at[total])
        fetch.start()
    copies = []
    for at, (step, sources) in reversed(list(enumerate(messages))):
        for part, (unit, source) in reversed(list(enumerate(sources))):
            if fetched and (unit, source) == (0, 0):
                fetch.wait()
            fill(packed[at].at[part], member ^ step, unit, source)
        copies.append(pltpu.make_async_copy(packed[at], sent[at], done.at[at]))
        copies[-1].start()
    for copy in copies:
        copy.wait()


def pack(cubes, words, held, messages, fetched, work):
    feat_local, nodes_local = next(iter(held.values())).shape
    shapes = [(len(sources), CAP, feat_local, BLK) for _, sources in messages]
    scratch = [pltpu.VMEM(shape, jnp.bfloat16) for shape in shapes]
    scratch += [pltpu.SemaphoreType.DMA((len(shapes) + 1,))]
    if fetched:
        scratch += [pltpu.VMEM((feat_local, nodes_local), jnp.bfloat16)]
        held = {**held, (0, 0): in_hbm(held[0, 0])}
    return pl.pallas_call(
        functools.partial(pack_kernel, cubes, tuple(held), messages, fetched),
        out_shape=[pltpu.HBM(shape, jnp.bfloat16) for shape in shapes],
        in_specs=[SMEM] + [HBM if fetched and at == (0, 0) else VMEM for at in held],
        out_specs=[HBM] * len(shapes),
        scratch_shapes=scratch,
        compiler_params=PARAMS,
        cost_estimate=pl.CostEstimate(flops=work, bytes_accessed=0, transcendentals=0),
    )(words, *held.values())


def in_hbm(array):
    return pltpu.with_memory_space_constraint(array, pltpu.HBM)


def keep_kernel(cubes, whole, words_ref, *refs):
    held, kept = refs[:-1], refs[-1]
    row_blocks = held[0].shape[1] // BLK
    node = lax.axis_index("node")
    cube, member = split(node, GROUP)
    for at, (unit, source) in enumerate(whole):
        owner = split(cube + unit, cubes)[1] * GROUP + (member ^ source)
        for slot, lane in enumerate(named_blocks(words_ref, member, owner, row_blocks)):
            kept[at, slot] = held[at][:, pl.ds(lane, BLK)]


def keep(cubes, words, held):
    shape = (len(held), CAP, held[0, 0].shape[0], BLK)
    return pl.pallas_call(
        functools.partial(keep_kernel, cubes, tuple(held)),
        out_shape=jax.ShapeDtypeStruct(shape, jnp.bfloat16),
        in_specs=[SMEM] + [VMEM] * len(held),
        out_specs=VMEM,
        compiler_params=PARAMS,
    )(words, *held.values())


def aggregate_kernel(cubes, limit, messages, fetched, lists_hbm, tiles, *refs):
    received, refs = refs[: len(messages)], refs[len(messages) :]
    out_ref, lists, blocks, total, done = refs[:5]
    pairs = [(lists_hbm, lists)]
    if fetched:
        pairs.append((tiles, refs[5]))
        tiles = refs[5]
    for (step, sources, far), array in zip(messages, received):
        for part, (unit, source) in enumerate(sources if far else ()):
            place = (unit * GROUP + (step ^ source)) * CAP
            pairs.append((array.at[part], blocks.at[place : place + CAP]))
    copies = [pltpu.make_async_copy(*pair, done.at[at]) for at, pair in enumerate(pairs)]
    for copy in copies:
        copy.start()
    total[...] = jnp.zeros_like(total)
    blocks[cubes * GROUP * CAP] = jnp.zeros_like(blocks[cubes * GROUP * CAP])
    for (step, sources, far), array in zip(messages, received):
        for part, (unit, source) in enumerate(() if far else sources):
            place = (unit * GROUP + (step ^ source)) * CAP
            blocks[place : place + CAP] = array[part]
    for copy in copies:
        copy.wait()

    @pl.loop(0, split(lists[0] + WIDTH - 1, WIDTH)[0])
    def _(loop_step):
        sums = []
        for wide in range(WIDTH):
            group = loop_step * WIDTH + wide
            left, right = [], []
            for at in range(DEPTH):
                entry = 1 + limit + 2 * (group * DEPTH + at)
                left.append(blocks[lists[entry + 1]])
                right.append(tiles[lists[entry]])
            summed = lax.dot_general(
                jnp.concatenate(left, axis=1),
                jnp.concatenate(right, axis=1),
                (((1,), (1,)), ((), ())),
                preferred_element_type=jnp.float32,
            )
            sums.append((lists[1 + group], summed))
        for row, summed in sums:
            total[row] += summed

    for row in range(out_ref.shape[1] // BLK):
        out_ref[:, row * BLK : (row + 1) * BLK] = total[row].astype(out_ref.dtype)


def aggregate(cubes, messages, fetched, lists, adj_tiles, received, nodes_local):
    feat_local = received[0].shape[2]
    row_blocks = nodes_local // BLK
    limit = group_limit(adj_tiles.shape[0], row_blocks)
    operands = [in_hbm(adj_tiles) if fetched else adj_tiles]
    operands += [in_hbm(one) if far else one for one, (_, _, far) in zip(received, messages)]
    spaces = [HBM if fetched else VMEM] + [HBM if far else VMEM for _, _, far in messages]
    scratch = [
        pltpu.SMEM(lists.shape, jnp.int32),
        pltpu.VMEM((cubes * GROUP * CAP + 1, feat_local, BLK), jnp.bfloat16),
        pltpu.VMEM((row_blocks + 1, feat_local, BLK), jnp.float32),
        pltpu.SemaphoreType.DMA((2 + cubes * GROUP,)),
    ]
    if fetched:
        scratch.append(pltpu.VMEM(adj_tiles.shape, jnp.bfloat16))
    return pl.pallas_call(
        functools.partial(aggregate_kernel, cubes, limit, messages, fetched),
        out_shape=jax.ShapeDtypeStruct((feat_local, nodes_local), jnp.bfloat16),
        in_specs=[HBM] + spaces,
        out_specs=VMEM,
        scratch_shapes=scratch,
        compiler_params=PARAMS,
        cost_estimate=pl.CostEstimate(
            flops=2 * adj_tiles.shape[0] * feat_local * BLK * BLK,
            bytes_accessed=2 * sum(one.size for one in operands),
            transcendentals=0,
        ),
    )(in_hbm(lists), *operands)


def gather_sums(feat_t, adj_tiles, plan, cubes, by_planes):
    words, lists = plan
    nodes = cubes * GROUP

    def to_member(array, step):
        return lax.ppermute(array, "node", [(n, n ^ step) for n in range(nodes)])

    relayed = {
        (unit, 0): lax.ppermute(
            feat_t, "node", [(n, (n - unit * GROUP) % nodes) for n in range(nodes)]
        )
        for unit in range(1, cubes)
    }
    if by_planes:
        held = {(0, 0): feat_t, **relayed}
        held.update({(unit, 4): to_member(array, 4) for (unit, _), array in held.items()})
        batches = [
            ([(0, 0)], 0),
            ([(0, 4)] + list(relayed), RELAY_WORK),
            ([(unit, 4) for unit, _ in relayed], RELAY_WORK),
        ]
        messages, received = [], []
        for number, (sources, work) in enumerate(batches):
            batch = [(step, sources) for step in (3, 1, 2, 0)]
            array = {at: held[at] for at in sources}
            sent = pack(cubes, words, array, batch, False, work)
            for one, (step, _) in zip(sent, batch):
                far = number == 0 or step == 0 or (number, step) == (2, 2)
                messages.append((step, sources, far))
                received.append(to_member(one, step) if step else one)
    else:
        near = {(0, step): to_member(feat_t, step) if step else feat_t for step in NEAR}
        held = {**relayed, **near}
        batch = [
            (step, ([(0, PASSED[step])] if step in PASSED else []) + list(relayed))
            for step in STEPS
        ]
        sent = list(pack(cubes, words, held, batch, True, 0))
        kept = keep(cubes, words, held)
        sent[4], kept, lists = lax.optimization_barrier((sent[4], kept, lists))
        received = [to_member(one, step) for one, (step, _) in zip(sent, batch)]
        received.append(kept)
        messages = [(*one, False) for one in batch] + [(0, list(held), False)]
    local = aggregate(
        cubes, messages, not by_planes, lists, adj_tiles, received, feat_t.shape[1]
    )
    return lax.all_gather(local, "col", axis=0, tiled=True)


def dense_kernel(weight, aggregated, bias, out_ref):
    out_ref[...] = (
        jnp.dot(weight[...], aggregated[...], preferred_element_type=jnp.float32) + bias[...]
    )


def dense(weight, aggregated, bias):
    return pl.pallas_call(
        dense_kernel,
        out_shape=jax.ShapeDtypeStruct((weight.shape[0], aggregated.shape[1]), jnp.float32),
        in_specs=[VMEM] * 3,
        out_specs=VMEM,
        compiler_params=PARAMS,
        cost_estimate=pl.CostEstimate(
            flops=2 * weight.size * aggregated.shape[1],
            bytes_accessed=2 * (weight.size + 3 * aggregated.size),
            transcendentals=0,
        ),
    )(weight, aggregated, bias[:, None])


def body(x_t, adj_tiles, tile_rows, tile_cols, tile_counts, w_first, b_first, w_second, b_second):
    cubes = lax.axis_size("node") // GROUP
    plan = make_plan(tile_rows, tile_cols, tile_counts, cubes, x_t.shape[1] // BLK)
    y_first = gather_sums(x_t, adj_tiles, plan, cubes, False)
    z_first = jnp.dot(w_first, y_first, preferred_element_type=jnp.float32) + b_first[:, None]
    h_first = jnp.maximum(z_first, 0.0).astype(jnp.bfloat16)
    y_second = gather_sums(h_first, adj_tiles, plan, cubes, True)
    return dense(w_second, y_second, b_second)


def solution(mesh):
    return jax.shard_map(
        body,
        mesh=mesh,
        in_specs=(
            P("col", "node"),
            P("node", None, None),
            P("node"),
            P("node"),
            P("node"),
            P("col", None),
            P("col"),
            P("col", None),
            P("col"),
        ),
        out_specs=P("col", "node"),
        check_vma=False,
    )
```

```python
import functools

import jax
import jax.numpy as jnp
from jax import lax
from jax.experimental import pallas as pl
from jax.experimental.pallas import tpu as pltpu
from jax.sharding import PartitionSpec as P

BLK = 128
CAP = 2
GROUP = 8
NEAR = (0, 1, 2, 4)
PASSED = {7: 0, 4: 1, 1: 2, 2: 4}
STEPS = (7, 6, 3, 4, 5, 1, 2)
DEPTH = 4
RELAY_WORK = 50_000_000_000
WIDTH = 4
SMEM = pl.BlockSpec(memory_space=pltpu.SMEM)
VMEM = pl.BlockSpec(memory_space=pltpu.VMEM)
HBM = pl.BlockSpec(memory_space=pltpu.HBM)
PARAMS = pltpu.CompilerParams(vmem_limit_bytes=24 * 1024 * 1024)


def split(value, size):
    shift = size.bit_length() - 1
    if size == 1 << shift:
        return value >> shift, value & (size - 1)
    return lax.div(value, size), lax.rem(value, size)


def lowest(mask):
    return jnp.where(mask & 1 != 0, 0, jnp.where(mask & 2 != 0, 1, jnp.where(mask & 4 != 0, 2, 3)))


def highest(mask):
    return jnp.where(mask & 8 != 0, 3, jnp.where(mask & 4 != 0, 2, jnp.where(mask & 2 != 0, 1, 0)))


def owner_mask(words, owner, row_blocks):
    first = owner * row_blocks
    word = words[0]
    for at in range(1, len(words)):
        word = jnp.where(first >> 5 == at, words[at], word)
    return (word >> (first & 31)) & ((1 << row_blocks) - 1)


def words_kernel(count_ref, cols_ref, words_ref):
    live = count_ref[0]
    word_total = words_ref.shape[1]

    def step(slot, found):
        column = cols_ref[slot]
        bit = jnp.where(slot < live, 1 << (column & 31), 0)
        word = column >> 5
        return tuple(one | jnp.where(word == at, bit, 0) for at, one in enumerate(found))

    start = tuple(jnp.int32(0) for _ in range(word_total))
    found = lax.fori_loop(0, cols_ref.shape[0], step, start, unroll=8)
    for member in range(GROUP):
        for at in range(word_total):
            words_ref[member, at] = found[at]


def group_limit(tile_total, row_blocks):
    return -(-(tile_total // DEPTH + row_blocks) // WIDTH) * WIDTH


def list_kernel(cubes, row_blocks, count_ref, rows_ref, cols_ref, words_ref, lists, filled):
    tile_total = cols_ref.shape[0]
    node = lax.axis_index("node")
    cube, member = split(node, GROUP)
    words = [words_ref[0, at] for at in range(words_ref.shape[1])]
    limit = group_limit(tile_total, row_blocks)

    @pl.loop(0, limit)
    def _(group):
        lists[1 + group] = row_blocks
        for at in range(DEPTH):
            entry = 1 + limit + 2 * (group * DEPTH + at)
            lists[entry] = 0
            lists[entry + 1] = cubes * GROUP * CAP

    for row in range(row_blocks):
        filled[row] = 0

    @pl.loop(0, count_ref[0])
    def _(slot):
        row = rows_ref[slot]
        filled[row] = filled[row] + 1

    start = 0
    for row in range(row_blocks):
        groups, _ = split(filled[row] + DEPTH - 1, DEPTH)
        filled[row] = start * DEPTH

        @pl.loop(start, start + groups)
        def _(group):
            lists[1 + group] = row

        start = start + groups
    lists[0] = start

    @pl.loop(0, count_ref[0])
    def _(slot):
        owner, block = split(cols_ref[slot], row_blocks)
        home, other = split(owner, GROUP)
        unit = jnp.where(home >= cube, home - cube, home - cube + cubes)
        second = block != lowest(owner_mask(words, owner, row_blocks))
        row = rows_ref[slot]
        entry = 1 + limit + 2 * filled[row]
        filled[row] = filled[row] + 1
        lists[entry] = slot
        lists[entry + 1] = (unit * GROUP + (other ^ member)) * CAP + jnp.where(second, 1, 0)


def make_plan(tile_rows, tile_cols, tile_counts, cubes, row_blocks):
    tile_total = tile_cols.shape[0]
    word_total = -(-cubes * GROUP * row_blocks // 32)
    list_length = 1 + group_limit(tile_total, row_blocks) * (1 + 2 * DEPTH)
    own = pl.pallas_call(
        words_kernel,
        out_shape=jax.ShapeDtypeStruct((GROUP, word_total), jnp.int32),
        in_specs=[SMEM] * 2,
        out_specs=SMEM,
    )(tile_counts, tile_cols)
    lists = pl.pallas_call(
        functools.partial(list_kernel, cubes, row_blocks),
        out_shape=jax.ShapeDtypeStruct((list_length,), jnp.int32),
        in_specs=[SMEM] * 4,
        out_specs=SMEM,
        scratch_shapes=[pltpu.SMEM((row_blocks,), jnp.int32)],
    )(tile_counts, tile_rows, tile_cols, own)
    groups = [[cube * GROUP + member for member in range(GROUP)] for cube in range(cubes)]
    words = exchange(own, groups)
    return words, lists


def exchange(array, groups):
    return lax.all_to_all(
        array, "node", split_axis=0, concat_axis=0, tiled=True, axis_index_groups=groups
    )


def named_blocks(words_ref, member, owner, row_blocks):
    words = [words_ref[member, at] for at in range(words_ref.shape[1])]
    mask = owner_mask(words, owner, row_blocks)
    return [pl.multiple_of(block * BLK, BLK) for block in (lowest(mask), highest(mask))]


def pack_kernel(cubes, whole, messages, fetched, words_ref, *refs):
    held, refs = dict(zip(whole, refs)), refs[len(whole) :]
    total = len(messages)
    sent, packed, done = refs[:total], refs[total : 2 * total], refs[2 * total]
    row_blocks = held[whole[0]].shape[1] // BLK
    node = lax.axis_index("node")
    cube, member = split(node, GROUP)

    def fill(target, other, unit, source):
        owner = split(cube + unit, cubes)[1] * GROUP + (member ^ source)
        for slot, lane in enumerate(named_blocks(words_ref, other, owner, row_blocks)):
            target[slot] = held[unit, source][:, pl.ds(lane, BLK)]

    if fetched:
        own, held[0, 0] = held[0, 0], refs[-1]
        fetch = pltpu.make_async_copy(own, held[0, 0], done.at[total])
        fetch.start()
    copies = []
    for at, (step, sources) in reversed(list(enumerate(messages))):
        for part, (unit, source) in reversed(list(enumerate(sources))):
            if fetched and (unit, source) == (0, 0):
                fetch.wait()
            fill(packed[at].at[part], member ^ step, unit, source)
        copies.append(pltpu.make_async_copy(packed[at], sent[at], done.at[at]))
        copies[-1].start()
    for copy in copies:
        copy.wait()


def pack(cubes, words, held, messages, fetched, work):
    feat_local, nodes_local = next(iter(held.values())).shape
    shapes = [(len(sources), CAP, feat_local, BLK) for _, sources in messages]
    scratch = [pltpu.VMEM(shape, jnp.bfloat16) for shape in shapes]
    scratch += [pltpu.SemaphoreType.DMA((len(shapes) + 1,))]
    if fetched:
        scratch += [pltpu.VMEM((feat_local, nodes_local), jnp.bfloat16)]
        held = {**held, (0, 0): in_hbm(held[0, 0])}
    return pl.pallas_call(
        functools.partial(pack_kernel, cubes, tuple(held), messages, fetched),
        out_shape=[pltpu.HBM(shape, jnp.bfloat16) for shape in shapes],
        in_specs=[SMEM] + [HBM if fetched and at == (0, 0) else VMEM for at in held],
        out_specs=[HBM] * len(shapes),
        scratch_shapes=scratch,
        compiler_params=PARAMS,
        cost_estimate=pl.CostEstimate(flops=work, bytes_accessed=0, transcendentals=0),
    )(words, *held.values())


def in_hbm(array):
    return pltpu.with_memory_space_constraint(array, pltpu.HBM)


def keep_kernel(cubes, whole, words_ref, *refs):
    held, kept = refs[:-1], refs[-1]
    row_blocks = held[0].shape[1] // BLK
    node = lax.axis_index("node")
    cube, member = split(node, GROUP)
    for at, (unit, source) in enumerate(whole):
        owner = split(cube + unit, cubes)[1] * GROUP + (member ^ source)
        for slot, lane in enumerate(named_blocks(words_ref, member, owner, row_blocks)):
            kept[at, slot] = held[at][:, pl.ds(lane, BLK)]


def keep(cubes, words, held):
    shape = (len(held), CAP, held[0, 0].shape[0], BLK)
    return pl.pallas_call(
        functools.partial(keep_kernel, cubes, tuple(held)),
        out_shape=jax.ShapeDtypeStruct(shape, jnp.bfloat16),
        in_specs=[SMEM] + [VMEM] * len(held),
        out_specs=VMEM,
        compiler_params=PARAMS,
    )(words, *held.values())


def aggregate_kernel(cubes, limit, messages, fetched, lists_hbm, tiles, *refs):
    received, refs = refs[: len(messages)], refs[len(messages) :]
    out_ref, lists, blocks, total, done = refs[:5]
    pairs = [(lists_hbm, lists)]
    if fetched:
        pairs.append((tiles, refs[5]))
        tiles = refs[5]
    for (step, sources, far), array in zip(messages, received):
        for part, (unit, source) in enumerate(sources if far else ()):
            place = (unit * GROUP + (step ^ source)) * CAP
            pairs.append((array.at[part], blocks.at[place : place + CAP]))
    copies = [pltpu.make_async_copy(*pair, done.at[at]) for at, pair in enumerate(pairs)]
    for copy in copies:
        copy.start()
    total[...] = jnp.zeros_like(total)
    blocks[cubes * GROUP * CAP] = jnp.zeros_like(blocks[cubes * GROUP * CAP])
    for (step, sources, far), array in zip(messages, received):
        for part, (unit, source) in enumerate(() if far else sources):
            place = (unit * GROUP + (step ^ source)) * CAP
            blocks[place : place + CAP] = array[part]
    for copy in copies:
        copy.wait()

    @pl.loop(0, split(lists[0] + WIDTH - 1, WIDTH)[0])
    def _(loop_step):
        sums = []
        for wide in range(WIDTH):
            group = loop_step * WIDTH + wide
            named, values = [], []
            for at in range(DEPTH):
                entry = 1 + limit + 2 * (group * DEPTH + at)
                named.append(blocks[lists[entry + 1]])
                values.append(tiles[lists[entry]])
            summed = lax.dot_general(
                jnp.concatenate(values, axis=1),
                jnp.concatenate(named, axis=1),
                (((1,), (1,)), ((), ())),
                preferred_element_type=jnp.float32,
            )
            sums.append((lists[1 + group], summed))
        for row, summed in sums:
            total[row] += summed

    for row in range(out_ref.shape[1] // BLK):
        out_ref[:, row * BLK : (row + 1) * BLK] = total[row].T.astype(out_ref.dtype)


def aggregate(cubes, messages, fetched, lists, adj_tiles, received, nodes_local):
    feat_local = received[0].shape[2]
    row_blocks = nodes_local // BLK
    limit = group_limit(adj_tiles.shape[0], row_blocks)
    operands = [in_hbm(adj_tiles) if fetched else adj_tiles]
    operands += [in_hbm(one) if far else one for one, (_, _, far) in zip(received, messages)]
    spaces = [HBM if fetched else VMEM] + [HBM if far else VMEM for _, _, far in messages]
    scratch = [
        pltpu.SMEM(lists.shape, jnp.int32),
        pltpu.VMEM((cubes * GROUP * CAP + 1, feat_local, BLK), jnp.bfloat16),
        pltpu.VMEM((row_blocks + 1, BLK, feat_local), jnp.float32),
        pltpu.SemaphoreType.DMA((2 + cubes * GROUP,)),
    ]
    if fetched:
        scratch.append(pltpu.VMEM(adj_tiles.shape, jnp.bfloat16))
    return pl.pallas_call(
        functools.partial(aggregate_kernel, cubes, limit, messages, fetched),
        out_shape=jax.ShapeDtypeStruct((feat_local, nodes_local), jnp.bfloat16),
        in_specs=[HBM] + spaces,
        out_specs=VMEM,
        scratch_shapes=scratch,
        compiler_params=PARAMS,
        cost_estimate=pl.CostEstimate(
            flops=2 * adj_tiles.shape[0] * feat_local * BLK * BLK,
            bytes_accessed=2 * sum(one.size for one in operands),
            transcendentals=0,
        ),
    )(in_hbm(lists), *operands)


def gather_sums(feat_t, adj_tiles, plan, cubes, by_planes):
    words, lists = plan
    nodes = cubes * GROUP

    def to_member(array, step):
        return lax.ppermute(array, "node", [(n, n ^ step) for n in range(nodes)])

    relayed = {
        (unit, 0): lax.ppermute(
            feat_t, "node", [(n, (n - unit * GROUP) % nodes) for n in range(nodes)]
        )
        for unit in range(1, cubes)
    }
    if by_planes:
        held = {(0, 0): feat_t, **relayed}
        held.update({(unit, 4): to_member(array, 4) for (unit, _), array in held.items()})
        batches = [
            ([(0, 0)], 0),
            ([(0, 4)] + list(relayed), RELAY_WORK),
            ([(unit, 4) for unit, _ in relayed], RELAY_WORK),
        ]
        messages, received = [], []
        for number, (sources, work) in enumerate(batches):
            batch = [(step, sources) for step in (3, 1, 2, 0)]
            array = {at: held[at] for at in sources}
            sent = pack(cubes, words, array, batch, False, work)
            for one, (step, _) in zip(sent, batch):
                far = number == 0 or step == 0 or (number, step) == (2, 2)
                messages.append((step, sources, far))
                received.append(to_member(one, step) if step else one)
    else:
        near = {(0, step): to_member(feat_t, step) if step else feat_t for step in NEAR}
        held = {**relayed, **near}
        batch = [
            (step, ([(0, PASSED[step])] if step in PASSED else []) + list(relayed))
            for step in STEPS
        ]
        sent = list(pack(cubes, words, held, batch, True, 0))
        kept = keep(cubes, words, held)
        sent[4], kept, lists = lax.optimization_barrier((sent[4], kept, lists))
        received = [to_member(one, step) for one, (step, _) in zip(sent, batch)]
        received.append(kept)
        messages = [(*one, False) for one in batch] + [(0, list(held), False)]
    local = aggregate(
        cubes, messages, not by_planes, lists, adj_tiles, received, feat_t.shape[1]
    )
    return lax.all_gather(local, "col", axis=0, tiled=True)


def dense_kernel(weight, aggregated, bias, out_ref):
    out_ref[...] = (
        jnp.dot(weight[...], aggregated[...], preferred_element_type=jnp.float32) + bias[...]
    )


def dense(weight, aggregated, bias):
    return pl.pallas_call(
        dense_kernel,
        out_shape=jax.ShapeDtypeStruct((weight.shape[0], aggregated.shape[1]), jnp.float32),
        in_specs=[VMEM] * 3,
        out_specs=VMEM,
        compiler_params=PARAMS,
        cost_estimate=pl.CostEstimate(
            flops=2 * weight.size * aggregated.shape[1],
            bytes_accessed=2 * (weight.size + 3 * aggregated.size),
            transcendentals=0,
        ),
    )(weight, aggregated, bias[:, None])


def body(x_t, adj_tiles, tile_rows, tile_cols, tile_counts, w_first, b_first, w_second, b_second):
    cubes = lax.axis_size("node") // GROUP
    plan = make_plan(tile_rows, tile_cols, tile_counts, cubes, x_t.shape[1] // BLK)
    y_first = gather_sums(x_t, adj_tiles, plan, cubes, False)
    z_first = jnp.dot(w_first, y_first, preferred_element_type=jnp.float32) + b_first[:, None]
    h_first = jnp.maximum(z_first, 0.0).astype(jnp.bfloat16)
    y_second = gather_sums(h_first, adj_tiles, plan, cubes, True)
    return dense(w_second, y_second, b_second)


def solution(mesh):
    return jax.shard_map(
        body,
        mesh=mesh,
        in_specs=(
            P("col", "node"),
            P("node", None, None),
            P("node"),
            P("node"),
            P("node"),
            P("col", None),
            P("col"),
            P("col", None),
            P("col"),
        ),
        out_specs=P("col", "node"),
        check_vma=False,
    )
```

```python
import functools

import jax
import jax.numpy as jnp
from jax import lax
from jax.experimental import pallas as pl
from jax.experimental.pallas import tpu as pltpu
from jax.sharding import PartitionSpec as P

BLK = 128
CAP = 2
GROUP = 8
PLANE = 4
NEAR = (0, 1, 2, 4)
PASSED = {7: 0, 4: 1, 1: 2, 2: 4}
STEPS = (7, 6, 3, 4, 5, 1, 2)
DEPTH = 4
RELAY_WORK = 50_000_000_000
WIDTH = 4
SMEM = pl.BlockSpec(memory_space=pltpu.SMEM)
VMEM = pl.BlockSpec(memory_space=pltpu.VMEM)
HBM = pl.BlockSpec(memory_space=pltpu.HBM)
PARAMS = pltpu.CompilerParams(vmem_limit_bytes=24 * 1024 * 1024)


def split(value, size):
    shift = size.bit_length() - 1
    if size == 1 << shift:
        return value >> shift, value & (size - 1)
    return lax.div(value, size), lax.rem(value, size)


def lowest(mask):
    return jnp.where(mask & 1 != 0, 0, jnp.where(mask & 2 != 0, 1, jnp.where(mask & 4 != 0, 2, 3)))


def highest(mask):
    return jnp.where(mask & 8 != 0, 3, jnp.where(mask & 4 != 0, 2, jnp.where(mask & 2 != 0, 1, 0)))


def owner_mask(words, owner, row_blocks):
    first = owner * row_blocks
    word = words[0]
    for at in range(1, len(words)):
        word = jnp.where(first >> 5 == at, words[at], word)
    return (word >> (first & 31)) & ((1 << row_blocks) - 1)


def words_kernel(count_ref, cols_ref, words_ref):
    live = count_ref[0]
    word_total = words_ref.shape[1]

    def step(slot, found):
        column = cols_ref[slot]
        bit = jnp.where(slot < live, 1 << (column & 31), 0)
        word = column >> 5
        return tuple(one | jnp.where(word == at, bit, 0) for at, one in enumerate(found))

    start = tuple(jnp.int32(0) for _ in range(word_total))
    found = lax.fori_loop(0, cols_ref.shape[0], step, start, unroll=8)
    for member in range(GROUP):
        for at in range(word_total):
            words_ref[member, at] = found[at]


def group_limit(tile_total, row_blocks):
    return -(-(tile_total // DEPTH + row_blocks) // WIDTH) * WIDTH


def list_kernel(cubes, row_blocks, count_ref, rows_ref, cols_ref, words_ref, lists, filled):
    tile_total = cols_ref.shape[0]
    node = lax.axis_index("node")
    cube, member = split(node, GROUP)
    words = [words_ref[0, at] for at in range(words_ref.shape[1])]
    limit = group_limit(tile_total, row_blocks)

    @pl.loop(0, limit)
    def _(group):
        lists[1 + group] = row_blocks
        for at in range(DEPTH):
            entry = 1 + limit + 2 * (group * DEPTH + at)
            lists[entry] = 0
            lists[entry + 1] = cubes * GROUP * CAP

    for row in range(row_blocks):
        filled[row] = 0

    @pl.loop(0, count_ref[0])
    def _(slot):
        row = rows_ref[slot]
        filled[row] = filled[row] + 1

    start = 0
    for row in range(row_blocks):
        groups, _ = split(filled[row] + DEPTH - 1, DEPTH)
        filled[row] = start * DEPTH

        @pl.loop(start, start + groups)
        def _(group):
            lists[1 + group] = row

        start = start + groups
    lists[0] = start

    @pl.loop(0, count_ref[0])
    def _(slot):
        owner, block = split(cols_ref[slot], row_blocks)
        home, other = split(owner, GROUP)
        unit = jnp.where(home >= cube, home - cube, home - cube + cubes)
        second = block != lowest(owner_mask(words, owner, row_blocks))
        row = rows_ref[slot]
        entry = 1 + limit + 2 * filled[row]
        filled[row] = filled[row] + 1
        lists[entry] = slot
        lists[entry + 1] = (unit * GROUP + (other ^ member)) * CAP + jnp.where(second, 1, 0)


def make_plan(tile_rows, tile_cols, tile_counts, cubes, row_blocks):
    tile_total = tile_cols.shape[0]
    word_total = -(-cubes * GROUP * row_blocks // 32)
    list_length = 1 + group_limit(tile_total, row_blocks) * (1 + 2 * DEPTH)
    own = pl.pallas_call(
        words_kernel,
        out_shape=jax.ShapeDtypeStruct((GROUP, word_total), jnp.int32),
        in_specs=[SMEM] * 2,
        out_specs=SMEM,
    )(tile_counts, tile_cols)
    lists = pl.pallas_call(
        functools.partial(list_kernel, cubes, row_blocks),
        out_shape=jax.ShapeDtypeStruct((list_length,), jnp.int32),
        in_specs=[SMEM] * 4,
        out_specs=SMEM,
        scratch_shapes=[pltpu.SMEM((row_blocks,), jnp.int32)],
    )(tile_counts, tile_rows, tile_cols, own)
    groups = [[cube * GROUP + member for member in range(GROUP)] for cube in range(cubes)]
    words = exchange(own, groups)
    return words, lists


def exchange(array, groups):
    return lax.all_to_all(
        array, "node", split_axis=0, concat_axis=0, tiled=True, axis_index_groups=groups
    )


def named_blocks(words_ref, member, owner, row_blocks):
    words = [words_ref[member, at] for at in range(words_ref.shape[1])]
    mask = owner_mask(words, owner, row_blocks)
    return [pl.multiple_of(block * BLK, BLK) for block in (lowest(mask), highest(mask))]


def pack_kernel(cubes, whole, messages, fetched, words_ref, *refs):
    held, refs = dict(zip(whole, refs)), refs[len(whole) :]
    total = len(messages)
    sent, packed, done = refs[:total], refs[total : 2 * total], refs[2 * total]
    row_blocks = held[whole[0]].shape[1] // BLK
    node = lax.axis_index("node")
    cube, member = split(node, GROUP)

    def fill(target, other, unit, source):
        owner = split(cube + unit, cubes)[1] * GROUP + (member ^ source)
        for slot, lane in enumerate(named_blocks(words_ref, other, owner, row_blocks)):
            target[slot] = held[unit, source][:, pl.ds(lane, BLK)]

    if fetched:
        own, held[0, 0] = held[0, 0], refs[-1]
        fetch = pltpu.make_async_copy(own, held[0, 0], done.at[total])
        fetch.start()
    copies = []
    for at, (step, sources) in reversed(list(enumerate(messages))):
        if step is None:
            for other in range(PLANE):
                for part, (unit, source) in enumerate(sources):
                    target = packed[at].at[other, part]
                    fill(target, (member & -PLANE) + other, unit, source)
        for part, (unit, source) in () if step is None else reversed(list(enumerate(sources))):
            if fetched and (unit, source) == (0, 0):
                fetch.wait()
            fill(packed[at].at[part], member ^ step, unit, source)
        copies.append(pltpu.make_async_copy(packed[at], sent[at], done.at[at]))
        copies[-1].start()
    for copy in copies:
        copy.wait()


def pack(cubes, words, held, messages, fetched, work):
    feat_local, nodes_local = next(iter(held.values())).shape
    shapes = [
        (() if step is not None else (PLANE,)) + (len(sources), CAP, feat_local, BLK)
        for step, sources in messages
    ]
    scratch = [pltpu.VMEM(shape, jnp.bfloat16) for shape in shapes]
    scratch += [pltpu.SemaphoreType.DMA((len(shapes) + 1,))]
    if fetched:
        scratch += [pltpu.VMEM((feat_local, nodes_local), jnp.bfloat16)]
        held = {**held, (0, 0): in_hbm(held[0, 0])}
    return pl.pallas_call(
        functools.partial(pack_kernel, cubes, tuple(held), messages, fetched),
        out_shape=[pltpu.HBM(shape, jnp.bfloat16) for shape in shapes],
        in_specs=[SMEM] + [HBM if fetched and at == (0, 0) else VMEM for at in held],
        out_specs=[HBM] * len(shapes),
        scratch_shapes=scratch,
        compiler_params=PARAMS,
        cost_estimate=pl.CostEstimate(flops=work, bytes_accessed=0, transcendentals=0),
    )(words, *held.values())


def in_hbm(array):
    return pltpu.with_memory_space_constraint(array, pltpu.HBM)


def keep_kernel(cubes, whole, words_ref, *refs):
    held, kept = refs[:-1], refs[-1]
    row_blocks = held[0].shape[1] // BLK
    node = lax.axis_index("node")
    cube, member = split(node, GROUP)
    for at, (unit, source) in enumerate(whole):
        owner = split(cube + unit, cubes)[1] * GROUP + (member ^ source)
        for slot, lane in enumerate(named_blocks(words_ref, member, owner, row_blocks)):
            kept[at, slot] = held[at][:, pl.ds(lane, BLK)]


def keep(cubes, words, held):
    shape = (len(held), CAP, held[0, 0].shape[0], BLK)
    return pl.pallas_call(
        functools.partial(keep_kernel, cubes, tuple(held)),
        out_shape=jax.ShapeDtypeStruct(shape, jnp.bfloat16),
        in_specs=[SMEM] + [VMEM] * len(held),
        out_specs=VMEM,
        compiler_params=PARAMS,
    )(words, *held.values())


def aggregate_kernel(cubes, limit, messages, fetched, lists_hbm, tiles, *refs):
    received, refs = refs[: len(messages)], refs[len(messages) :]
    out_ref, lists, blocks, total, done = refs[:5]
    pairs = [(lists_hbm, lists)]
    if fetched:
        pairs.append((tiles, refs[5]))
        tiles = refs[5]
    corner = lax.axis_index("node") & (PLANE - 1)
    for (step, sources, far), array in zip(messages, received):
        for part, (unit, source) in enumerate(sources if far else ()):
            if step is None:
                for other in range(PLANE):
                    place = (unit * GROUP + source + (other ^ corner)) * CAP
                    pairs.append((array.at[other, part], blocks.at[pl.ds(place, CAP)]))
                continue
            place = (unit * GROUP + (step ^ source)) * CAP
            pairs.append((array.at[part], blocks.at[place : place + CAP]))
    copies = [pltpu.make_async_copy(*pair, done.at[at]) for at, pair in enumerate(pairs)]
    for copy in copies:
        copy.start()
    total[...] = jnp.zeros_like(total)
    blocks[cubes * GROUP * CAP] = jnp.zeros_like(blocks[cubes * GROUP * CAP])
    for (step, sources, far), array in zip(messages, received):
        for part, (unit, source) in enumerate(() if far else sources):
            place = (unit * GROUP + (step ^ source)) * CAP
            blocks[place : place + CAP] = array[part]
    for copy in copies:
        copy.wait()

    @pl.loop(0, split(lists[0] + WIDTH - 1, WIDTH)[0])
    def _(loop_step):
        sums = []
        for wide in range(WIDTH):
            group = loop_step * WIDTH + wide
            left, right = [], []
            for at in range(DEPTH):
                entry = 1 + limit + 2 * (group * DEPTH + at)
                left.append(blocks[lists[entry + 1]])
                right.append(tiles[lists[entry]])
            summed = lax.dot_general(
                jnp.concatenate(left, axis=1),
                jnp.concatenate(right, axis=1),
                (((1,), (1,)), ((), ())),
                preferred_element_type=jnp.float32,
            )
            sums.append((lists[1 + group], summed))
        for row, summed in sums:
            total[row] += summed

    for row in range(out_ref.shape[1] // BLK):
        out_ref[:, row * BLK : (row + 1) * BLK] = total[row].astype(out_ref.dtype)


def aggregate(cubes, messages, fetched, lists, adj_tiles, received, nodes_local):
    feat_local = received[0].shape[-2]
    row_blocks = nodes_local // BLK
    limit = group_limit(adj_tiles.shape[0], row_blocks)
    operands = [in_hbm(adj_tiles) if fetched else adj_tiles]
    operands += [in_hbm(one) if far else one for one, (_, _, far) in zip(received, messages)]
    spaces = [HBM if fetched else VMEM] + [HBM if far else VMEM for _, _, far in messages]
    scratch = [
        pltpu.SMEM(lists.shape, jnp.int32),
        pltpu.VMEM((cubes * GROUP * CAP + 1, feat_local, BLK), jnp.bfloat16),
        pltpu.VMEM((row_blocks + 1, feat_local, BLK), jnp.float32),
        pltpu.SemaphoreType.DMA((2 + cubes * GROUP,)),
    ]
    if fetched:
        scratch.append(pltpu.VMEM(adj_tiles.shape, jnp.bfloat16))
    return pl.pallas_call(
        functools.partial(aggregate_kernel, cubes, limit, messages, fetched),
        out_shape=jax.ShapeDtypeStruct((feat_local, nodes_local), jnp.bfloat16),
        in_specs=[HBM] + spaces,
        out_specs=VMEM,
        scratch_shapes=scratch,
        compiler_params=PARAMS,
        cost_estimate=pl.CostEstimate(
            flops=2 * adj_tiles.shape[0] * feat_local * BLK * BLK,
            bytes_accessed=2 * sum(one.size for one in operands),
            transcendentals=0,
        ),
    )(in_hbm(lists), *operands)


def gather_sums(feat_t, adj_tiles, plan, cubes, by_planes):
    words, lists = plan
    nodes = cubes * GROUP

    def to_member(array, step):
        return lax.ppermute(array, "node", [(n, n ^ step) for n in range(nodes)])

    relayed = {
        (unit, 0): lax.ppermute(
            feat_t, "node", [(n, (n - unit * GROUP) % nodes) for n in range(nodes)]
        )
        for unit in range(1, cubes)
    }
    if by_planes:
        held = {(0, 0): feat_t, **relayed}
        held.update({(unit, 4): to_member(array, 4) for (unit, _), array in held.items()})
        batches = [
            (list(relayed) + [(0, 4)], RELAY_WORK),
            ([(unit, 4) for unit, _ in relayed], RELAY_WORK),
        ]
        planes = [list(range(first, first + PLANE)) for first in range(0, nodes, PLANE)]
        own = [(None, [(0, 0)])]
        sent = pack(cubes, words, {(0, 0): feat_t}, own, False, 0)
        messages, received = [(*own[0], True)], [exchange(sent[0], planes)]
        for number, (sources, work) in enumerate(batches):
            batch = [(step, sources) for step in (3, 1, 2, 0)]
            array = {at: held[at] for at in sources}
            if number == 0:
                array, received[0] = lax.optimization_barrier((array, received[0]))
            sent = pack(cubes, words, array, batch, False, work)
            for one, (step, _) in zip(sent, batch):
                far = step == 0 or (number, step) == (1, 2)
                messages.append((step, sources, far))
                received.append(to_member(one, step) if step else one)
    else:
        near = {(0, step): to_member(feat_t, step) if step else feat_t for step in NEAR}
        held = {**relayed, **near}
        batch = [
            (step, ([(0, PASSED[step])] if step in PASSED else []) + list(relayed))
            for step in STEPS
        ]
        sent = list(pack(cubes, words, held, batch, True, 0))
        kept = keep(cubes, words, held)
        sent[4], kept, lists = lax.optimization_barrier((sent[4], kept, lists))
        received = [to_member(one, step) for one, (step, _) in zip(sent, batch)]
        received.append(kept)
        messages = [(*one, False) for one in batch] + [(0, list(held), False)]
    local = aggregate(
        cubes, messages, not by_planes, lists, adj_tiles, received, feat_t.shape[1]
    )
    return lax.all_gather(local, "col", axis=0, tiled=True)


def dense_kernel(weight, aggregated, bias, out_ref):
    out_ref[...] = (
        jnp.dot(weight[...], aggregated[...], preferred_element_type=jnp.float32) + bias[...]
    )


def dense(weight, aggregated, bias):
    return pl.pallas_call(
        dense_kernel,
        out_shape=jax.ShapeDtypeStruct((weight.shape[0], aggregated.shape[1]), jnp.float32),
        in_specs=[VMEM] * 3,
        out_specs=VMEM,
        compiler_params=PARAMS,
        cost_estimate=pl.CostEstimate(
            flops=2 * weight.size * aggregated.shape[1],
            bytes_accessed=2 * (weight.size + 3 * aggregated.size),
            transcendentals=0,
        ),
    )(weight, aggregated, bias[:, None])


def body(x_t, adj_tiles, tile_rows, tile_cols, tile_counts, w_first, b_first, w_second, b_second):
    cubes = lax.axis_size("node") // GROUP
    plan = make_plan(tile_rows, tile_cols, tile_counts, cubes, x_t.shape[1] // BLK)
    y_first = gather_sums(x_t, adj_tiles, plan, cubes, False)
    z_first = jnp.dot(w_first, y_first, preferred_element_type=jnp.float32) + b_first[:, None]
    h_first = jnp.maximum(z_first, 0.0).astype(jnp.bfloat16)
    y_second = gather_sums(h_first, adj_tiles, plan, cubes, True)
    return dense(w_second, y_second, b_second)


def solution(mesh):
    return jax.shard_map(
        body,
        mesh=mesh,
        in_specs=(
            P("col", "node"),
            P("node", None, None),
            P("node"),
            P("node"),
            P("node"),
            P("col", None),
            P("col"),
            P("col", None),
            P("col"),
        ),
        out_specs=P("col", "node"),
        check_vma=False,
    )
```

```python
import functools

import jax
import jax.numpy as jnp
from jax import lax
from jax.experimental import pallas as pl
from jax.experimental.pallas import tpu as pltpu
from jax.sharding import PartitionSpec as P

BLK = 128
CAP = 2
GROUP = 8
NEAR = (0, 1, 2, 4)
PASSED = {7: 0, 4: 1, 1: 2, 2: 4}
STEPS = (7, 6, 5, 4, 3, 1, 2)
DEPTH = 4
RELAY_WORK = 50_000_000_000
WIDTH = 4
SMEM = pl.BlockSpec(memory_space=pltpu.SMEM)
VMEM = pl.BlockSpec(memory_space=pltpu.VMEM)
HBM = pl.BlockSpec(memory_space=pltpu.HBM)
PARAMS = pltpu.CompilerParams(vmem_limit_bytes=24 * 1024 * 1024)


def split(value, size):
    shift = size.bit_length() - 1
    if size == 1 << shift:
        return value >> shift, value & (size - 1)
    return lax.div(value, size), lax.rem(value, size)


def lowest(mask):
    return jnp.where(mask & 1 != 0, 0, jnp.where(mask & 2 != 0, 1, jnp.where(mask & 4 != 0, 2, 3)))


def highest(mask):
    return jnp.where(mask & 8 != 0, 3, jnp.where(mask & 4 != 0, 2, jnp.where(mask & 2 != 0, 1, 0)))


def owner_mask(words, owner, row_blocks):
    first = owner * row_blocks
    word = words[0]
    for at in range(1, len(words)):
        word = jnp.where(first >> 5 == at, words[at], word)
    return (word >> (first & 31)) & ((1 << row_blocks) - 1)


def words_kernel(count_ref, cols_ref, words_ref):
    live = count_ref[0]
    word_total = words_ref.shape[1]

    def step(slot, found):
        column = cols_ref[slot]
        bit = jnp.where(slot < live, 1 << (column & 31), 0)
        word = column >> 5
        return tuple(one | jnp.where(word == at, bit, 0) for at, one in enumerate(found))

    start = tuple(jnp.int32(0) for _ in range(word_total))
    found = lax.fori_loop(0, cols_ref.shape[0], step, start, unroll=8)
    for member in range(GROUP):
        for at in range(word_total):
            words_ref[member, at] = found[at]


def group_limit(tile_total, row_blocks):
    return -(-(tile_total // DEPTH + row_blocks) // WIDTH) * WIDTH


def list_kernel(cubes, row_blocks, count_ref, rows_ref, cols_ref, words_ref, lists, filled):
    tile_total = cols_ref.shape[0]
    node = lax.axis_index("node")
    cube, member = split(node, GROUP)
    words = [words_ref[0, at] for at in range(words_ref.shape[1])]
    limit = group_limit(tile_total, row_blocks)

    @pl.loop(0, limit)
    def _(group):
        lists[1 + group] = row_blocks
        for at in range(DEPTH):
            entry = 1 + limit + 2 * (group * DEPTH + at)
            lists[entry] = 0
            lists[entry + 1] = cubes * GROUP * CAP

    for row in range(row_blocks):
        filled[row] = 0

    @pl.loop(0, count_ref[0])
    def _(slot):
        row = rows_ref[slot]
        filled[row] = filled[row] + 1

    start = 0
    for row in range(row_blocks):
        groups, _ = split(filled[row] + DEPTH - 1, DEPTH)
        filled[row] = start * DEPTH

        @pl.loop(start, start + groups)
        def _(group):
            lists[1 + group] = row

        start = start + groups
    lists[0] = start

    @pl.loop(0, count_ref[0])
    def _(slot):
        owner, block = split(cols_ref[slot], row_blocks)
        home, other = split(owner, GROUP)
        unit = jnp.where(home >= cube, home - cube, home - cube + cubes)
        second = block != lowest(owner_mask(words, owner, row_blocks))
        row = rows_ref[slot]
        entry = 1 + limit + 2 * filled[row]
        filled[row] = filled[row] + 1
        lists[entry] = slot
        lists[entry + 1] = (unit * GROUP + (other ^ member)) * CAP + jnp.where(second, 1, 0)


def make_plan(tile_rows, tile_cols, tile_counts, cubes, row_blocks):
    tile_total = tile_cols.shape[0]
    word_total = -(-cubes * GROUP * row_blocks // 32)
    list_length = 1 + group_limit(tile_total, row_blocks) * (1 + 2 * DEPTH)
    own = pl.pallas_call(
        words_kernel,
        out_shape=jax.ShapeDtypeStruct((GROUP, word_total), jnp.int32),
        in_specs=[SMEM] * 2,
        out_specs=SMEM,
    )(tile_counts, tile_cols)
    lists = pl.pallas_call(
        functools.partial(list_kernel, cubes, row_blocks),
        out_shape=jax.ShapeDtypeStruct((list_length,), jnp.int32),
        in_specs=[SMEM] * 4,
        out_specs=SMEM,
        scratch_shapes=[pltpu.SMEM((row_blocks,), jnp.int32)],
    )(tile_counts, tile_rows, tile_cols, own)
    groups = [[cube * GROUP + member for member in range(GROUP)] for cube in range(cubes)]
    words = exchange(own, groups)
    return words, lists


def exchange(array, groups):
    return lax.all_to_all(
        array, "node", split_axis=0, concat_axis=0, tiled=True, axis_index_groups=groups
    )


def named_blocks(words_ref, member, owner, row_blocks):
    words = [words_ref[member, at] for at in range(words_ref.shape[1])]
    mask = owner_mask(words, owner, row_blocks)
    return [pl.multiple_of(block * BLK, BLK) for block in (lowest(mask), highest(mask))]


def pack_kernel(cubes, whole, messages, fetched, words_ref, *refs):
    held, refs = dict(zip(whole, refs)), refs[len(whole) :]
    total = len(messages)
    sent, packed, done = refs[:total], refs[total : 2 * total], refs[2 * total]
    row_blocks = held[whole[0]].shape[1] // BLK
    node = lax.axis_index("node")
    cube, member = split(node, GROUP)

    def fill(target, other, unit, source):
        owner = split(cube + unit, cubes)[1] * GROUP + (member ^ source)
        for slot, lane in enumerate(named_blocks(words_ref, other, owner, row_blocks)):
            target[slot] = held[unit, source][:, pl.ds(lane, BLK)]

    if fetched:
        own, held[0, 0] = held[0, 0], refs[-1]
        fetch = pltpu.make_async_copy(own, held[0, 0], done.at[total])
        fetch.start()
    copies = []
    for at, (step, sources) in reversed(list(enumerate(messages))):
        for part, (unit, source) in reversed(list(enumerate(sources))):
            if fetched and (unit, source) == (0, 0):
                fetch.wait()
            fill(packed[at].at[part], member ^ step, unit, source)
        copies.append(pltpu.make_async_copy(packed[at], sent[at], done.at[at]))
        copies[-1].start()
    for copy in copies:
        copy.wait()


def pack(cubes, words, held, messages, fetched, work):
    feat_local, nodes_local = next(iter(held.values())).shape
    shapes = [(len(sources), CAP, feat_local, BLK) for _, sources in messages]
    scratch = [pltpu.VMEM(shape, jnp.bfloat16) for shape in shapes]
    scratch += [pltpu.SemaphoreType.DMA((len(shapes) + 1,))]
    if fetched:
        scratch += [pltpu.VMEM((feat_local, nodes_local), jnp.bfloat16)]
        held = {**held, (0, 0): in_hbm(held[0, 0])}
    return pl.pallas_call(
        functools.partial(pack_kernel, cubes, tuple(held), messages, fetched),
        out_shape=[pltpu.HBM(shape, jnp.bfloat16) for shape in shapes],
        in_specs=[SMEM] + [HBM if fetched and at == (0, 0) else VMEM for at in held],
        out_specs=[HBM] * len(shapes),
        scratch_shapes=scratch,
        compiler_params=PARAMS,
        cost_estimate=pl.CostEstimate(flops=work, bytes_accessed=0, transcendentals=0),
    )(words, *held.values())


def in_hbm(array):
    return pltpu.with_memory_space_constraint(array, pltpu.HBM)


def keep_kernel(cubes, whole, words_ref, *refs):
    held, kept = refs[:-1], refs[-1]
    row_blocks = held[0].shape[1] // BLK
    node = lax.axis_index("node")
    cube, member = split(node, GROUP)
    for at, (unit, source) in enumerate(whole):
        owner = split(cube + unit, cubes)[1] * GROUP + (member ^ source)
        for slot, lane in enumerate(named_blocks(words_ref, member, owner, row_blocks)):
            kept[at, slot] = held[at][:, pl.ds(lane, BLK)]


def keep(cubes, words, held):
    shape = (len(held), CAP, held[0, 0].shape[0], BLK)
    return pl.pallas_call(
        functools.partial(keep_kernel, cubes, tuple(held)),
        out_shape=jax.ShapeDtypeStruct(shape, jnp.bfloat16),
        in_specs=[SMEM] + [VMEM] * len(held),
        out_specs=VMEM,
        compiler_params=PARAMS,
    )(words, *held.values())


def aggregate_kernel(cubes, limit, messages, fetched, lists_hbm, tiles, *refs):
    received, refs = refs[: len(messages)], refs[len(messages) :]
    out_ref, lists, blocks, total, done = refs[:5]
    pairs = [(lists_hbm, lists)]
    if fetched:
        pairs.append((tiles, refs[5]))
        tiles = refs[5]
    for (step, sources, far), array in zip(messages, received):
        for part, (unit, source) in enumerate(sources if far else ()):
            place = (unit * GROUP + (step ^ source)) * CAP
            pairs.append((array.at[part], blocks.at[place : place + CAP]))
    copies = [pltpu.make_async_copy(*pair, done.at[at]) for at, pair in enumerate(pairs)]
    for copy in copies:
        copy.start()
    total[...] = jnp.zeros_like(total)
    blocks[cubes * GROUP * CAP] = jnp.zeros_like(blocks[cubes * GROUP * CAP])
    for (step, sources, far), array in zip(messages, received):
        for part, (unit, source) in enumerate(() if far else sources):
            place = (unit * GROUP + (step ^ source)) * CAP
            blocks[place : place + CAP] = array[part]
    for copy in copies:
        copy.wait()

    @pl.loop(0, split(lists[0] + WIDTH - 1, WIDTH)[0])
    def _(loop_step):
        sums = []
        for wide in range(WIDTH):
            group = loop_step * WIDTH + wide
            left, right = [], []
            for at in range(DEPTH):
                entry = 1 + limit + 2 * (group * DEPTH + at)
                left.append(blocks[lists[entry + 1]])
                right.append(tiles[lists[entry]])
            summed = lax.dot_general(
                jnp.concatenate(left, axis=1),
                jnp.concatenate(right, axis=1),
                (((1,), (1,)), ((), ())),
                preferred_element_type=jnp.float32,
            )
            sums.append((lists[1 + group], summed))
        for row, summed in sums:
            total[row] += summed

    for row in range(out_ref.shape[1] // BLK):
        out_ref[:, row * BLK : (row + 1) * BLK] = total[row].astype(out_ref.dtype)


def aggregate(cubes, messages, fetched, lists, adj_tiles, received, nodes_local):
    feat_local = received[0].shape[2]
    row_blocks = nodes_local // BLK
    limit = group_limit(adj_tiles.shape[0], row_blocks)
    operands = [in_hbm(adj_tiles) if fetched else adj_tiles]
    operands += [in_hbm(one) if far else one for one, (_, _, far) in zip(received, messages)]
    spaces = [HBM if fetched else VMEM] + [HBM if far else VMEM for _, _, far in messages]
    scratch = [
        pltpu.SMEM(lists.shape, jnp.int32),
        pltpu.VMEM((cubes * GROUP * CAP + 1, feat_local, BLK), jnp.bfloat16),
        pltpu.VMEM((row_blocks + 1, feat_local, BLK), jnp.float32),
        pltpu.SemaphoreType.DMA((2 + cubes * GROUP,)),
    ]
    if fetched:
        scratch.append(pltpu.VMEM(adj_tiles.shape, jnp.bfloat16))
    return pl.pallas_call(
        functools.partial(aggregate_kernel, cubes, limit, messages, fetched),
        out_shape=jax.ShapeDtypeStruct((feat_local, nodes_local), jnp.bfloat16),
        in_specs=[HBM] + spaces,
        out_specs=VMEM,
        scratch_shapes=scratch,
        compiler_params=PARAMS,
        cost_estimate=pl.CostEstimate(
            flops=2 * adj_tiles.shape[0] * feat_local * BLK * BLK,
            bytes_accessed=2 * sum(one.size for one in operands),
            transcendentals=0,
        ),
    )(in_hbm(lists), *operands)


def gather_sums(feat_t, adj_tiles, plan, cubes, by_planes):
    words, lists = plan
    nodes = cubes * GROUP

    def to_member(array, step):
        return lax.ppermute(array, "node", [(n, n ^ step) for n in range(nodes)])

    relayed = {
        (unit, 0): lax.ppermute(
            feat_t, "node", [(n, (n - unit * GROUP) % nodes) for n in range(nodes)]
        )
        for unit in range(1, cubes)
    }
    if by_planes:
        held = {(0, 0): feat_t, **relayed}
        held.update({(unit, 4): to_member(array, 4) for (unit, _), array in held.items()})
        batches = [
            ([(0, 0)], 0),
            ([(0, 4)] + list(relayed), RELAY_WORK),
            ([(unit, 4) for unit, _ in relayed], RELAY_WORK),
        ]
        messages, received = [], []
        for number, (sources, work) in enumerate(batches):
            batch = [(step, sources) for step in (3, 1, 2, 0)]
            array = {at: held[at] for at in sources}
            sent = pack(cubes, words, array, batch, False, work)
            for one, (step, _) in zip(sent, batch):
                far = number == 0 or step == 0 or (number, step) == (2, 2)
                messages.append((step, sources, far))
                received.append(to_member(one, step) if step else one)
    else:
        near = {(0, step): to_member(feat_t, step) if step else feat_t for step in NEAR}
        held = {**relayed, **near}
        batch = [
            (step, ([(0, PASSED[step])] if step in PASSED else []) + list(relayed))
            for step in STEPS
        ]
        sent = list(pack(cubes, words, held, batch, True, 0))
        kept = keep(cubes, words, held)
        sent[4], kept, lists = lax.optimization_barrier((sent[4], kept, lists))
        received = [to_member(one, step) for one, (step, _) in zip(sent, batch)]
        received.append(kept)
        messages = [(*one, False) for one in batch] + [(0, list(held), False)]
    local = aggregate(
        cubes, messages, not by_planes, lists, adj_tiles, received, feat_t.shape[1]
    )
    return lax.all_gather(local, "col", axis=0, tiled=True)


def dense_kernel(weight, aggregated, bias, out_ref):
    out_ref[...] = (
        jnp.dot(weight[...], aggregated[...], preferred_element_type=jnp.float32) + bias[...]
    )


def dense(weight, aggregated, bias):
    return pl.pallas_call(
        dense_kernel,
        out_shape=jax.ShapeDtypeStruct((weight.shape[0], aggregated.shape[1]), jnp.float32),
        in_specs=[VMEM] * 3,
        out_specs=VMEM,
        compiler_params=PARAMS,
        cost_estimate=pl.CostEstimate(
            flops=2 * weight.size * aggregated.shape[1],
            bytes_accessed=2 * (weight.size + 3 * aggregated.size),
            transcendentals=0,
        ),
    )(weight, aggregated, bias[:, None])


def body(x_t, adj_tiles, tile_rows, tile_cols, tile_counts, w_first, b_first, w_second, b_second):
    cubes = lax.axis_size("node") // GROUP
    plan = make_plan(tile_rows, tile_cols, tile_counts, cubes, x_t.shape[1] // BLK)
    y_first = gather_sums(x_t, adj_tiles, plan, cubes, False)
    z_first = jnp.dot(w_first, y_first, preferred_element_type=jnp.float32) + b_first[:, None]
    h_first = jnp.maximum(z_first, 0.0).astype(jnp.bfloat16)
    y_second = gather_sums(h_first, adj_tiles, plan, cubes, True)
    return dense(w_second, y_second, b_second)


def solution(mesh):
    return jax.shard_map(
        body,
        mesh=mesh,
        in_specs=(
            P("col", "node"),
            P("node", None, None),
            P("node"),
            P("node"),
            P("node"),
            P("col", None),
            P("col"),
            P("col", None),
            P("col"),
        ),
        out_specs=P("col", "node"),
        check_vma=False,
    )
```

```python
import functools

import jax
import jax.numpy as jnp
from jax import lax
from jax.experimental import pallas as pl
from jax.experimental.pallas import tpu as pltpu
from jax.sharding import PartitionSpec as P

BLK = 128
CAP = 2
GROUP = 8
NEAR = (0, 1, 2, 4)
PASSED = {7: 0, 4: 1, 1: 2, 2: 4}
STEPS = (7, 6, 3, 4, 5, 1, 2)
DEPTH = 8
RELAY_WORK = 50_000_000_000
WIDTH = 2
SMEM = pl.BlockSpec(memory_space=pltpu.SMEM)
VMEM = pl.BlockSpec(memory_space=pltpu.VMEM)
HBM = pl.BlockSpec(memory_space=pltpu.HBM)
PARAMS = pltpu.CompilerParams(vmem_limit_bytes=24 * 1024 * 1024)


def split(value, size):
    shift = size.bit_length() - 1
    if size == 1 << shift:
        return value >> shift, value & (size - 1)
    return lax.div(value, size), lax.rem(value, size)


def lowest(mask):
    return jnp.where(mask & 1 != 0, 0, jnp.where(mask & 2 != 0, 1, jnp.where(mask & 4 != 0, 2, 3)))


def highest(mask):
    return jnp.where(mask & 8 != 0, 3, jnp.where(mask & 4 != 0, 2, jnp.where(mask & 2 != 0, 1, 0)))


def owner_mask(words, owner, row_blocks):
    first = owner * row_blocks
    word = words[0]
    for at in range(1, len(words)):
        word = jnp.where(first >> 5 == at, words[at], word)
    return (word >> (first & 31)) & ((1 << row_blocks) - 1)


def words_kernel(count_ref, cols_ref, words_ref):
    live = count_ref[0]
    word_total = words_ref.shape[1]

    def step(slot, found):
        column = cols_ref[slot]
        bit = jnp.where(slot < live, 1 << (column & 31), 0)
        word = column >> 5
        return tuple(one | jnp.where(word == at, bit, 0) for at, one in enumerate(found))

    start = tuple(jnp.int32(0) for _ in range(word_total))
    found = lax.fori_loop(0, cols_ref.shape[0], step, start, unroll=8)
    for member in range(GROUP):
        for at in range(word_total):
            words_ref[member, at] = found[at]


def group_limit(tile_total, row_blocks):
    return -(-(tile_total // DEPTH + row_blocks) // WIDTH) * WIDTH


def list_kernel(cubes, row_blocks, count_ref, rows_ref, cols_ref, words_ref, lists, filled):
    tile_total = cols_ref.shape[0]
    node = lax.axis_index("node")
    cube, member = split(node, GROUP)
    words = [words_ref[0, at] for at in range(words_ref.shape[1])]
    limit = group_limit(tile_total, row_blocks)

    @pl.loop(0, limit)
    def _(group):
        lists[1 + group] = row_blocks
        for at in range(DEPTH):
            entry = 1 + limit + 2 * (group * DEPTH + at)
            lists[entry] = 0
            lists[entry + 1] = cubes * GROUP * CAP

    for row in range(row_blocks):
        filled[row] = 0

    @pl.loop(0, count_ref[0])
    def _(slot):
        row = rows_ref[slot]
        filled[row] = filled[row] + 1

    start = 0
    for row in range(row_blocks):
        groups, _ = split(filled[row] + DEPTH - 1, DEPTH)
        filled[row] = start * DEPTH

        @pl.loop(start, start + groups)
        def _(group):
            lists[1 + group] = row

        start = start + groups
    lists[0] = start

    @pl.loop(0, count_ref[0])
    def _(slot):
        owner, block = split(cols_ref[slot], row_blocks)
        home, other = split(owner, GROUP)
        unit = jnp.where(home >= cube, home - cube, home - cube + cubes)
        second = block != lowest(owner_mask(words, owner, row_blocks))
        row = rows_ref[slot]
        entry = 1 + limit + 2 * filled[row]
        filled[row] = filled[row] + 1
        lists[entry] = slot
        lists[entry + 1] = (unit * GROUP + (other ^ member)) * CAP + jnp.where(second, 1, 0)


def make_plan(tile_rows, tile_cols, tile_counts, cubes, row_blocks):
    tile_total = tile_cols.shape[0]
    word_total = -(-cubes * GROUP * row_blocks // 32)
    list_length = 1 + group_limit(tile_total, row_blocks) * (1 + 2 * DEPTH)
    own = pl.pallas_call(
        words_kernel,
        out_shape=jax.ShapeDtypeStruct((GROUP, word_total), jnp.int32),
        in_specs=[SMEM] * 2,
        out_specs=SMEM,
    )(tile_counts, tile_cols)
    lists = pl.pallas_call(
        functools.partial(list_kernel, cubes, row_blocks),
        out_shape=jax.ShapeDtypeStruct((list_length,), jnp.int32),
        in_specs=[SMEM] * 4,
        out_specs=SMEM,
        scratch_shapes=[pltpu.SMEM((row_blocks,), jnp.int32)],
    )(tile_counts, tile_rows, tile_cols, own)
    groups = [[cube * GROUP + member for member in range(GROUP)] for cube in range(cubes)]
    words = exchange(own, groups)
    return words, lists


def exchange(array, groups):
    return lax.all_to_all(
        array, "node", split_axis=0, concat_axis=0, tiled=True, axis_index_groups=groups
    )


def named_blocks(words_ref, member, owner, row_blocks):
    words = [words_ref[member, at] for at in range(words_ref.shape[1])]
    mask = owner_mask(words, owner, row_blocks)
    return [pl.multiple_of(block * BLK, BLK) for block in (lowest(mask), highest(mask))]


def pack_kernel(cubes, whole, messages, fetched, words_ref, *refs):
    held, refs = dict(zip(whole, refs)), refs[len(whole) :]
    total = len(messages)
    sent, packed, done = refs[:total], refs[total : 2 * total], refs[2 * total]
    row_blocks = held[whole[0]].shape[1] // BLK
    node = lax.axis_index("node")
    cube, member = split(node, GROUP)

    def fill(target, other, unit, source):
        owner = split(cube + unit, cubes)[1] * GROUP + (member ^ source)
        for slot, lane in enumerate(named_blocks(words_ref, other, owner, row_blocks)):
            target[slot] = held[unit, source][:, pl.ds(lane, BLK)]

    if fetched:
        own, held[0, 0] = held[0, 0], refs[-1]
        fetch = pltpu.make_async_copy(own, held[0, 0], done.at[total])
        fetch.start()
    copies = []
    for at, (step, sources) in reversed(list(enumerate(messages))):
        for part, (unit, source) in reversed(list(enumerate(sources))):
            if fetched and (unit, source) == (0, 0):
                fetch.wait()
            fill(packed[at].at[part], member ^ step, unit, source)
        copies.append(pltpu.make_async_copy(packed[at], sent[at], done.at[at]))
        copies[-1].start()
    for copy in copies:
        copy.wait()


def pack(cubes, words, held, messages, fetched, work):
    feat_local, nodes_local = next(iter(held.values())).shape
    shapes = [(len(sources), CAP, feat_local, BLK) for _, sources in messages]
    scratch = [pltpu.VMEM(shape, jnp.bfloat16) for shape in shapes]
    scratch += [pltpu.SemaphoreType.DMA((len(shapes) + 1,))]
    if fetched:
        scratch += [pltpu.VMEM((feat_local, nodes_local), jnp.bfloat16)]
        held = {**held, (0, 0): in_hbm(held[0, 0])}
    return pl.pallas_call(
        functools.partial(pack_kernel, cubes, tuple(held), messages, fetched),
        out_shape=[pltpu.HBM(shape, jnp.bfloat16) for shape in shapes],
        in_specs=[SMEM] + [HBM if fetched and at == (0, 0) else VMEM for at in held],
        out_specs=[HBM] * len(shapes),
        scratch_shapes=scratch,
        compiler_params=PARAMS,
        cost_estimate=pl.CostEstimate(flops=work, bytes_accessed=0, transcendentals=0),
    )(words, *held.values())


def in_hbm(array):
    return pltpu.with_memory_space_constraint(array, pltpu.HBM)


def keep_kernel(cubes, whole, words_ref, *refs):
    held, kept = refs[:-1], refs[-1]
    row_blocks = held[0].shape[1] // BLK
    node = lax.axis_index("node")
    cube, member = split(node, GROUP)
    for at, (unit, source) in enumerate(whole):
        owner = split(cube + unit, cubes)[1] * GROUP + (member ^ source)
        for slot, lane in enumerate(named_blocks(words_ref, member, owner, row_blocks)):
            kept[at, slot] = held[at][:, pl.ds(lane, BLK)]


def keep(cubes, words, held):
    shape = (len(held), CAP, held[0, 0].shape[0], BLK)
    return pl.pallas_call(
        functools.partial(keep_kernel, cubes, tuple(held)),
        out_shape=jax.ShapeDtypeStruct(shape, jnp.bfloat16),
        in_specs=[SMEM] + [VMEM] * len(held),
        out_specs=VMEM,
        compiler_params=PARAMS,
    )(words, *held.values())


def aggregate_kernel(cubes, limit, messages, fetched, lists_hbm, tiles, *refs):
    received, refs = refs[: len(messages)], refs[len(messages) :]
    out_ref, lists, blocks, total, done = refs[:5]
    pairs = [(lists_hbm, lists)]
    if fetched:
        pairs.append((tiles, refs[5]))
        tiles = refs[5]
    for (step, sources, far), array in zip(messages, received):
        for part, (unit, source) in enumerate(sources if far else ()):
            place = (unit * GROUP + (step ^ source)) * CAP
            pairs.append((array.at[part], blocks.at[place : place + CAP]))
    copies = [pltpu.make_async_copy(*pair, done.at[at]) for at, pair in enumerate(pairs)]
    for copy in copies:
        copy.start()
    total[...] = jnp.zeros_like(total)
    blocks[cubes * GROUP * CAP] = jnp.zeros_like(blocks[cubes * GROUP * CAP])
    for (step, sources, far), array in zip(messages, received):
        for part, (unit, source) in enumerate(() if far else sources):
            place = (unit * GROUP + (step ^ source)) * CAP
            blocks[place : place + CAP] = array[part]
    for copy in copies:
        copy.wait()

    @pl.loop(0, split(lists[0] + WIDTH - 1, WIDTH)[0])
    def _(loop_step):
        sums = []
        for wide in range(WIDTH):
            group = loop_step * WIDTH + wide
            left, right = [], []
            for at in range(DEPTH):
                entry = 1 + limit + 2 * (group * DEPTH + at)
                left.append(blocks[lists[entry + 1]])
                right.append(tiles[lists[entry]])
            summed = lax.dot_general(
                jnp.concatenate(left, axis=1),
                jnp.concatenate(right, axis=1),
                (((1,), (1,)), ((), ())),
                preferred_element_type=jnp.float32,
            )
            sums.append((lists[1 + group], summed))
        for row, summed in sums:
            total[row] += summed

    for row in range(out_ref.shape[1] // BLK):
        out_ref[:, row * BLK : (row + 1) * BLK] = total[row].astype(out_ref.dtype)


def aggregate(cubes, messages, fetched, lists, adj_tiles, received, nodes_local):
    feat_local = received[0].shape[2]
    row_blocks = nodes_local // BLK
    limit = group_limit(adj_tiles.shape[0], row_blocks)
    operands = [in_hbm(adj_tiles) if fetched else adj_tiles]
    operands += [in_hbm(one) if far else one for one, (_, _, far) in zip(received, messages)]
    spaces = [HBM if fetched else VMEM] + [HBM if far else VMEM for _, _, far in messages]
    scratch = [
        pltpu.SMEM(lists.shape, jnp.int32),
        pltpu.VMEM((cubes * GROUP * CAP + 1, feat_local, BLK), jnp.bfloat16),
        pltpu.VMEM((row_blocks + 1, feat_local, BLK), jnp.float32),
        pltpu.SemaphoreType.DMA((2 + cubes * GROUP,)),
    ]
    if fetched:
        scratch.append(pltpu.VMEM(adj_tiles.shape, jnp.bfloat16))
    return pl.pallas_call(
        functools.partial(aggregate_kernel, cubes, limit, messages, fetched),
        out_shape=jax.ShapeDtypeStruct((feat_local, nodes_local), jnp.bfloat16),
        in_specs=[HBM] + spaces,
        out_specs=VMEM,
        scratch_shapes=scratch,
        compiler_params=PARAMS,
        cost_estimate=pl.CostEstimate(
            flops=2 * adj_tiles.shape[0] * feat_local * BLK * BLK,
            bytes_accessed=2 * sum(one.size for one in operands),
            transcendentals=0,
        ),
    )(in_hbm(lists), *operands)


def gather_sums(feat_t, adj_tiles, plan, cubes, by_planes):
    words, lists = plan
    nodes = cubes * GROUP

    def to_member(array, step):
        return lax.ppermute(array, "node", [(n, n ^ step) for n in range(nodes)])

    relayed = {
        (unit, 0): lax.ppermute(
            feat_t, "node", [(n, (n - unit * GROUP) % nodes) for n in range(nodes)]
        )
        for unit in range(1, cubes)
    }
    if by_planes:
        held = {(0, 0): feat_t, **relayed}
        held.update({(unit, 4): to_member(array, 4) for (unit, _), array in held.items()})
        batches = [
            ([(0, 0)], 0),
            ([(0, 4)] + list(relayed), RELAY_WORK),
            ([(unit, 4) for unit, _ in relayed], RELAY_WORK),
        ]
        messages, received = [], []
        for number, (sources, work) in enumerate(batches):
            batch = [(step, sources) for step in (3, 1, 2, 0)]
            array = {at: held[at] for at in sources}
            sent = pack(cubes, words, array, batch, False, work)
            for one, (step, _) in zip(sent, batch):
                far = number == 0 or step == 0 or (number, step) == (2, 2)
                messages.append((step, sources, far))
                received.append(to_member(one, step) if step else one)
    else:
        near = {(0, step): to_member(feat_t, step) if step else feat_t for step in NEAR}
        held = {**relayed, **near}
        batch = [
            (step, ([(0, PASSED[step])] if step in PASSED else []) + list(relayed))
            for step in STEPS
        ]
        sent = list(pack(cubes, words, held, batch, True, 0))
        kept = keep(cubes, words, held)
        sent[4], kept, lists = lax.optimization_barrier((sent[4], kept, lists))
        received = [to_member(one, step) for one, (step, _) in zip(sent, batch)]
        received.append(kept)
        messages = [(*one, False) for one in batch] + [(0, list(held), False)]
    local = aggregate(
        cubes, messages, not by_planes, lists, adj_tiles, received, feat_t.shape[1]
    )
    return lax.all_gather(local, "col", axis=0, tiled=True)


def dense_kernel(weight, aggregated, bias, out_ref):
    out_ref[...] = (
        jnp.dot(weight[...], aggregated[...], preferred_element_type=jnp.float32) + bias[...]
    )


def dense(weight, aggregated, bias):
    return pl.pallas_call(
        dense_kernel,
        out_shape=jax.ShapeDtypeStruct((weight.shape[0], aggregated.shape[1]), jnp.float32),
        in_specs=[VMEM] * 3,
        out_specs=VMEM,
        compiler_params=PARAMS,
        cost_estimate=pl.CostEstimate(
            flops=2 * weight.size * aggregated.shape[1],
            bytes_accessed=2 * (weight.size + 3 * aggregated.size),
            transcendentals=0,
        ),
    )(weight, aggregated, bias[:, None])


def body(x_t, adj_tiles, tile_rows, tile_cols, tile_counts, w_first, b_first, w_second, b_second):
    cubes = lax.axis_size("node") // GROUP
    plan = make_plan(tile_rows, tile_cols, tile_counts, cubes, x_t.shape[1] // BLK)
    y_first = gather_sums(x_t, adj_tiles, plan, cubes, False)
    z_first = jnp.dot(w_first, y_first, preferred_element_type=jnp.float32) + b_first[:, None]
    h_first = jnp.maximum(z_first, 0.0).astype(jnp.bfloat16)
    y_second = gather_sums(h_first, adj_tiles, plan, cubes, True)
    return dense(w_second, y_second, b_second)


def solution(mesh):
    return jax.shard_map(
        body,
        mesh=mesh,
        in_specs=(
            P("col", "node"),
            P("node", None, None),
            P("node"),
            P("node"),
            P("node"),
            P("col", None),
            P("col"),
            P("col", None),
            P("col"),
        ),
        out_specs=P("col", "node"),
        check_vma=False,
    )
```

```python
import functools

import jax
import jax.numpy as jnp
from jax import lax
from jax.experimental import pallas as pl
from jax.experimental.pallas import tpu as pltpu
from jax.sharding import PartitionSpec as P

BLK = 128
CAP = 2
GROUP = 8
NEAR = (0, 1, 2, 4)
PASSED = {7: 0, 4: 1, 1: 2, 2: 4}
STEPS = (7, 6, 3, 4, 5, 1, 2)
DEPTH = 4
RELAY_WORK = 50_000_000_000
WIDTH = 3
SMEM = pl.BlockSpec(memory_space=pltpu.SMEM)
VMEM = pl.BlockSpec(memory_space=pltpu.VMEM)
HBM = pl.BlockSpec(memory_space=pltpu.HBM)
PARAMS = pltpu.CompilerParams(vmem_limit_bytes=24 * 1024 * 1024)


def split(value, size):
    shift = size.bit_length() - 1
    if size == 1 << shift:
        return value >> shift, value & (size - 1)
    return lax.div(value, size), lax.rem(value, size)


def lowest(mask):
    return jnp.where(mask & 1 != 0, 0, jnp.where(mask & 2 != 0, 1, jnp.where(mask & 4 != 0, 2, 3)))


def highest(mask):
    return jnp.where(mask & 8 != 0, 3, jnp.where(mask & 4 != 0, 2, jnp.where(mask & 2 != 0, 1, 0)))


def owner_mask(words, owner, row_blocks):
    first = owner * row_blocks
    word = words[0]
    for at in range(1, len(words)):
        word = jnp.where(first >> 5 == at, words[at], word)
    return (word >> (first & 31)) & ((1 << row_blocks) - 1)


def words_kernel(count_ref, cols_ref, words_ref):
    live = count_ref[0]
    word_total = words_ref.shape[1]

    def step(slot, found):
        column = cols_ref[slot]
        bit = jnp.where(slot < live, 1 << (column & 31), 0)
        word = column >> 5
        return tuple(one | jnp.where(word == at, bit, 0) for at, one in enumerate(found))

    start = tuple(jnp.int32(0) for _ in range(word_total))
    found = lax.fori_loop(0, cols_ref.shape[0], step, start, unroll=8)
    for member in range(GROUP):
        for at in range(word_total):
            words_ref[member, at] = found[at]


def group_limit(tile_total, row_blocks):
    return -(-(tile_total // DEPTH + row_blocks) // WIDTH) * WIDTH


def list_kernel(cubes, row_blocks, count_ref, rows_ref, cols_ref, words_ref, lists, filled):
    tile_total = cols_ref.shape[0]
    node = lax.axis_index("node")
    cube, member = split(node, GROUP)
    words = [words_ref[0, at] for at in range(words_ref.shape[1])]
    limit = group_limit(tile_total, row_blocks)

    @pl.loop(0, limit)
    def _(group):
        lists[1 + group] = row_blocks
        for at in range(DEPTH):
            entry = 1 + limit + 2 * (group * DEPTH + at)
            lists[entry] = 0
            lists[entry + 1] = cubes * GROUP * CAP

    for row in range(row_blocks):
        filled[row] = 0

    @pl.loop(0, count_ref[0])
    def _(slot):
        row = rows_ref[slot]
        filled[row] = filled[row] + 1

    start = 0
    for row in range(row_blocks):
        groups, _ = split(filled[row] + DEPTH - 1, DEPTH)
        filled[row] = start * DEPTH

        @pl.loop(start, start + groups)
        def _(group):
            lists[1 + group] = row

        start = start + groups
    lists[0] = start

    @pl.loop(0, count_ref[0])
    def _(slot):
        owner, block = split(cols_ref[slot], row_blocks)
        home, other = split(owner, GROUP)
        unit = jnp.where(home >= cube, home - cube, home - cube + cubes)
        second = block != lowest(owner_mask(words, owner, row_blocks))
        row = rows_ref[slot]
        entry = 1 + limit + 2 * filled[row]
        filled[row] = filled[row] + 1
        lists[entry] = slot
        lists[entry + 1] = (unit * GROUP + (other ^ member)) * CAP + jnp.where(second, 1, 0)


def make_plan(tile_rows, tile_cols, tile_counts, cubes, row_blocks):
    tile_total = tile_cols.shape[0]
    word_total = -(-cubes * GROUP * row_blocks // 32)
    list_length = 1 + group_limit(tile_total, row_blocks) * (1 + 2 * DEPTH)
    own = pl.pallas_call(
        words_kernel,
        out_shape=jax.ShapeDtypeStruct((GROUP, word_total), jnp.int32),
        in_specs=[SMEM] * 2,
        out_specs=SMEM,
    )(tile_counts, tile_cols)
    lists = pl.pallas_call(
        functools.partial(list_kernel, cubes, row_blocks),
        out_shape=jax.ShapeDtypeStruct((list_length,), jnp.int32),
        in_specs=[SMEM] * 4,
        out_specs=SMEM,
        scratch_shapes=[pltpu.SMEM((row_blocks,), jnp.int32)],
    )(tile_counts, tile_rows, tile_cols, own)
    groups = [[cube * GROUP + member for member in range(GROUP)] for cube in range(cubes)]
    words = exchange(own, groups)
    return words, lists


def exchange(array, groups):
    return lax.all_to_all(
        array, "node", split_axis=0, concat_axis=0, tiled=True, axis_index_groups=groups
    )


def named_blocks(words_ref, member, owner, row_blocks):
    words = [words_ref[member, at] for at in range(words_ref.shape[1])]
    mask = owner_mask(words, owner, row_blocks)
    return [pl.multiple_of(block * BLK, BLK) for block in (lowest(mask), highest(mask))]


def pack_kernel(cubes, whole, messages, fetched, words_ref, *refs):
    held, refs = dict(zip(whole, refs)), refs[len(whole) :]
    total = len(messages)
    sent, packed, done = refs[:total], refs[total : 2 * total], refs[2 * total]
    row_blocks = held[whole[0]].shape[1] // BLK
    node = lax.axis_index("node")
    cube, member = split(node, GROUP)

    def fill(target, other, unit, source):
        owner = split(cube + unit, cubes)[1] * GROUP + (member ^ source)
        for slot, lane in enumerate(named_blocks(words_ref, other, owner, row_blocks)):
            target[slot] = held[unit, source][:, pl.ds(lane, BLK)]

    if fetched:
        own, held[0, 0] = held[0, 0], refs[-1]
        fetch = pltpu.make_async_copy(own, held[0, 0], done.at[total])
        fetch.start()
    copies = []
    for at, (step, sources) in reversed(list(enumerate(messages))):
        for part, (unit, source) in reversed(list(enumerate(sources))):
            if fetched and (unit, source) == (0, 0):
                fetch.wait()
            fill(packed[at].at[part], member ^ step, unit, source)
        copies.append(pltpu.make_async_copy(packed[at], sent[at], done.at[at]))
        copies[-1].start()
    for copy in copies:
        copy.wait()


def pack(cubes, words, held, messages, fetched, work):
    feat_local, nodes_local = next(iter(held.values())).shape
    shapes = [(len(sources), CAP, feat_local, BLK) for _, sources in messages]
    scratch = [pltpu.VMEM(shape, jnp.bfloat16) for shape in shapes]
    scratch += [pltpu.SemaphoreType.DMA((len(shapes) + 1,))]
    if fetched:
        scratch += [pltpu.VMEM((feat_local, nodes_local), jnp.bfloat16)]
        held = {**held, (0, 0): in_hbm(held[0, 0])}
    return pl.pallas_call(
        functools.partial(pack_kernel, cubes, tuple(held), messages, fetched),
        out_shape=[pltpu.HBM(shape, jnp.bfloat16) for shape in shapes],
        in_specs=[SMEM] + [HBM if fetched and at == (0, 0) else VMEM for at in held],
        out_specs=[HBM] * len(shapes),
        scratch_shapes=scratch,
        compiler_params=PARAMS,
        cost_estimate=pl.CostEstimate(flops=work, bytes_accessed=0, transcendentals=0),
    )(words, *held.values())


def in_hbm(array):
    return pltpu.with_memory_space_constraint(array, pltpu.HBM)


def keep_kernel(cubes, whole, words_ref, *refs):
    held, kept = refs[:-1], refs[-1]
    row_blocks = held[0].shape[1] // BLK
    node = lax.axis_index("node")
    cube, member = split(node, GROUP)
    for at, (unit, source) in enumerate(whole):
        owner = split(cube + unit, cubes)[1] * GROUP + (member ^ source)
        for slot, lane in enumerate(named_blocks(words_ref, member, owner, row_blocks)):
            kept[at, slot] = held[at][:, pl.ds(lane, BLK)]


def keep(cubes, words, held):
    shape = (len(held), CAP, held[0, 0].shape[0], BLK)
    return pl.pallas_call(
        functools.partial(keep_kernel, cubes, tuple(held)),
        out_shape=jax.ShapeDtypeStruct(shape, jnp.bfloat16),
        in_specs=[SMEM] + [VMEM] * len(held),
        out_specs=VMEM,
        compiler_params=PARAMS,
    )(words, *held.values())


def aggregate_kernel(cubes, limit, messages, fetched, lists_hbm, tiles, *refs):
    received, refs = refs[: len(messages)], refs[len(messages) :]
    out_ref, lists, blocks, total, done = refs[:5]
    pairs = [(lists_hbm, lists)]
    if fetched:
        pairs.append((tiles, refs[5]))
        tiles = refs[5]
    for (step, sources, far), array in zip(messages, received):
        for part, (unit, source) in enumerate(sources if far else ()):
            place = (unit * GROUP + (step ^ source)) * CAP
            pairs.append((array.at[part], blocks.at[place : place + CAP]))
    copies = [pltpu.make_async_copy(*pair, done.at[at]) for at, pair in enumerate(pairs)]
    for copy in copies:
        copy.start()
    total[...] = jnp.zeros_like(total)
    blocks[cubes * GROUP * CAP] = jnp.zeros_like(blocks[cubes * GROUP * CAP])
    for (step, sources, far), array in zip(messages, received):
        for part, (unit, source) in enumerate(() if far else sources):
            place = (unit * GROUP + (step ^ source)) * CAP
            blocks[place : place + CAP] = array[part]
    for copy in copies:
        copy.wait()

    @pl.loop(0, split(lists[0] + WIDTH - 1, WIDTH)[0])
    def _(loop_step):
        sums = []
        for wide in range(WIDTH):
            group = loop_step * WIDTH + wide
            left, right = [], []
            for at in range(DEPTH):
                entry = 1 + limit + 2 * (group * DEPTH + at)
                left.append(blocks[lists[entry + 1]])
                right.append(tiles[lists[entry]])
            summed = lax.dot_general(
                jnp.concatenate(left, axis=1),
                jnp.concatenate(right, axis=1),
                (((1,), (1,)), ((), ())),
                preferred_element_type=jnp.float32,
            )
            sums.append((lists[1 + group], summed))
        for row, summed in sums:
            total[row] += summed

    for row in range(out_ref.shape[1] // BLK):
        out_ref[:, row * BLK : (row + 1) * BLK] = total[row].astype(out_ref.dtype)


def aggregate(cubes, messages, fetched, lists, adj_tiles, received, nodes_local):
    feat_local = received[0].shape[2]
    row_blocks = nodes_local // BLK
    limit = group_limit(adj_tiles.shape[0], row_blocks)
    operands = [in_hbm(adj_tiles) if fetched else adj_tiles]
    operands += [in_hbm(one) if far else one for one, (_, _, far) in zip(received, messages)]
    spaces = [HBM if fetched else VMEM] + [HBM if far else VMEM for _, _, far in messages]
    scratch = [
        pltpu.SMEM(lists.shape, jnp.int32),
        pltpu.VMEM((cubes * GROUP * CAP + 1, feat_local, BLK), jnp.bfloat16),
        pltpu.VMEM((row_blocks + 1, feat_local, BLK), jnp.float32),
        pltpu.SemaphoreType.DMA((2 + cubes * GROUP,)),
    ]
    if fetched:
        scratch.append(pltpu.VMEM(adj_tiles.shape, jnp.bfloat16))
    return pl.pallas_call(
        functools.partial(aggregate_kernel, cubes, limit, messages, fetched),
        out_shape=jax.ShapeDtypeStruct((feat_local, nodes_local), jnp.bfloat16),
        in_specs=[HBM] + spaces,
        out_specs=VMEM,
        scratch_shapes=scratch,
        compiler_params=PARAMS,
        cost_estimate=pl.CostEstimate(
            flops=2 * adj_tiles.shape[0] * feat_local * BLK * BLK,
            bytes_accessed=2 * sum(one.size for one in operands),
            transcendentals=0,
        ),
    )(in_hbm(lists), *operands)


def gather_sums(feat_t, adj_tiles, plan, cubes, by_planes):
    words, lists = plan
    nodes = cubes * GROUP

    def to_member(array, step):
        return lax.ppermute(array, "node", [(n, n ^ step) for n in range(nodes)])

    relayed = {
        (unit, 0): lax.ppermute(
            feat_t, "node", [(n, (n - unit * GROUP) % nodes) for n in range(nodes)]
        )
        for unit in range(1, cubes)
    }
    if by_planes:
        held = {(0, 0): feat_t, **relayed}
        held.update({(unit, 4): to_member(array, 4) for (unit, _), array in held.items()})
        batches = [
            ([(0, 0)], 0),
            ([(0, 4)] + list(relayed), RELAY_WORK),
            ([(unit, 4) for unit, _ in relayed], RELAY_WORK),
        ]
        messages, received = [], []
        for number, (sources, work) in enumerate(batches):
            batch = [(step, sources) for step in (3, 1, 2, 0)]
            array = {at: held[at] for at in sources}
            sent = pack(cubes, words, array, batch, False, work)
            for one, (step, _) in zip(sent, batch):
                far = number == 0 or step == 0 or (number, step) == (2, 2)
                messages.append((step, sources, far))
                received.append(to_member(one, step) if step else one)
    else:
        near = {(0, step): to_member(feat_t, step) if step else feat_t for step in NEAR}
        held = {**relayed, **near}
        batch = [
            (step, ([(0, PASSED[step])] if step in PASSED else []) + list(relayed))
            for step in STEPS
        ]
        sent = list(pack(cubes, words, held, batch, True, 0))
        kept = keep(cubes, words, held)
        sent[4], kept, lists = lax.optimization_barrier((sent[4], kept, lists))
        received = [to_member(one, step) for one, (step, _) in zip(sent, batch)]
        received.append(kept)
        messages = [(*one, False) for one in batch] + [(0, list(held), False)]
    local = aggregate(
        cubes, messages, not by_planes, lists, adj_tiles, received, feat_t.shape[1]
    )
    return lax.all_gather(local, "col", axis=0, tiled=True)


def dense_kernel(weight, aggregated, bias, out_ref):
    out_ref[...] = (
        jnp.dot(weight[...], aggregated[...], preferred_element_type=jnp.float32) + bias[...]
    )


def dense(weight, aggregated, bias):
    return pl.pallas_call(
        dense_kernel,
        out_shape=jax.ShapeDtypeStruct((weight.shape[0], aggregated.shape[1]), jnp.float32),
        in_specs=[VMEM] * 3,
        out_specs=VMEM,
        compiler_params=PARAMS,
        cost_estimate=pl.CostEstimate(
            flops=2 * weight.size * aggregated.shape[1],
            bytes_accessed=2 * (weight.size + 3 * aggregated.size),
            transcendentals=0,
        ),
    )(weight, aggregated, bias[:, None])


def body(x_t, adj_tiles, tile_rows, tile_cols, tile_counts, w_first, b_first, w_second, b_second):
    cubes = lax.axis_size("node") // GROUP
    plan = make_plan(tile_rows, tile_cols, tile_counts, cubes, x_t.shape[1] // BLK)
    y_first = gather_sums(x_t, adj_tiles, plan, cubes, False)
    z_first = jnp.dot(w_first, y_first, preferred_element_type=jnp.float32) + b_first[:, None]
    h_first = jnp.maximum(z_first, 0.0).astype(jnp.bfloat16)
    y_second = gather_sums(h_first, adj_tiles, plan, cubes, True)
    return dense(w_second, y_second, b_second)


def solution(mesh):
    return jax.shard_map(
        body,
        mesh=mesh,
        in_specs=(
            P("col", "node"),
            P("node", None, None),
            P("node"),
            P("node"),
            P("node"),
            P("col", None),
            P("col"),
            P("col", None),
            P("col"),
        ),
        out_specs=P("col", "node"),
        check_vma=False,
    )
```
